32 devices in a mesh: dp: 8 (over y, x, core), mp: 4 (over z).
Axes of the slice: x: 2, y: 2, z: 4, core: 2. Of those that a mesh axis runs over, the one named last changes fastest.
Arguments:
- image: bfloat16 [8, 1024, 1024], P('dp'), may hold values from -6 to 6
- text: bfloat16 [8, 128, 1024], P('dp'), may hold values from -6 to 6
- grad_out: bfloat16 [8, 1024, 1024], P('dp'), may hold values from -6 to 6
- lengths: int32 [8], P('dp'), may hold values from 8 to 128, as said below
- ln1_gain: float32 [1024], replicated, may hold values from 0.5 to 1.5
- ln1_bias: float32 [1024], replicated, may hold values from -1.5 to 1.5
- self_qkv: bfloat16 [1024, 3, 1024], P(None, None, 'mp'), may hold values from -0.1875 to 0.1875
- self_out: bfloat16 [1024, 1024], P('mp'), may hold values from -0.75 to 0.75
- ln2_gain: float32 [1024], replicated, may hold values from 0.5 to 1.5
- ln2_bias: float32 [1024], replicated, may hold values from -1.5 to 1.5
- cross_q: bfloat16 [1024, 1024], P(None, 'mp'), may hold values from -0.1875 to 0.1875
- cross_kv: bfloat16 [1024, 2, 1024], P(None, None, 'mp'), may hold values from -0.1875 to 0.1875
- cross_out: bfloat16 [1024, 1024], P('mp'), may hold values from -0.5 to 0.5
- ln3_gain: float32 [1024], replicated, may hold values from 0.5 to 1.5
- ln3_bias: float32 [1024], replicated, may hold values from -1.5 to 1.5
- mlp_in: bfloat16 [1024, 4096], P(None, 'mp'), may hold values from -0.1875 to 0.1875
- mlp_in_bias: float32 [4096], P('mp'), may hold values from -2.5 to 2.5
- mlp_out: bfloat16 [4096, 1024], P('mp'), may hold values from -0.09375 to 0.09375
- mlp_out_bias: float32 [1024], replicated, may hold values from -1.5 to 1.5
Outputs:
- out: bfloat16 [8, 1024, 1024], P('dp', 'mp')
- image_grad: float32 [8, 1024, 1024], P('dp', 'mp')
- text_grad: float32 [8, 128, 1024], P('dp', 'mp')
- ln1_gain_grad: float32 [1024], replicated
- ln1_bias_grad: float32 [1024], replicated
- self_qkv_grad: float32 [1024, 3, 1024], P(None, None, 'mp')
- self_out_grad: float32 [1024, 1024], P('mp')
- ln2_gain_grad: float32 [1024], replicated
- ln2_bias_grad: float32 [1024], replicated
- cross_q_grad: float32 [1024, 1024], P(None, 'mp')
- cross_kv_grad: float32 [1024, 2, 1024], P(None, None, 'mp')
- cross_out_grad: float32 [1024, 1024], P('mp')
- ln3_gain_grad: float32 [1024], replicated
- ln3_bias_grad: float32 [1024], replicated
- mlp_in_grad: float32 [1024, 4096], P(None, 'mp')
- mlp_in_bias_grad: float32 [4096], P('mp')
- mlp_out_grad: float32 [4096, 1024], P('mp')
- mlp_out_bias_grad: float32 [1024], replicated
The draws below stay inside these ranges and needn't reach their ends.
Inputs may be any that keep to these rules, and one draw needn't show every extreme that they name: `lengths`: the number of leading text slots that item i's prompt fills; the other slots are padding. Some item has 8 and some item has 128.
All inputs are finite; a program needn't handle non-finite values.
Results may differ from the reference program's by a relative error of at most 0.023.
Values may be sent and summed in bfloat16 or wider, within the bound.
A program may use at most 192 MiB of HBM per device.

```python
import jax
import jax.numpy as jnp
from jax import lax

D = 1024
HEADS = 16
HEAD_DIM = 64
FF = 4096
SEQ = 1024
SLOTS = 128
ITEMS = 8


def draw_lengths(key, part):
    key = jax.random.fold_in(key, 7)
    first, second = jax.random.split(key)
    values = jax.random.randint(first, (ITEMS,), 8, SLOTS + 1)
    order = jax.random.permutation(second, ITEMS)
    values = values.at[order[0]].set(SLOTS).at[order[1]].set(8)
    return values.astype(jnp.int32)


def levels(stream_key, shape, cuts, low, top_value):
    loudness = 1.0
    for position, blocks in cuts:
        draws = jax.random.uniform(jax.random.fold_in(jax.random.fold_in(stream_key, 6), position), (blocks,), jnp.float32, low / len(cuts), top_value / len(cuts))
        loudness = loudness * jnp.repeat(jnp.exp(draws), shape[position] // blocks).reshape((-1,) + (1,) * (len(shape) - 1 - position))
    return loudness


def bell_draw(own_key, extent, spread, most, cuts=(), held_as=jnp.bfloat16):
    level = levels(own_key, extent, cuts, -0.22, 0.18) if cuts else 1.0
    entries = jax.random.normal(own_key, extent, jnp.float32) * spread * level
    return jnp.minimum(jnp.maximum(entries, -most), most).astype(held_as)


def setup_inputs(seed: int = 0) -> dict:
    splits = jax.random.split(jax.random.key(seed), 20)
    image = bell_draw(splits[0], (ITEMS, SEQ, D), 1.0, 6.0, ((0, 8),))
    text = bell_draw(splits[1], (ITEMS, SLOTS, D), 1.0, 6.0, ((0, 8),))
    grad_out = bell_draw(splits[2], (ITEMS, SEQ, D), 1.0, 6.0, ((0, 8),))
    lengths = draw_lengths(jax.random.fold_in(splits[19], 71), 0)
    ln1_gain = jnp.clip(1.0 + 0.1 * jax.random.normal(splits[4], (D,), jnp.float32), 0.5, 1.5)
    ln1_bias = bell_draw(splits[5], (D,), 0.3, 1.5, (), jnp.float32)
    self_qkv = bell_draw(splits[6], (D, 3, D), D ** -0.5, 0.1875, ((2, 4),))
    self_out = bell_draw(splits[7], (D, D), (D // 16) ** -0.5, 0.75, ((0, 4),))
    ln2_gain = jnp.clip(1.0 + 0.1 * jax.random.normal(splits[8], (D,), jnp.float32), 0.5, 1.5)
    ln2_bias = bell_draw(splits[9], (D,), 0.3, 1.5, (), jnp.float32)
    cross_q = bell_draw(splits[10], (D, D), D ** -0.5, 0.1875, ((1, 4),))
    cross_kv = bell_draw(splits[11], (D, 2, D), D ** -0.5, 0.1875, ((2, 4),))
    cross_out = bell_draw(splits[12], (D, D), (D // 8) ** -0.5, 0.5, ((0, 4),))
    ln3_gain = jnp.clip(1.0 + 0.1 * jax.random.normal(splits[13], (D,), jnp.float32), 0.5, 1.5)
    ln3_bias = bell_draw(splits[14], (D,), 0.3, 1.5, (), jnp.float32)
    mlp_in = bell_draw(splits[15], (D, FF), D ** -0.5, 0.1875, ((1, 4),))
    mlp_in_bias = bell_draw(splits[16], (FF,), 0.5, 2.5, ((0, 4),), jnp.float32)
    mlp_out = bell_draw(splits[17], (FF, D), FF ** -0.5, 0.09375, ((0, 4),))
    mlp_out_bias = bell_draw(splits[18], (D,), 0.3, 1.5, (), jnp.float32)
    return dict(image=image, text=text, grad_out=grad_out, lengths=lengths, ln1_gain=ln1_gain, ln1_bias=ln1_bias, self_qkv=self_qkv, self_out=self_out, ln2_gain=ln2_gain, ln2_bias=ln2_bias, cross_q=cross_q, cross_kv=cross_kv, cross_out=cross_out, ln3_gain=ln3_gain, ln3_bias=ln3_bias, mlp_in=mlp_in, mlp_in_bias=mlp_in_bias, mlp_out=mlp_out, mlp_out_bias=mlp_out_bias)


@jax.custom_vjp
def low(v):
    return lax.optimization_barrier(v.astype(jnp.bfloat16)).astype(jnp.float32)

@jax.custom_vjp
def low_back(v):
    return v

def low_keep(v):
    return (low(v), None)

def low_pass(kept, grad):
    return (grad,)

def back_keep(v):
    return (v, None)

def back_low(kept, grad):
    return (low(grad),)
low.defvjp(low_keep, low_pass)
low_back.defvjp(back_keep, back_low)
epsilon = 1e-05
highest = lax.Precision.HIGHEST

def layer_norm(value, gain, shift):
    center = value - lax.optimization_barrier(jnp.mean(value, axis=-1, keepdims=True))
    return center * lax.rsqrt(lax.optimization_barrier(jnp.mean(center * center, axis=-1, keepdims=True)) + epsilon) * gain + shift

def attend(query, keys, values, allowed):
    scores = low_back(jnp.einsum('qhe,khe->hqk', query, keys, precision=highest)) * HEAD_DIM ** (-0.5)
    scores = jnp.where(allowed[None], scores, -1e+30)
    weights = low(jax.nn.softmax(scores, axis=-1))
    mixed = jnp.einsum('hqk,khe->qhe', weights, values, precision=highest)
    return low(low_back(mixed.reshape(query.shape[0], HEADS * HEAD_DIM)))

def item_layer(params, image, text, length):
    ln1_gain, ln1_bias, self_qkv, self_out, ln2_gain, ln2_bias, cross_q, cross_kv, cross_out, ln3_gain, ln3_bias, mlp_in, mlp_in_bias, mlp_out, mlp_out_bias = params
    normed = low(layer_norm(image, ln1_gain, ln1_bias))
    projected = low(low_back(jnp.dot(normed, self_qkv.reshape(D, 3 * D), precision=highest)))
    projected = projected.reshape(SEQ, 3, HEADS, HEAD_DIM)
    causal = lax.iota(jnp.int32, SEQ)[:, None] >= lax.iota(jnp.int32, SEQ)[None, :]
    mixed = attend(projected[:, 0], projected[:, 1], projected[:, 2], causal)
    first = image + low_back(jnp.dot(mixed, self_out, precision=highest))
    normed = low(layer_norm(first, ln2_gain, ln2_bias))
    query = low(low_back(jnp.dot(normed, cross_q, precision=highest))).reshape(SEQ, HEADS, HEAD_DIM)
    text_proj = low(low_back(jnp.dot(text, cross_kv.reshape(D, 2 * D), precision=highest)))
    text_proj = text_proj.reshape(SLOTS, 2, HEADS, HEAD_DIM)
    filled = jnp.broadcast_to((lax.iota(jnp.int32, SLOTS) < length)[None, :], (SEQ, SLOTS))
    mixed = attend(query, text_proj[:, 0], text_proj[:, 1], filled)
    second = first + low_back(jnp.dot(mixed, cross_out, precision=highest))
    normed = low(layer_norm(second, ln3_gain, ln3_bias))
    hidden = low_back(jnp.dot(normed, mlp_in, precision=highest) + mlp_in_bias)
    active = low(jax.nn.gelu(hidden, approximate=False))
    return second + low_back(jnp.dot(active, mlp_out, precision=highest) + mlp_out_bias)

def reference(image, text, grad_out, lengths, ln1_gain, ln1_bias, self_qkv, self_out, ln2_gain, ln2_bias, cross_q, cross_kv, cross_out, ln3_gain, ln3_bias, mlp_in, mlp_in_bias, mlp_out, mlp_out_bias):
    params = tuple((value.astype(jnp.float32) for value in (ln1_gain, ln1_bias, self_qkv, self_out, ln2_gain, ln2_bias, cross_q, cross_kv, cross_out, ln3_gain, ln3_bias, mlp_in, mlp_in_bias, mlp_out, mlp_out_bias)))

    def forward(image_full, text_full, weights):

        def step(carry, item):
            return (carry, jax.checkpoint(item_layer)(weights, item[0], item[1], item[2]))
        return lax.scan(step, None, (image_full, text_full, lengths))[1]
    result, pullback = jax.vjp(forward, image.astype(jnp.float32), text.astype(jnp.float32), params)
    image_grad, text_grad, grads = pullback(grad_out.astype(jnp.float32))
    gain1, shift1, qkv_grad, self_out_grad, gain2, shift2, query_grad, text_weight_grad, cross_out_grad, gain3, shift3, mlp_in_grad, in_bias_grad, mlp_out_grad, out_bias_grad = grads
    return (result.astype(jnp.bfloat16), image_grad, text_grad, gain1, shift1, qkv_grad, self_out_grad, gain2, shift2, query_grad, text_weight_grad, cross_out_grad, gain3, shift3, mlp_in_grad, in_bias_grad, mlp_out_grad, out_bias_grad)
```

```python
from functools import partial

import jax
import jax.numpy as jnp
from jax import lax
from jax.experimental import pallas as pl
from jax.experimental.pallas import tpu as pltpu
from jax.sharding import PartitionSpec as P

HEAD_DIM = 64
PAIR = 2 * HEAD_DIM
EPSILON = 1e-05
SCALE = HEAD_DIM ** (-0.5)
MASKED = -1e30
BF = jnp.bfloat16
F32 = jnp.float32
MESH = pl.DeviceIdType.MESH
VMEM_LIMIT = 56 << 20


def nn(a, b):
    return lax.dot_general(a, b, (((1,), (0,)), ((), ())), preferred_element_type=F32)


def nt(a, b):
    return lax.dot_general(a, b, (((1,), (1,)), ((), ())), preferred_element_type=F32)


def tn(a, b):
    return lax.dot_general(a, b, (((0,), (0,)), ((), ())), preferred_element_type=F32)


def norm_parts(value):
    center = value - jnp.mean(value, axis=-1, keepdims=True)
    inverse = lax.rsqrt(jnp.mean(center * center, axis=-1, keepdims=True) + EPSILON)
    return center * inverse, inverse


def half_masks():
    lane = lax.broadcasted_iota(jnp.int32, (1, PAIR), 1)
    first = jnp.where(lane < HEAD_DIM, 1.0, 0.0)
    return first, 1.0 - first


def stack_heads(pair, scale=None):
    first, second = half_masks()
    if scale is not None:
        first, second = first * scale, second * scale
    wide = pair.astype(F32)
    return jnp.concatenate([wide * first, wide * second], axis=0).astype(BF)


def fold_heads(stacked):
    rows = stacked.shape[1] // 2
    both = jnp.concatenate([stacked[:HEAD_DIM, :rows], stacked[HEAD_DIM:, rows:]], axis=0)
    return both.T


def causal(tile_keys, tile_rows):
    key = lax.broadcasted_iota(jnp.int32, (tile_keys, tile_rows), 0)
    row = lax.broadcasted_iota(jnp.int32, (tile_keys, tile_rows), 1)
    both = key <= row
    return jnp.concatenate([both, both], axis=1)


class Place:
    def __init__(self, sizes):
        self.n = sizes["mp"]
        self.dp = sizes["dp"]
        self.share = sizes["share"]
        self.d = lax.axis_index("dp")
        self.m = lax.axis_index("mp")
        self.core = lax.rem(self.d, 2)
        self.partner = (self.d + 1 - 2 * self.core, self.m)
        self.member = lax.rem(self.d, self.share)
        self.chip = self.member // 2
        self.base = self.d - self.member
        self.piece = self.core * (self.share // 2) + self.chip

    def along(self, offset):
        return lax.rem(self.m + offset, self.n)

    def peer(self, offset):
        return (self.d, self.along(offset))

    def chip_peer(self, offset):
        chip = lax.rem(self.chip + offset, self.share // 2)
        return (self.base + 2 * chip + self.core, self.m), self.core * (self.share // 2) + chip


def barrier(devices):
    sem = pltpu.get_barrier_semaphore()
    for device in devices:
        pl.semaphore_signal(sem, inc=1, device_id=device, device_id_type=MESH)
    pl.semaphore_wait(sem, len(devices))


class Gather:
    def __init__(self, place, own, full, offsets, slot_of, sems):
        self.place, self.own, self.full, self.offsets, self.slot_of = place, own, full, offsets, slot_of
        self.rows = own.shape[0]
        self.count = self.rows // place.share
        self.sems = sems

    def rows_of(self, slot, piece, pieces=1):
        start = pl.multiple_of(piece * self.count, self.count)
        return self.full.at[slot, pl.ds(start, pieces * self.count), :]

    def first(self, index):
        place, offset = self.place, self.offsets[index]
        start = pl.multiple_of(place.piece * self.count, self.count)
        return pltpu.make_async_remote_copy(
            src_ref=self.own.at[pl.ds(start, self.count), :],
            dst_ref=self.rows_of(self.slot_of(place.m), place.piece),
            send_sem=self.sems[0].at[index, 0],
            recv_sem=self.sems[1].at[index, 0],
            device_id=place.peer(offset),
            device_id_type=MESH,
        )

    def slot(self, index):
        place = self.place
        return self.slot_of(place.along(place.n - self.offsets[index]))

    def second(self, index, hop):
        place = self.place
        device, _ = place.chip_peer(hop)
        block = self.rows_of(self.slot(index), place.piece)
        return pltpu.make_async_remote_copy(
            src_ref=block,
            dst_ref=block,
            send_sem=self.sems[0].at[index, hop],
            recv_sem=self.sems[1].at[index, hop],
            device_id=device,
            device_id_type=MESH,
        )

    def third(self, index):
        place = self.place
        half = place.share // 2
        block = self.rows_of(self.slot(index), place.core * half, half)
        return pltpu.make_async_remote_copy(
            src_ref=block,
            dst_ref=block,
            send_sem=self.sems[0].at[index, half],
            recv_sem=self.sems[1].at[index, half],
            device_id=place.partner,
            device_id_type=MESH,
        )

    def local(self):
        return pltpu.make_async_copy(self.own, self.full.at[self.slot_of(self.place.m)], self.sems[2])

    def step(self, number):
        hops = range(1, self.place.share // 2)
        for index in range(len(self.offsets)):
            if number == 0:
                self.first(index).start()
            elif number == 1:
                self.first(index).wait_recv()
                for hop in hops:
                    self.second(index, hop).start()
            elif number == 2:
                for hop in hops:
                    self.second(index, hop).wait_recv()
                self.third(index).start()
            else:
                self.third(index).wait()
                self.first(index).wait_send()
                for hop in hops:
                    self.second(index, hop).wait_send()
        if number == 0:
            self.local().start()
        if number == 3:
            self.local().wait()


def attend_block(projected, mixed, totals, i, hp, size, local):
    rows = pl.ds(pl.multiple_of(i * size, size), size)
    column = pl.multiple_of(hp * PAIR, PAIR)
    query = stack_heads(projected[rows, pl.ds(column, PAIR)], SCALE)

    def tile(j, carry, diagonal):
        largest, total, acc = carry
        keys = pl.ds(pl.multiple_of(j * size, size), size)
        key = projected[keys, pl.ds(column + local, PAIR)]
        value = projected[keys, pl.ds(column + 2 * local, PAIR)]
        scores = nt(key, query)
        if diagonal:
            scores = jnp.where(causal(size, size), scores, MASKED)
        top = jnp.maximum(largest, jnp.max(scores, axis=0, keepdims=True))
        powers = jnp.exp(scores - top)
        shrink = jnp.exp(largest - top)
        total = total * shrink + jnp.sum(powers, axis=0, keepdims=True)
        acc = acc * shrink + tn(value, powers.astype(BF))
        return top, total, acc

    carry = (
        jnp.full((1, 2 * size), MASKED, F32),
        jnp.zeros((1, 2 * size), F32),
        jnp.zeros((PAIR, 2 * size), F32),
    )
    carry = tile(i, carry, True)
    largest, total, acc = lax.fori_loop(0, i, lambda j, c: tile(j, c, False), carry)
    mixed[rows, pl.ds(column, PAIR)] = fold_heads(acc / total).astype(BF)
    totals[hp, i] = largest + jnp.log(total)


def attention_kernel(
    sizes,
    image, gain, shift, qkv, text, kv, so, cq, co, mi, mo,
    projected, normed, mixed, totals, mixed_rows, text_proj, so_full, cq_full, co_full, mi_full, mo_full,
    text_own, small_send, small_recv, small_own, wide_send, wide_recv, wide_own,
    mix_send, mix_recv, mix_own, text_send, text_recv, text_local,
):
    place = Place(sizes)
    n, share = place.n, place.share
    rows = image.shape[0]
    size = rows // n
    local = so.shape[0]
    offsets = list(range(1, n))
    greet = [place.peer(k) for k in offsets]
    greet += [place.chip_peer(k)[0] for k in range(1, share // 2)]
    greet.append(place.partner)
    barrier(greet)

    small = [
        Gather(place, own, full, offsets, lambda s: s, (small_send.at[t], small_recv.at[t], small_own.at[t]))
        for t, (own, full) in enumerate(((so, so_full), (cq, cq_full), (co, co_full)))
    ]
    wide = [
        Gather(place, own, full, list(range(2, n, 2)), lambda s: s // 2, (wide_send.at[t], wide_recv.at[t], wide_own.at[t]))
        for t, (own, full) in enumerate(((mi, mi_full), (mo, mo_full)))
    ]
    for item in small + wide:
        item.step(0)

    def project(i, _):
        block = pl.ds(pl.multiple_of(i * size, size), size)
        normal, _ = norm_parts(image[block, :].astype(F32))
        row = (normal * gain[...] + shift[...]).astype(BF)
        normed[block, :] = row
        projected[block, :] = nn(row, qkv[...]).astype(BF)
        return 0

    lax.fori_loop(0, n, project, 0)
    text_own[...] = nn(text[...], kv[...]).astype(BF)

    def text_copy(k):
        return pltpu.make_async_remote_copy(
            src_ref=text_own, dst_ref=text_proj.at[place.m],
            send_sem=text_send.at[k], recv_sem=text_recv.at[k],
            device_id=place.peer(k), device_id_type=MESH,
        )

    for k in offsets:
        text_copy(k).start()
    text_keep = pltpu.make_async_copy(text_own, text_proj.at[place.m], text_local)
    text_keep.start()

    def mix_copy(i):
        gap = lax.rem(i - place.m + n, n)
        block = pl.ds(pl.multiple_of(i * size, size), size)
        return pltpu.make_async_remote_copy(
            src_ref=mixed.at[block, :], dst_ref=mixed_rows.at[place.m],
            send_sem=mix_send.at[gap], recv_sem=mix_recv.at[gap],
            device_id=(place.d, i), device_id_type=MESH,
        )

    def mix_keep():
        block = pl.ds(pl.multiple_of(place.m * size, size), size)
        return pltpu.make_async_copy(mixed.at[block, :], mixed_rows.at[place.m], mix_own)

    plan = [(small[0], 1), (small[1], 1), (small[0], 2), (small[2], 1), (small[1], 2), (small[2], 2)]
    plan += [(wide[0], 1), (wide[1], 1), (wide[0], 2), (wide[1], 2)]
    each = -(-len(plan) // n)
    for i in range(n):
        lax.fori_loop(0, local // PAIR, lambda hp, _: (attend_block(projected, mixed, totals, i, hp, size, local), 0)[1], 0)

        @pl.when(place.m != i)
        def _():
            mix_copy(i).start()

        @pl.when(place.m == i)
        def _():
            mix_keep().start()

        for item, number in plan[i * each : (i + 1) * each]:
            item.step(number)

    for item in small + wide:
        item.step(3)
    for k in offsets:
        text_copy(k).wait()
    text_keep.wait()
    for k in offsets:
        mix_copy(place.along(k)).wait()
    mix_keep().wait()


def share_of(local, dp):
    share = dp
    while (local // share) % 16:
        share //= 2
    return share


def attention(sizes, image, gain, shift, qkv, text, kv, so, cq, co, mi, mo):
    n, share = sizes["mp"], sizes["share"]
    rows, width = image.shape
    slots = text.shape[0]
    local, hidden = so.shape[0], mi.shape[1]
    size = rows // n
    pairs = local // PAIR
    hops = share // 2 + 1
    half = max(n // 2, 1)
    vmem, hbm = pl.BlockSpec(memory_space=pltpu.VMEM), pl.BlockSpec(memory_space=pl.ANY)
    dma = pltpu.SemaphoreType.DMA
    return pl.pallas_call(
        partial(attention_kernel, sizes),
        out_shape=[
            jax.ShapeDtypeStruct((rows, 3 * local), BF),
            jax.ShapeDtypeStruct((rows, width), BF),
            jax.ShapeDtypeStruct((rows, local), BF),
            jax.ShapeDtypeStruct((pairs, n, 1, 2 * size), F32),
            jax.ShapeDtypeStruct((n, size, local), BF),
            jax.ShapeDtypeStruct((n, slots, 2 * local), BF),
            jax.ShapeDtypeStruct((n, local, width), BF),
            jax.ShapeDtypeStruct((n, width, local), BF),
            jax.ShapeDtypeStruct((n, local, width), BF),
            jax.ShapeDtypeStruct((half, width, hidden), BF),
            jax.ShapeDtypeStruct((half, hidden, width), BF),
        ],
        in_specs=[vmem] * 6 + [hbm] * 5,
        out_specs=[vmem] * 4 + [hbm] * 7,
        scratch_shapes=[
            pltpu.VMEM((slots, 2 * local), BF),
            dma((3, n - 1, hops)), dma((3, n - 1, hops)), dma((3,)),
            dma((2, half - 1, hops)), dma((2, half - 1, hops)), dma((2,)),
            dma((n,)), dma((n,)), dma(()),
            dma((n,)), dma((n,)), dma(()),
        ],
        compiler_params=pltpu.CompilerParams(collective_id=1, has_side_effects=True, vmem_limit_bytes=VMEM_LIMIT),
        cost_estimate=pl.CostEstimate(flops=6 << 30, bytes_accessed=32 << 20, transcendentals=4 << 20),
    )(image, gain, shift, qkv, text, kv, so, cq, co, mi, mo)


def row_norm(value, gain, shift):
    normal, inverse = norm_parts(value)
    return (normal * gain + shift).astype(BF), normal, inverse


def norm_back(grad, normal, inverse, gain):
    scaled = grad * gain
    return inverse * (
        scaled
        - jnp.mean(scaled, axis=-1, keepdims=True)
        - normal * jnp.mean(scaled * normal, axis=-1, keepdims=True)
    )


def swap_pairs(value, n):
    return lax.ppermute(value, "mp", [(s, s + 1 - 2 * (s % 2)) for s in range(n)])


def split_heads(value):
    return value.reshape(value.shape[0], -1, HEAD_DIM)


def middle(n, image_rows, grad_rows, grad_pair, length, mixed_rows, text_proj, so, cq, co, mi, mo, in_bias, out_bias,
           gain2, shift2, gain3, shift3):
    size, width = image_rows.shape
    local = so.shape[1]
    mixed = jnp.concatenate(list(mixed_rows), axis=1)
    so, co = so.reshape(-1, width), co.reshape(-1, width)
    cq = jnp.concatenate(list(cq), axis=1)
    first = image_rows + nn(mixed, so)
    n2, normal2, inverse2 = row_norm(first, gain2, shift2)
    query = split_heads(nn(n2, cq).astype(BF))
    keys = split_heads(jnp.concatenate([t[:, :local] for t in text_proj], axis=1))
    values = split_heads(jnp.concatenate([t[:, local:] for t in text_proj], axis=1))
    scores = jnp.einsum("qhe,khe->hqk", query, keys, preferred_element_type=F32) * SCALE
    scores = jnp.where(lax.iota(jnp.int32, keys.shape[0]) < length, scores, MASKED)
    weights = jax.nn.softmax(scores, axis=-1)
    rounded = weights.astype(BF)
    cross = jnp.einsum("hqk,khe->qhe", rounded, values, preferred_element_type=F32).astype(BF).reshape(size, -1)
    second = first + nn(cross, co)
    n3, normal3, inverse3 = row_norm(second, gain3, shift3)
    n3_pair = jnp.stack([n3, swap_pairs(n3, n)])
    hidden = jnp.einsum("psd,kdf->pksf", n3_pair, mi, preferred_element_type=F32) + in_bias[None, :, None, :]
    active, gelu_back = jax.vjp(partial(jax.nn.gelu, approximate=False), hidden)
    active = active.astype(BF)
    out_part = jnp.einsum("pksf,kfd->psd", active, mo, preferred_element_type=F32)
    out = second + out_part[0] + swap_pairs(out_part[1].astype(BF), n).astype(F32) + out_bias
    grad_active = jnp.einsum("psd,kfd->pksf", grad_pair, mo, preferred_element_type=F32)
    grad_hidden = gelu_back(grad_active)[0].astype(BF)
    mo_grad = jnp.einsum("pksf,psd->kfd", active, grad_pair, preferred_element_type=F32)
    mi_grad = jnp.einsum("psd,pksf->kdf", n3_pair, grad_hidden, preferred_element_type=F32)
    in_bias_grad = jnp.sum(grad_hidden.astype(F32), axis=(0, 2))
    dn3_part = jnp.einsum("pksf,kdf->psd", grad_hidden, mi, preferred_element_type=F32)
    dn3 = dn3_part[0] + swap_pairs(dn3_part[1].astype(BF), n).astype(F32)
    residual = grad_rows + norm_back(dn3, normal3, inverse3, gain3)
    r2 = residual.astype(BF)
    co_grad = tn(cross, r2)
    dcross = split_heads(nt(r2, co).astype(BF))
    dweights = jnp.einsum("qhe,khe->hqk", dcross, values, preferred_element_type=F32)
    dscores = weights * (dweights - jnp.sum(weights * dweights, axis=-1, keepdims=True)) * SCALE
    dscores = dscores.astype(BF)
    dquery = jnp.einsum("hqk,khe->qhe", dscores, keys, preferred_element_type=F32).astype(BF).reshape(size, -1)
    dkeys = jnp.einsum("hqk,qhe->khe", dscores, query, preferred_element_type=F32).reshape(keys.shape[0], -1)
    dvalues = jnp.einsum("hqk,qhe->khe", rounded, dcross, preferred_element_type=F32).reshape(keys.shape[0], -1)
    dtext = jnp.concatenate(
        [t[:, g * local : (g + 1) * local] for g in range(n) for t in (dkeys, dvalues)], axis=1
    ).astype(BF)
    cq_grad = tn(n2, dquery)
    dn2 = nt(dquery, cq)
    residual = residual + norm_back(dn2, normal2, inverse2, gain2)
    r1 = residual.astype(BF)
    so_grad = tn(mixed, r1)
    dmixed = nt(r1, so).astype(BF)
    dmixed = jnp.stack([dmixed[:, g * local : (g + 1) * local] for g in range(n)])
    dmixed = lax.all_to_all(dmixed, "mp", 0, 0)
    vectors = [
        jnp.sum(dn2 * normal2, axis=0), jnp.sum(dn2, axis=0), jnp.sum(dn3 * normal3, axis=0), jnp.sum(dn3, axis=0),
        jnp.sum(grad_rows, axis=0),
    ]
    return (out.astype(BF), residual, dmixed.reshape(-1, local), dtext, so_grad, cq_grad, co_grad, mi_grad, mo_grad,
            in_bias_grad, vectors)


def attention_back(n, projected, totals, dmixed, local):
    rows = projected.shape[0]
    heads = local // HEAD_DIM
    q, k, v = (split_heads(projected[:, t * local : (t + 1) * local]) for t in range(3))
    size = rows // n
    log_total = totals.reshape(heads // 2, n, 2, size).transpose(0, 2, 1, 3).reshape(heads, rows)
    scores = jnp.einsum("qhe,khe->hqk", q, k, preferred_element_type=F32) * SCALE
    keep = lax.iota(jnp.int32, rows)[:, None] >= lax.iota(jnp.int32, rows)[None, :]
    weights = jnp.exp(jnp.where(keep, scores, MASKED) - log_total[:, :, None])
    do = split_heads(dmixed)
    dweights = jnp.einsum("qhe,khe->hqk", do, v, preferred_element_type=F32)
    dscores = weights * (dweights - jnp.sum(weights * dweights, axis=-1, keepdims=True)) * SCALE
    dscores = dscores.astype(BF)
    dq = jnp.einsum("hqk,khe->qhe", dscores, k, preferred_element_type=F32)
    dk = jnp.einsum("hqk,qhe->khe", dscores, q, preferred_element_type=F32)
    dv = jnp.einsum("hqk,qhe->khe", weights.astype(BF), do, preferred_element_type=F32)
    return jnp.concatenate([t.reshape(rows, local) for t in (dq, dk, dv)], axis=1).astype(BF)


def body(sizes, image, text, grad_out, lengths, gain1, shift1, qkv, so, gain2, shift2, cq, kv, co, gain3, shift3, mi,
         in_bias, mo, out_bias):
    n = sizes["mp"]
    image, text, grad_out = image[0], text[0], grad_out[0]
    rows, width = image.shape
    size = rows // n
    local = so.shape[0]
    m = lax.axis_index("mp")
    sizes = dict(sizes, share=share_of(local, sizes["dp"]))
    qkv, kv = qkv.reshape(width, 3 * local), kv.reshape(width, 2 * local)
    own = lambda value: lax.dynamic_slice_in_dim(value, m * size, size, 0)
    (projected, normed1, mixed, totals, mixed_rows, text_proj, so_full, cq_full, co_full, mi_full, mo_full) = attention(
        sizes, image, gain1[None], shift1[None], qkv, text, kv, so, cq, co, mi, mo)
    bias_full = lax.all_gather(in_bias, "mp").reshape(n // 2, 2, -1)[:, m % 2]
    image_rows = own(image).astype(F32)
    grad_rows = own(grad_out)
    other = lax.dynamic_slice_in_dim(grad_out, (m + 1 - 2 * (m % 2)) * size, size, 0)
    (out, residual, dmixed, dtext, so_grad, cq_grad, co_grad, mi_grad, mo_grad, in_bias_grad, vectors) = middle(
        n, image_rows, grad_rows.astype(F32), jnp.stack([grad_rows, other]), lengths[0], mixed_rows, text_proj,
        so_full, cq_full, co_full, mi_full, mo_full, bias_full, out_bias, gain2, shift2, gain3, shift3)
    dprojected = attention_back(n, projected, totals, dmixed, local)
    qkv_grad = tn(normed1, dprojected)
    dn1 = lax.psum_scatter(nt(dprojected, qkv).astype(BF), "mp", scatter_dimension=0, tiled=True).astype(F32)
    normal1, inverse1 = norm_parts(image_rows)
    image_grad = residual + norm_back(dn1, normal1, inverse1, gain1)
    dtext = lax.psum_scatter(dtext, "mp", scatter_dimension=1, tiled=True)
    kv_grad = tn(text, dtext)
    text_grad = lax.psum_scatter(nt(dtext, kv).astype(BF), "mp", scatter_dimension=0, tiled=True).astype(F32)
    scatter = lambda value, dim: lax.psum_scatter(value.astype(BF), "mp", scatter_dimension=dim, tiled=True)
    so_grad, co_grad, cq_grad = scatter(so_grad, 0), scatter(co_grad, 0), scatter(cq_grad, 1)

    def own_shard(value):
        total = jnp.zeros((n,) + value.shape[1:], F32)
        for j in range(n // 2):
            total = lax.dynamic_update_index_in_dim(total, value[j], 2 * j + m % 2, 0)
        return lax.psum_scatter(total.astype(BF), "mp", scatter_dimension=0, tiled=True)[0]

    mi_grad, mo_grad, in_bias_grad = own_shard(mi_grad), own_shard(mo_grad), own_shard(in_bias_grad)
    total = lambda value: lax.psum(value.astype(BF), "dp").astype(F32)
    vectors = [jnp.sum(dn1 * normal1, axis=0), jnp.sum(dn1, axis=0)] + vectors
    g1, s1, g2, s2, g3, s3, ob = lax.psum(tuple(vectors), ("dp", "mp"))
    return (
        out[None], image_grad[None], text_grad[None], g1, s1, total(qkv_grad).reshape(width, 3, local), total(so_grad),
        g2, s2, total(cq_grad), total(kv_grad).reshape(width, 2, local), total(co_grad), g3, s3, total(mi_grad),
        total(in_bias_grad), total(mo_grad), ob,
    )


def solution(mesh):
    rows3, rows2, rows1 = P(None, None, "mp"), P(None, "mp"), P("mp")
    item = P("dp", None, None)
    in_specs = (item, item, item, P("dp"), P(), P(), rows3, P("mp", None), P(), P(), rows2, rows3, P("mp", None), P(), P(),
                rows2, rows1, P("mp", None), P())
    split = P("dp", "mp", None)
    out_specs = (split, split, split, P(), P(), rows3, P("mp", None), P(), P(), rows2, rows3, P("mp", None), P(), P(),
                 rows2, rows1, P("mp", None), P())
    sizes = dict(mesh.shape)
    return jax.shard_map(partial(body, sizes), mesh=mesh, in_specs=in_specs, out_specs=out_specs, check_vma=False)
```

```python
from functools import partial

import jax
import jax.numpy as jnp
from jax import lax
from jax.experimental import pallas as pl
from jax.experimental.pallas import tpu as pltpu
from jax.sharding import PartitionSpec as P

HEAD_DIM = 64
PAIR = 2 * HEAD_DIM
EPSILON = 1e-05
SCALE = HEAD_DIM ** (-0.5)
MASKED = -1e30
BF = jnp.bfloat16
F32 = jnp.float32
MESH = pl.DeviceIdType.MESH
VMEM_LIMIT = 56 << 20


def nn(a, b):
    return lax.dot_general(a, b, (((1,), (0,)), ((), ())), preferred_element_type=F32)


def nt(a, b):
    return lax.dot_general(a, b, (((1,), (1,)), ((), ())), preferred_element_type=F32)


def tn(a, b):
    return lax.dot_general(a, b, (((0,), (0,)), ((), ())), preferred_element_type=F32)


def norm_parts(value):
    center = value - jnp.mean(value, axis=-1, keepdims=True)
    inverse = lax.rsqrt(jnp.mean(center * center, axis=-1, keepdims=True) + EPSILON)
    return center * inverse, inverse


def half_masks():
    lane = lax.broadcasted_iota(jnp.int32, (1, PAIR), 1)
    first = jnp.where(lane < HEAD_DIM, 1.0, 0.0)
    return first, 1.0 - first


def stack_heads(pair, scale=None):
    first, second = half_masks()
    if scale is not None:
        first, second = first * scale, second * scale
    wide = pair.astype(F32)
    return jnp.concatenate([wide * first, wide * second], axis=0).astype(BF)


def fold_heads(stacked):
    rows = stacked.shape[1] // 2
    both = jnp.concatenate([stacked[:HEAD_DIM, :rows], stacked[HEAD_DIM:, rows:]], axis=0)
    return both.T


def causal(tile_keys, tile_rows):
    key = lax.broadcasted_iota(jnp.int32, (tile_keys, tile_rows), 0)
    row = lax.broadcasted_iota(jnp.int32, (tile_keys, tile_rows), 1)
    both = key <= row
    return jnp.concatenate([both, both], axis=1)


class Place:
    def __init__(self, sizes):
        self.n = sizes["mp"]
        self.dp = sizes["dp"]
        self.share = sizes["share"]
        self.d = lax.axis_index("dp")
        self.m = lax.axis_index("mp")
        self.core = lax.rem(self.d, 2)
        self.partner = (self.d + 1 - 2 * self.core, self.m)
        self.member = lax.rem(self.d, self.share)
        self.chip = self.member // 2
        self.base = self.d - self.member
        self.piece = self.core * (self.share // 2) + self.chip

    def along(self, offset):
        return lax.rem(self.m + offset, self.n)

    def peer(self, offset):
        return (self.d, self.along(offset))

    def chip_peer(self, offset):
        chip = lax.rem(self.chip + offset, self.share // 2)
        return (self.base + 2 * chip + self.core, self.m), self.core * (self.share // 2) + chip


def barrier(devices):
    sem = pltpu.get_barrier_semaphore()
    for device in devices:
        pl.semaphore_signal(sem, inc=1, device_id=device, device_id_type=MESH)
    pl.semaphore_wait(sem, len(devices))


class Gather:
    def __init__(self, place, own, full, offsets, slot_of, sems):
        self.place, self.own, self.full, self.offsets, self.slot_of = place, own, full, offsets, slot_of
        self.rows = own.shape[0]
        self.count = self.rows // place.share
        self.sems = sems

    def rows_of(self, slot, piece, pieces=1):
        start = pl.multiple_of(piece * self.count, self.count)
        return self.full.at[slot, pl.ds(start, pieces * self.count), :]

    def first(self, index):
        place, offset = self.place, self.offsets[index]
        start = pl.multiple_of(place.piece * self.count, self.count)
        return pltpu.make_async_remote_copy(
            src_ref=self.own.at[pl.ds(start, self.count), :],
            dst_ref=self.rows_of(self.slot_of(place.m), place.piece),
            send_sem=self.sems[0].at[index, 0],
            recv_sem=self.sems[1].at[index, 0],
            device_id=place.peer(offset),
            device_id_type=MESH,
        )

    def slot(self, index):
        place = self.place
        return self.slot_of(place.along(place.n - self.offsets[index]))

    def second(self, index, hop):
        place = self.place
        device, _ = place.chip_peer(hop)
        block = self.rows_of(self.slot(index), place.piece)
        return pltpu.make_async_remote_copy(
            src_ref=block,
            dst_ref=block,
            send_sem=self.sems[0].at[index, hop],
            recv_sem=self.sems[1].at[index, hop],
            device_id=device,
            device_id_type=MESH,
        )

    def third(self, index):
        place = self.place
        half = place.share // 2
        block = self.rows_of(self.slot(index), place.core * half, half)
        return pltpu.make_async_remote_copy(
            src_ref=block,
            dst_ref=block,
            send_sem=self.sems[0].at[index, half],
            recv_sem=self.sems[1].at[index, half],
            device_id=place.partner,
            device_id_type=MESH,
        )

    def local(self):
        return pltpu.make_async_copy(self.own, self.full.at[self.slot_of(self.place.m)], self.sems[2])

    def step(self, number):
        hops = range(1, self.place.share // 2)
        for index in range(len(self.offsets)):
            if number == 0:
                self.first(index).start()
            elif number == 1:
                self.first(index).wait_recv()
                for hop in hops:
                    self.second(index, hop).start()
            elif number == 2:
                for hop in hops:
                    self.second(index, hop).wait_recv()
                self.third(index).start()
            else:
                self.third(index).wait()
                self.first(index).wait_send()
                for hop in hops:
                    self.second(index, hop).wait_send()

    def finish(self):
        self.step(3)
        self.local().wait()


def attend_block(projected, mixed, totals, i, hp, size, local):
    rows = pl.ds(pl.multiple_of(i * size, size), size)
    column = pl.multiple_of(hp * PAIR, PAIR)
    query = stack_heads(projected[rows, pl.ds(column, PAIR)], SCALE)

    def tile(j, carry, diagonal):
        largest, total, acc = carry
        keys = pl.ds(pl.multiple_of(j * size, size), size)
        key = projected[keys, pl.ds(column + local, PAIR)]
        value = projected[keys, pl.ds(column + 2 * local, PAIR)]
        scores = nt(key, query)
        if diagonal:
            scores = jnp.where(causal(size, size), scores, MASKED)
        top = jnp.maximum(largest, jnp.max(scores, axis=0, keepdims=True))
        powers = jnp.exp(scores - top)
        shrink = jnp.exp(largest - top)
        total = total * shrink + jnp.sum(powers, axis=0, keepdims=True)
        acc = acc * shrink + tn(value, powers.astype(BF))
        return top, total, acc

    carry = (
        jnp.full((1, 2 * size), MASKED, F32),
        jnp.zeros((1, 2 * size), F32),
        jnp.zeros((PAIR, 2 * size), F32),
    )
    carry = tile(i, carry, True)
    largest, total, acc = lax.fori_loop(0, i, lambda j, c: tile(j, c, False), carry)
    mixed[rows, pl.ds(column, PAIR)] = fold_heads(acc / total).astype(BF)
    totals[hp, i] = largest + jnp.log(total)


def share_of(local, dp):
    share = dp
    while (local // share) % 16:
        share //= 2
    return share


def norm_back(grad, normal, inverse, gain):
    scaled = grad * gain
    return inverse * (
        scaled
        - jnp.mean(scaled, axis=-1, keepdims=True)
        - normal * jnp.mean(scaled * normal, axis=-1, keepdims=True)
    )


def add_rows(ref, index, value):
    ref[pl.ds(index, 1), :] += jnp.sum(value, axis=0, keepdims=True)


def in_chunks(total, chunk, step):
    def run(i, _):
        step(pl.ds(pl.multiple_of(i * chunk, chunk), chunk))
        return 0

    lax.fori_loop(0, total // chunk, run, 0)


def cross_pair(query, text_proj, length, idx, local):
    per = local // PAIR
    g, hp = idx // per, lax.rem(idx, per)
    near = pl.multiple_of(hp * PAIR, PAIR)
    column = pl.multiple_of(idx * PAIR, PAIR)
    stacked = stack_heads(query[:, pl.ds(column, PAIR)], SCALE)
    key = text_proj[g, :, pl.ds(near, PAIR)]
    value = text_proj[g, :, pl.ds(near + local, PAIR)]
    scores = nt(key, stacked)
    slot = lax.broadcasted_iota(jnp.int32, scores.shape, 0)
    return g, near, column, stacked, key, value, jnp.where(slot < length, scores, MASKED)


ROWS_AT_ONCE = 32


def layer_kernel(
    sizes,
    image, gain1, shift1, qkv, text, kv, length, gain2, shift2, gain3, shift3, in_bias, out_bias,
    so, cq, co, mi, mo, grad_out,
    projected, normed, mixed, totals, out, residual, dmixed, dtext, so_grad, cq_grad, co_grad, mi_grad, mo_grad,
    bias_grad, vectors,
    mixed_rows, text_proj, so_full, cq_full, co_full, mi_full, mo_full, bias_full,
    grad_pair, mixed_all, first, second, work, grad2, out_part,
    n2, query, cross, cross_totals, dquery, n3_pair, active, dhidden,
    dn3_send, dn3_recv, out_send, out_recv, r2, dcross, r1, dmixed_send, dtext_send, dtext_recv,
    text_own, so_keep, co_keep, small_send, small_recv, small_own, wide_send, wide_recv, wide_own,
    mix_send, mix_recv, mix_own, text_send, text_recv, bias_send, bias_recv, load_sem,
    pair_send, pair_recv, dmix_send, dmix_recv, dtext_ssem, dtext_rsem, store_sem,
):
    place = Place(sizes)
    n, share = place.n, place.share
    rows, width = image.shape
    size = rows // n
    local, hidden = so.shape[0], mi.shape[1]
    half = n // 2
    offsets = list(range(1, n))
    parity = lax.rem(place.m, 2)
    mate = (place.d, place.m + 1 - 2 * parity)
    mine = place.m // 2
    greet = [place.peer(k) for k in offsets]
    greet += [place.chip_peer(k)[0] for k in range(1, share // 2)]
    greet.append(place.partner)
    barrier(greet)

    def remote(src, dst, send, recv, device):
        return pltpu.make_async_remote_copy(
            src_ref=src, dst_ref=dst, send_sem=send, recv_sem=recv, device_id=device, device_id_type=MESH
        )

    small = [
        Gather(place, own, full, offsets, lambda s: s, (small_send.at[t], small_recv.at[t], small_own.at[t]))
        for t, (own, full) in enumerate(((so, so_full), (cq, cq_full), (co, co_full)))
    ]
    wide = [
        Gather(place, own, full, list(range(2, n, 2)), lambda s: s // 2, (wide_send.at[t], wide_recv.at[t], wide_own.at[t]))
        for t, (own, full) in enumerate(((mi, mi_full), (mo, mo_full)))
    ]
    for item in small:
        item.step(0)
    for item in small + wide:
        item.local().start()

    def block_of(index):
        return pl.ds(pl.multiple_of(index * size, size), size)

    own_rows = block_of(place.m)
    loads = [
        pltpu.make_async_copy(grad_out.at[own_rows, :], grad_pair.at[0], load_sem.at[0]),
        pltpu.make_async_copy(grad_out.at[block_of(mate[1]), :], grad_pair.at[1], load_sem.at[1]),
    ]
    for load in loads:
        load.start()
    bias_full[mine] = in_bias[...]

    def bias_copy(k):
        return remote(in_bias, bias_full.at[mine], bias_send.at[k], bias_recv.at[k], place.peer(2 * k))

    for k in range(1, half):
        bias_copy(k).start()

    def project(i, _):
        block = block_of(i)

        def norm(chunk):
            at = pl.ds(pl.multiple_of(i * size + chunk.start, ROWS_AT_ONCE), ROWS_AT_ONCE)
            normal, _ = norm_parts(image[at, :].astype(F32))
            normed[at, :] = (normal * gain1[...] + shift1[...]).astype(BF)

        in_chunks(size, ROWS_AT_ONCE, norm)
        projected[block, :] = nn(normed[block, :], qkv[...]).astype(BF)
        return 0

    lax.fori_loop(0, n, project, 0)
    text_own[...] = nn(text[...], kv[...]).astype(BF)
    text_proj[place.m] = text_own[...]

    def text_copy(k):
        return remote(text_own, text_proj.at[place.m], text_send.at[k], text_recv.at[k], place.peer(k))

    for k in offsets:
        text_copy(k).start()

    def mix_copy(i):
        gap = lax.rem(i - place.m + n, n)
        return remote(mixed.at[block_of(i), :], mixed_rows.at[place.m], mix_send.at[gap], mix_recv.at[gap], (place.d, i))

    mix_keep = pltpu.make_async_copy(mixed.at[own_rows, :], mixed_rows.at[place.m], mix_own)
    plan = [(small[0], 1), (small[1], 1), (small[0], 2), (small[2], 1), (small[1], 2), (small[2], 2)]
    plan += [(wide[0], 0), (wide[1], 0)]
    each = -(-len(plan) // n)
    for i in range(n):
        lax.fori_loop(0, local // PAIR, lambda hp, _: (attend_block(projected, mixed, totals, i, hp, size, local), 0)[1], 0)

        @pl.when(place.m != i)
        def _():
            mix_copy(i).start()

        @pl.when(place.m == i)
        def _():
            mix_keep.start()

        for item, number in plan[i * each : (i + 1) * each]:
            item.step(number)

    for k in offsets:
        mix_copy(place.along(k)).wait()
    mix_keep.wait()
    small[0].finish()
    for g in range(n):
        mixed_all[:, g * local : (g + 1) * local] = mixed_rows[g]
    first[...] = nn(mixed_all[...], so_full[...].reshape(n * local, width))

    def first_norm(chunk):
        at = pl.ds(pl.multiple_of(place.m * size + chunk.start, ROWS_AT_ONCE), ROWS_AT_ONCE)
        value = image[at, :].astype(F32) + first[chunk, :]
        first[chunk, :] = value
        n2[chunk, :] = (norm_parts(value)[0] * gain2[...] + shift2[...]).astype(BF)

    in_chunks(size, ROWS_AT_ONCE, first_norm)
    small[1].finish()
    for g in range(n):
        query[:, g * local : (g + 1) * local] = nn(n2[...], cq_full[g]).astype(BF)
    for k in offsets:
        text_copy(k).wait()
    for item in wide:
        item.step(1)
    limit = length[0, 0]
    all_pairs = n * local // PAIR

    def cross_forward(idx, _):
        g, near, column, stacked, key, value, scores = cross_pair(query, text_proj, limit, idx, local)
        largest = jnp.max(scores, axis=0, keepdims=True)
        powers = jnp.exp(scores - largest)
        total = jnp.sum(powers, axis=0, keepdims=True)
        cross_totals[idx] = largest + jnp.log(total)
        cross[:, pl.ds(column, PAIR)] = fold_heads(tn(value, (powers / total).astype(BF))).astype(BF)
        return 0

    lax.fori_loop(0, all_pairs, cross_forward, 0)
    small[2].finish()
    second[...] = nn(cross[...], co_full[...].reshape(n * local, width))

    def second_norm(chunk):
        value = first[chunk, :] + second[chunk, :]
        second[chunk, :] = value
        n3_pair[0, chunk, :] = (norm_parts(value)[0] * gain3[...] + shift3[...]).astype(BF)

    in_chunks(size, ROWS_AT_ONCE, second_norm)

    n3_copy = remote(n3_pair.at[0], n3_pair.at[1], pair_send.at[0], pair_recv.at[0], mate)
    n3_copy.start()
    for load in loads:
        load.wait()
    for k in range(1, half):
        bias_copy(k).wait()
    for item in wide:
        item.local().wait()
    step = min(256, hidden)

    def feed(p, slot):
        grads = grad_pair[p]

        def chunk(c, _):
            columns = pl.ds(pl.multiple_of(c * step, step), step)
            value = nn(n3_pair[p], mi_full[slot, :, columns]) + bias_full[slot, :, columns]
            inner = 0.5 * (1.0 + lax.erf(value * (0.5**0.5)))
            slope = inner + value * jnp.exp(-0.5 * value * value) * ((2.0 * jnp.pi) ** -0.5)
            active[slot, p, :, columns] = (value * inner).astype(BF)
            dhidden[slot, p, :, columns] = (nt(grads, mo_full[slot, columns, :]) * slope).astype(BF)
            return 0

        lax.fori_loop(0, hidden // step, chunk, 0)

    def sum_slots(term):
        total = term(0)
        for slot in range(1, half):
            total += term(slot)
        return total

    feed(0, mine)
    n3_copy.wait()
    feed(1, mine)
    for item in wide:
        item.step(2)
    for item in wide:
        item.step(3)
    others = [lax.rem(mine + k, half) for k in range(1, half)]
    for slot in others:
        feed(1, slot)
    dn3_send[...] = sum_slots(lambda slot: nt(dhidden[slot, 1], mi_full[slot])).astype(BF)
    dn3_copy = remote(dn3_send, dn3_recv, pair_send.at[1], pair_recv.at[1], mate)
    dn3_copy.start()
    out_send[...] = sum_slots(lambda slot: nn(active[slot, 1], mo_full[slot])).astype(BF)
    out_copy = remote(out_send, out_recv, pair_send.at[2], pair_recv.at[2], mate)
    out_copy.start()
    for slot in others:
        feed(0, slot)
    work[...] = sum_slots(lambda slot: nt(dhidden[slot, 0], mi_full[slot]))
    out_part[...] = sum_slots(lambda slot: nn(active[slot, 0], mo_full[slot]))
    dn3_copy.wait()

    vectors[...] = jnp.zeros_like(vectors)

    def third_back(chunk):
        grad = work[chunk, :] + dn3_recv[chunk, :].astype(F32)
        normal, inverse = norm_parts(second[chunk, :])
        above = grad_pair[0, chunk, :].astype(F32)
        add_rows(vectors, 4, grad * normal)
        add_rows(vectors, 5, grad)
        add_rows(vectors, 6, above)
        value = above + norm_back(grad, normal, inverse, gain3[...])
        work[chunk, :] = value
        r2[chunk, :] = value.astype(BF)

    in_chunks(size, ROWS_AT_ONCE, third_back)
    dcross[...] = nt(r2[...], co_full[...].reshape(n * local, width)).astype(BF)

    def cross_back(idx, _):
        g, near, column, stacked, key, value, scores = cross_pair(query, text_proj, limit, idx, local)
        weights = jnp.exp(scores - cross_totals[idx])
        above = stack_heads(dcross[:, pl.ds(column, PAIR)])
        dweights = nt(value, above)
        dscores = (weights * (dweights - jnp.sum(weights * dweights, axis=0, keepdims=True))).astype(BF)
        dquery[:, pl.ds(column, PAIR)] = (fold_heads(tn(key, dscores)) * SCALE).astype(BF)
        dtext_send[g, :, pl.ds(near, PAIR)] = nn(dscores, stacked).astype(BF)
        dtext_send[g, :, pl.ds(near + local, PAIR)] = nn(weights.astype(BF), above).astype(BF)
        return 0

    lax.fori_loop(0, all_pairs, cross_back, 0)

    def dtext_copy(k):
        return remote(dtext_send.at[place.along(k)], dtext_recv.at[place.m], dtext_ssem.at[k], dtext_rsem.at[k], place.peer(k))

    for k in offsets:
        dtext_copy(k).start()
    def both(term):
        total = term(0)
        for g in range(1, n):
            total += term(g)
        return total

    grad2[...] = both(lambda g: nt(dquery[:, g * local : (g + 1) * local], cq_full[g]))

    def second_back(chunk):
        grad = grad2[chunk, :]
        normal, inverse = norm_parts(first[chunk, :])
        add_rows(vectors, 2, grad * normal)
        add_rows(vectors, 3, grad)
        value = work[chunk, :] + norm_back(grad, normal, inverse, gain2[...])
        residual[chunk, :] = value
        r1[chunk, :] = value.astype(BF)

    in_chunks(size, ROWS_AT_ONCE, second_back)

    def dmix_copy(k):
        return remote(dmixed_send.at[k], dmixed.at[own_rows, :], dmix_send.at[k], dmix_recv.at[k], place.peer(k))

    for k in offsets:
        dmixed_send[k] = nt(r1[...], so_full[place.along(k)]).astype(BF)
        dmix_copy(k).start()
    dmixed[own_rows, :] = nt(r1[...], so_full[place.m]).astype(BF)

    tile = min(256, width)

    def wide_grads(slot):
        inner = n3_pair.shape[0] * size
        hidden_grad = dhidden[slot].reshape(inner, hidden)
        grads = grad_pair[...].reshape(inner, width)
        bias_grad[slot] = jnp.sum(hidden_grad.astype(F32), axis=0, keepdims=True)

        def into(t, _):
            at = pl.ds(pl.multiple_of(t * tile, tile), tile)
            mi_full[slot, at, :] = tn(n3_pair[:, :, at].reshape(inner, tile), hidden_grad).astype(BF)
            return 0

        lax.fori_loop(0, width // tile, into, 0)

        def back(t, _):
            at = pl.ds(pl.multiple_of(t * step, step), step)
            mo_full[slot, at, :] = tn(active[slot, :, :, at].reshape(inner, step), grads).astype(BF)
            return 0

        lax.fori_loop(0, hidden // step, back, 0)

    for slot in range(half):
        wide_grads(slot)
    stores = [
        pltpu.make_async_copy(mi_full, mi_grad, store_sem.at[0]),
        pltpu.make_async_copy(mo_full, mo_grad, store_sem.at[1]),
    ]
    for store in stores:
        store.start()

    def small_grad(left, right, keep, target, index):
        def into(t, _):
            at = pl.ds(pl.multiple_of(t * tile, tile), tile)
            turned = left[:, at]
            for g in range(n):
                keep[g, at, :] = tn(turned, right[:, g * local : (g + 1) * local]).astype(BF)
            return 0

        lax.fori_loop(0, width // tile, into, 0)
        copy = pltpu.make_async_copy(keep, target, store_sem.at[index])
        copy.start()
        stores.append(copy)

    small_grad(n2, dquery, cq_full, cq_grad, 2)
    small_grad(r1, mixed_all, so_keep, so_grad, 3)
    small_grad(r2, cross, co_keep, co_grad, 4)

    out_copy.wait()

    def finish_out(chunk):
        value = second[chunk, :] + out_part[chunk, :] + out_recv[chunk, :].astype(F32) + out_bias[...]
        out[chunk, :] = value.astype(BF)

    in_chunks(size, ROWS_AT_ONCE, finish_out)
    for k in offsets:
        dtext_copy(k).wait()
    total = dtext_send[place.m].astype(F32)
    for k in offsets:
        total += dtext_recv[place.along(k)].astype(F32)
    dtext[...] = total.astype(BF)
    for k in offsets:
        dmix_copy(k).wait()
    for store in stores:
        store.wait()


def layer(sizes, image, gain1, shift1, qkv, text, kv, length, gain2, shift2, gain3, shift3, in_bias, out_bias,
          so, cq, co, mi, mo, grad_out):
    n, share = sizes["mp"], sizes["share"]
    rows, width = image.shape
    slots = text.shape[0]
    local, hidden = so.shape[0], mi.shape[1]
    size = rows // n
    pairs = local // PAIR
    hops = share // 2 + 1
    half = n // 2
    vmem, hbm = pl.BlockSpec(memory_space=pltpu.VMEM), pl.BlockSpec(memory_space=pl.ANY)
    dma, mem = pltpu.SemaphoreType.DMA, pltpu.VMEM
    shape = jax.ShapeDtypeStruct
    few = max(half - 1, 1)
    return pl.pallas_call(
        partial(layer_kernel, sizes),
        out_shape=[
            shape((rows, 3 * local), BF), shape((rows, width), BF), shape((rows, local), BF),
            shape((pairs, n, 1, 2 * size), F32), shape((size, width), BF), shape((size, width), F32),
            shape((rows, local), BF), shape((slots, 2 * local), BF),
            shape((n, width, local), BF), shape((n, width, local), BF), shape((n, width, local), BF),
            shape((half, width, hidden), BF), shape((half, hidden, width), BF),
            shape((half, 1, hidden), F32), shape((8, width), F32),
        ],
        in_specs=[vmem] * 6 + [pl.BlockSpec(memory_space=pltpu.SMEM)] + [vmem] * 6 + [hbm] * 6,
        out_specs=[vmem] * 8 + [hbm] * 5 + [vmem] * 2,
        scratch_shapes=[
            mem((n, size, local), BF), mem((n, slots, 2 * local), BF),
            mem((n, local, width), BF), mem((n, width, local), BF), mem((n, local, width), BF),
            mem((half, width, hidden), BF), mem((half, hidden, width), BF), mem((half, 1, hidden), F32),
            mem((2, size, width), BF), mem((size, n * local), BF),
            mem((size, width), F32), mem((size, width), F32), mem((size, width), F32), mem((size, width), F32),
            mem((size, width), F32),
            mem((size, width), BF), mem((size, n * local), BF), mem((size, n * local), BF),
            mem((n * pairs, 1, 2 * size), F32), mem((size, n * local), BF),
            mem((2, size, width), BF), mem((half, 2, size, hidden), BF), mem((half, 2, size, hidden), BF),
            mem((size, width), BF), mem((size, width), BF), mem((size, width), BF), mem((size, width), BF),
            mem((size, width), BF), mem((size, n * local), BF), mem((size, width), BF),
            mem((n, size, local), BF), mem((n, slots, 2 * local), BF), mem((n, slots, 2 * local), BF),
            mem((slots, 2 * local), BF), mem((n, width, local), BF), mem((n, width, local), BF),
            dma((3, n - 1, hops)), dma((3, n - 1, hops)), dma((3,)),
            dma((2, few, hops)), dma((2, few, hops)), dma((2,)),
            dma((n,)), dma((n,)), dma(()),
            dma((n,)), dma((n,)), dma((half,)), dma((half,)), dma((2,)),
            dma((3,)), dma((3,)), dma((n,)), dma((n,)), dma((n,)), dma((n,)), dma((5,)),
        ],
        compiler_params=pltpu.CompilerParams(collective_id=1, has_side_effects=True, vmem_limit_bytes=VMEM_LIMIT),
        cost_estimate=pl.CostEstimate(flops=22 << 30, bytes_accessed=48 << 20, transcendentals=8 << 20),
    )(image, gain1, shift1, qkv, text, kv, length, gain2, shift2, gain3, shift3, in_bias, out_bias,
      so, cq, co, mi, mo, grad_out)


def split_heads(value):
    return value.reshape(value.shape[0], -1, HEAD_DIM)


def attention_back(n, projected, totals, dmixed, local):
    rows = projected.shape[0]
    heads = local // HEAD_DIM
    q, k, v = (split_heads(projected[:, t * local : (t + 1) * local]) for t in range(3))
    size = rows // n
    log_total = totals.reshape(heads // 2, n, 2, size).transpose(0, 2, 1, 3).reshape(heads, rows)
    scores = jnp.einsum("qhe,khe->hqk", q, k, preferred_element_type=F32) * SCALE
    keep = lax.iota(jnp.int32, rows)[:, None] >= lax.iota(jnp.int32, rows)[None, :]
    weights = jnp.exp(jnp.where(keep, scores, MASKED) - log_total[:, :, None])
    do = split_heads(dmixed)
    dweights = jnp.einsum("qhe,khe->hqk", do, v, preferred_element_type=F32)
    dscores = weights * (dweights - jnp.sum(weights * dweights, axis=-1, keepdims=True)) * SCALE
    dscores = dscores.astype(BF)
    dq = jnp.einsum("hqk,khe->qhe", dscores, k, preferred_element_type=F32)
    dk = jnp.einsum("hqk,qhe->khe", dscores, q, preferred_element_type=F32)
    dv = jnp.einsum("hqk,qhe->khe", weights.astype(BF), do, preferred_element_type=F32)
    return jnp.concatenate([t.reshape(rows, local) for t in (dq, dk, dv)], axis=1).astype(BF)


def body(sizes, image, text, grad_out, lengths, gain1, shift1, qkv, so, gain2, shift2, cq, kv, co, gain3, shift3, mi,
         in_bias, mo, out_bias):
    n = sizes["mp"]
    image, text, grad_out = image[0], text[0], grad_out[0]
    rows, width = image.shape
    size = rows // n
    local = so.shape[0]
    m = lax.axis_index("mp")
    sizes = dict(sizes, share=share_of(local, sizes["dp"]))
    qkv, kv = qkv.reshape(width, 3 * local), kv.reshape(width, 2 * local)
    own = lambda value: lax.dynamic_slice_in_dim(value, m * size, size, 0)
    row = lambda value: value[None]
    image_rows = own(image).astype(F32)
    (projected, normed1, mixed, totals, out, residual, dmixed, dtext, so_grad, cq_grad, co_grad, mi_grad, mo_grad,
     in_bias_grad, vectors) = layer(
        sizes, image, row(gain1), row(shift1), qkv, text, kv, row(lengths), row(gain2), row(shift2), row(gain3),
        row(shift3), row(in_bias), row(out_bias), so, cq, co, mi, mo, grad_out)
    in_bias_grad = in_bias_grad[:, 0]
    vectors = [vectors[t] for t in range(2, 7)]
    dprojected = attention_back(n, projected, totals, dmixed, local)
    qkv_grad = tn(normed1, dprojected)
    dn1 = lax.psum_scatter(nt(dprojected, qkv).astype(BF), "mp", scatter_dimension=0, tiled=True).astype(F32)
    normal1, inverse1 = norm_parts(image_rows)
    image_grad = residual + norm_back(dn1, normal1, inverse1, gain1)
    kv_grad = tn(text, dtext)
    text_grad = lax.psum_scatter(nt(dtext, kv).astype(BF), "mp", scatter_dimension=0, tiled=True).astype(F32)
    scatter = lambda value: lax.psum_scatter(value, "mp", scatter_dimension=0, tiled=True)[0]
    so_grad, co_grad, cq_grad = scatter(so_grad).T, scatter(co_grad).T, scatter(cq_grad)

    def own_shard(value):
        total = jnp.zeros((n,) + value.shape[1:], F32)
        for j in range(n // 2):
            total = lax.dynamic_update_index_in_dim(total, value[j].astype(F32), 2 * j + m % 2, 0)
        return lax.psum_scatter(total.astype(BF), "mp", scatter_dimension=0, tiled=True)[0]

    mi_grad, mo_grad, in_bias_grad = own_shard(mi_grad), own_shard(mo_grad), own_shard(in_bias_grad)
    total = lambda value: lax.psum(value.astype(BF), "dp").astype(F32)
    vectors = [jnp.sum(dn1 * normal1, axis=0), jnp.sum(dn1, axis=0)] + vectors
    g1, s1, g2, s2, g3, s3, ob = lax.psum(tuple(vectors), ("dp", "mp"))
    return (
        out[None], image_grad[None], text_grad[None], g1, s1, total(qkv_grad).reshape(width, 3, local), total(so_grad),
        g2, s2, total(cq_grad), total(kv_grad).reshape(width, 2, local), total(co_grad), g3, s3, total(mi_grad),
        total(in_bias_grad), total(mo_grad), ob,
    )


def solution(mesh):
    rows3, rows2, rows1 = P(None, None, "mp"), P(None, "mp"), P("mp")
    item = P("dp", None, None)
    in_specs = (item, item, item, P("dp"), P(), P(), rows3, P("mp", None), P(), P(), rows2, rows3, P("mp", None), P(), P(),
                rows2, rows1, P("mp", None), P())
    split = P("dp", "mp", None)
    out_specs = (split, split, split, P(), P(), rows3, P("mp", None), P(), P(), rows2, rows3, P("mp", None), P(), P(),
                 rows2, rows1, P("mp", None), P())
    sizes = dict(mesh.shape)
    return jax.shard_map(partial(body, sizes), mesh=mesh, in_specs=in_specs, out_specs=out_specs, check_vma=False)
```

```python
from functools import partial

import jax
import jax.numpy as jnp
from jax import lax
from jax.experimental import pallas as pl
from jax.experimental.pallas import tpu as pltpu
from jax.sharding import PartitionSpec as P

HEAD_DIM = 64
PAIR = 2 * HEAD_DIM
EPSILON = 1e-05
SCALE = HEAD_DIM ** (-0.5)
MASKED = -1e30
BF = jnp.bfloat16
F32 = jnp.float32
MESH = pl.DeviceIdType.MESH
VMEM_LIMIT = 56 << 20


def nn(a, b):
    return lax.dot_general(a, b, (((1,), (0,)), ((), ())), preferred_element_type=F32)


def nt(a, b):
    return lax.dot_general(a, b, (((1,), (1,)), ((), ())), preferred_element_type=F32)


def tn(a, b):
    return lax.dot_general(a, b, (((0,), (0,)), ((), ())), preferred_element_type=F32)


def norm_parts(value):
    center = value - jnp.mean(value, axis=-1, keepdims=True)
    inverse = lax.rsqrt(jnp.mean(center * center, axis=-1, keepdims=True) + EPSILON)
    return center * inverse, inverse


def half_masks():
    lane = lax.broadcasted_iota(jnp.int32, (1, PAIR), 1)
    first = jnp.where(lane < HEAD_DIM, 1.0, 0.0)
    return first, 1.0 - first


def stack_heads(pair, scale=None):
    first, second = half_masks()
    if scale is not None:
        first, second = first * scale, second * scale
    wide = pair.astype(F32)
    return jnp.concatenate([wide * first, wide * second], axis=0).astype(BF)


def fold_heads(stacked):
    rows = stacked.shape[1] // 2
    both = jnp.concatenate([stacked[:HEAD_DIM, :rows], stacked[HEAD_DIM:, rows:]], axis=0)
    return both.T


def causal(tile_keys, tile_rows):
    key = lax.broadcasted_iota(jnp.int32, (tile_keys, tile_rows), 0)
    row = lax.broadcasted_iota(jnp.int32, (tile_keys, tile_rows), 1)
    both = key <= row
    return jnp.concatenate([both, both], axis=1)


class Place:
    def __init__(self, sizes):
        self.n = sizes["mp"]
        self.dp = sizes["dp"]
        self.share = sizes["share"]
        self.d = lax.axis_index("dp")
        self.m = lax.axis_index("mp")
        self.core = lax.rem(self.d, 2)
        self.partner = (self.d + 1 - 2 * self.core, self.m)
        self.member = lax.rem(self.d, self.share)
        self.chip = self.member // 2
        self.base = self.d - self.member
        self.piece = self.core * (self.share // 2) + self.chip

    def along(self, offset):
        return lax.rem(self.m + offset, self.n)

    def peer(self, offset):
        return (self.d, self.along(offset))

    def chip_peer(self, offset):
        chip = lax.rem(self.chip + offset, self.share // 2)
        return (self.base + 2 * chip + self.core, self.m), self.core * (self.share // 2) + chip


def barrier(devices):
    sem = pltpu.get_barrier_semaphore()
    for device in devices:
        pl.semaphore_signal(sem, inc=1, device_id=device, device_id_type=MESH)
    pl.semaphore_wait(sem, len(devices))


class Gather:
    def __init__(self, place, own, full, offsets, slot_of, sems):
        self.place, self.own, self.full, self.offsets, self.slot_of = place, own, full, offsets, slot_of
        self.rows = own.shape[0]
        self.count = self.rows // place.share
        self.sems = sems

    def rows_of(self, slot, piece, pieces=1):
        start = pl.multiple_of(piece * self.count, self.count)
        return self.full.at[slot, pl.ds(start, pieces * self.count), :]

    def first(self, index):
        place, offset = self.place, self.offsets[index]
        start = pl.multiple_of(place.piece * self.count, self.count)
        return pltpu.make_async_remote_copy(
            src_ref=self.own.at[pl.ds(start, self.count), :],
            dst_ref=self.rows_of(self.slot_of(place.m), place.piece),
            send_sem=self.sems[0].at[index, 0],
            recv_sem=self.sems[1].at[index, 0],
            device_id=place.peer(offset),
            device_id_type=MESH,
        )

    def slot(self, index):
        place = self.place
        return self.slot_of(place.along(place.n - self.offsets[index]))

    def second(self, index, hop):
        place = self.place
        device, _ = place.chip_peer(hop)
        block = self.rows_of(self.slot(index), place.piece)
        return pltpu.make_async_remote_copy(
            src_ref=block,
            dst_ref=block,
            send_sem=self.sems[0].at[index, hop],
            recv_sem=self.sems[1].at[index, hop],
            device_id=device,
            device_id_type=MESH,
        )

    def third(self, index):
        place = self.place
        half = place.share // 2
        block = self.rows_of(self.slot(index), place.core * half, half)
        return pltpu.make_async_remote_copy(
            src_ref=block,
            dst_ref=block,
            send_sem=self.sems[0].at[index, half],
            recv_sem=self.sems[1].at[index, half],
            device_id=place.partner,
            device_id_type=MESH,
        )

    def local(self):
        return pltpu.make_async_copy(self.own, self.full.at[self.slot_of(self.place.m)], self.sems[2])

    def step(self, number):
        hops = range(1, self.place.share // 2)
        for index in range(len(self.offsets)):
            if number == 0:
                self.first(index).start()
            elif number == 1:
                self.first(index).wait_recv()
                for hop in hops:
                    self.second(index, hop).start()
            elif number == 2:
                for hop in hops:
                    self.second(index, hop).wait_recv()
                self.third(index).start()
            else:
                self.third(index).wait()
                self.first(index).wait_send()
                for hop in hops:
                    self.second(index, hop).wait_send()

    def finish(self):
        self.step(3)
        self.local().wait()


def attend_block(projected, mixed, totals, i, hp, size, local):
    rows = pl.ds(pl.multiple_of(i * size, size), size)
    column = pl.multiple_of(hp * PAIR, PAIR)
    query = stack_heads(projected[rows, pl.ds(column, PAIR)], SCALE)

    def tile(j, carry, diagonal):
        largest, total, acc = carry
        keys = pl.ds(pl.multiple_of(j * size, size), size)
        key = projected[keys, pl.ds(column + local, PAIR)]
        value = projected[keys, pl.ds(column + 2 * local, PAIR)]
        scores = nt(key, query)
        if diagonal:
            scores = jnp.where(causal(size, size), scores, MASKED)
        top = jnp.maximum(largest, jnp.max(scores, axis=0, keepdims=True))
        powers = jnp.exp(scores - top)
        shrink = jnp.exp(largest - top)
        total = total * shrink + jnp.sum(powers, axis=0, keepdims=True)
        acc = acc * shrink + tn(value, powers.astype(BF))
        return top, total, acc

    carry = (
        jnp.full((1, 2 * size), MASKED, F32),
        jnp.zeros((1, 2 * size), F32),
        jnp.zeros((PAIR, 2 * size), F32),
    )
    carry = tile(i, carry, True)
    largest, total, acc = lax.fori_loop(0, i, lambda j, c: tile(j, c, False), carry)
    mixed[rows, pl.ds(column, PAIR)] = fold_heads(acc / total).astype(BF)
    totals[hp, i] = largest + jnp.log(total)


def share_of(local, dp):
    share = dp
    while (local // share) % 16:
        share //= 2
    return share


def norm_back(grad, normal, inverse, gain):
    scaled = grad * gain
    return inverse * (
        scaled
        - jnp.mean(scaled, axis=-1, keepdims=True)
        - normal * jnp.mean(scaled * normal, axis=-1, keepdims=True)
    )


def add_rows(ref, index, value):
    ref[pl.ds(index, 1), :] += jnp.sum(value, axis=0, keepdims=True)


def in_chunks(total, chunk, step):
    def run(i, _):
        step(pl.ds(pl.multiple_of(i * chunk, chunk), chunk))
        return 0

    lax.fori_loop(0, total // chunk, run, 0)


def cross_pair(query, text_proj, length, idx, local):
    per = local // PAIR
    g, hp = idx // per, lax.rem(idx, per)
    near = pl.multiple_of(hp * PAIR, PAIR)
    column = pl.multiple_of(idx * PAIR, PAIR)
    stacked = stack_heads(query[:, pl.ds(column, PAIR)], SCALE)
    key = text_proj[g, :, pl.ds(near, PAIR)]
    value = text_proj[g, :, pl.ds(near + local, PAIR)]
    scores = nt(key, stacked)
    slot = lax.broadcasted_iota(jnp.int32, scores.shape, 0)
    return g, near, column, stacked, key, value, jnp.where(slot < length, scores, MASKED)


ROWS_AT_ONCE = 32


def layer_kernel(
    sizes,
    image, gain1, shift1, qkv, text, kv, length, gain2, shift2, gain3, shift3, in_bias, out_bias,
    so, cq, co, mi, mo, grad_out,
    projected, normed, mixed, totals, out, residual, dmixed, dtext, so_grad, cq_grad, co_grad, mi_grad, mo_grad,
    bias_grad, vectors,
    mixed_rows, text_proj, so_full, cq_full, co_full, mi_full, mo_full, bias_full,
    grad_pair, mixed_all, first, second, work, grad2, out_part,
    n2, query, cross, cross_totals, dquery, n3_pair, active, dhidden,
    dn3_send, dn3_recv, out_send, out_recv, r2, dcross, r1, dmixed_send, dtext_send, dtext_recv,
    text_own, so_keep, co_keep, small_send, small_recv, small_own, wide_send, wide_recv, wide_own,
    mix_send, mix_recv, mix_own, text_send, text_recv, bias_send, bias_recv, load_sem,
    pair_send, pair_recv, dmix_send, dmix_recv, dtext_ssem, dtext_rsem, store_sem,
):
    place = Place(sizes)
    n, share = place.n, place.share
    rows, width = image.shape
    size = rows // n
    local, hidden = so.shape[0], mi.shape[1]
    half = n // 2
    offsets = list(range(1, n))
    parity = lax.rem(place.m, 2)
    mate = (place.d, place.m + 1 - 2 * parity)
    mine = place.m // 2
    greet = [place.peer(k) for k in offsets]
    greet += [place.chip_peer(k)[0] for k in range(1, share // 2)]
    greet.append(place.partner)
    barrier(greet)

    def remote(src, dst, send, recv, device):
        return pltpu.make_async_remote_copy(
            src_ref=src, dst_ref=dst, send_sem=send, recv_sem=recv, device_id=device, device_id_type=MESH
        )

    small = [
        Gather(place, own, full, offsets, lambda s: s, (small_send.at[t], small_recv.at[t], small_own.at[t]))
        for t, (own, full) in enumerate(((so, so_full), (cq, cq_full), (co, co_full)))
    ]
    wide = [
        Gather(place, own, full, list(range(2, n, 2)), lambda s: s // 2, (wide_send.at[t], wide_recv.at[t], wide_own.at[t]))
        for t, (own, full) in enumerate(((mi, mi_full), (mo, mo_full)))
    ]
    for item in small:
        item.step(0)
    for item in small + wide:
        item.local().start()

    def block_of(index):
        return pl.ds(pl.multiple_of(index * size, size), size)

    own_rows = block_of(place.m)
    loads = [
        pltpu.make_async_copy(grad_out.at[own_rows, :], grad_pair.at[0], load_sem.at[0]),
        pltpu.make_async_copy(grad_out.at[block_of(mate[1]), :], grad_pair.at[1], load_sem.at[1]),
    ]
    for load in loads:
        load.start()
    bias_full[mine] = in_bias[...]

    def bias_copy(k):
        return remote(in_bias, bias_full.at[mine], bias_send.at[k], bias_recv.at[k], place.peer(2 * k))

    for k in range(1, half):
        bias_copy(k).start()

    def project(i, _):
        block = block_of(i)

        def norm(chunk):
            at = pl.ds(pl.multiple_of(i * size + chunk.start, ROWS_AT_ONCE), ROWS_AT_ONCE)
            normal, _ = norm_parts(image[at, :].astype(F32))
            normed[at, :] = (normal * gain1[...] + shift1[...]).astype(BF)

        in_chunks(size, ROWS_AT_ONCE, norm)
        projected[block, :] = nn(normed[block, :], qkv[...]).astype(BF)
        return 0

    lax.fori_loop(0, n, project, 0)
    text_own[...] = nn(text[...], kv[...]).astype(BF)
    text_proj[place.m] = text_own[...]

    def text_copy(k):
        return remote(text_own, text_proj.at[place.m], text_send.at[k], text_recv.at[k], place.peer(k))

    for k in offsets:
        text_copy(k).start()

    def mix_copy(i):
        gap = lax.rem(i - place.m + n, n)
        return remote(mixed.at[block_of(i), :], mixed_rows.at[place.m], mix_send.at[gap], mix_recv.at[gap], (place.d, i))

    mix_keep = pltpu.make_async_copy(mixed.at[own_rows, :], mixed_rows.at[place.m], mix_own)
    plan = [(small[0], 1), (small[1], 1), (small[0], 2), (small[2], 1), (small[1], 2), (small[2], 2)]
    plan += [(wide[0], 0), (wide[1], 0)]
    each = -(-len(plan) // n)
    for i in range(n):
        lax.fori_loop(0, local // PAIR, lambda hp, _: (attend_block(projected, mixed, totals, i, hp, size, local), 0)[1], 0)

        @pl.when(place.m != i)
        def _():
            mix_copy(i).start()

        @pl.when(place.m == i)
        def _():
            mix_keep.start()

        for item, number in plan[i * each : (i + 1) * each]:
            item.step(number)

    for k in offsets:
        mix_copy(place.along(k)).wait()
    mix_keep.wait()
    small[0].finish()
    for g in range(n):
        mixed_all[:, g * local : (g + 1) * local] = mixed_rows[g]
    first[...] = nn(mixed_all[...], so_full[...].reshape(n * local, width))

    def first_norm(chunk):
        at = pl.ds(pl.multiple_of(place.m * size + chunk.start, ROWS_AT_ONCE), ROWS_AT_ONCE)
        value = image[at, :].astype(F32) + first[chunk, :]
        first[chunk, :] = value
        n2[chunk, :] = (norm_parts(value)[0] * gain2[...] + shift2[...]).astype(BF)

    in_chunks(size, ROWS_AT_ONCE, first_norm)
    small[1].finish()
    for g in range(n):
        query[:, g * local : (g + 1) * local] = nn(n2[...], cq_full[g]).astype(BF)
    for k in offsets:
        text_copy(k).wait()
    for item in wide:
        item.step(1)
    limit = length[0, 0]
    all_pairs = n * local // PAIR

    def cross_forward(idx, _):
        g, near, column, stacked, key, value, scores = cross_pair(query, text_proj, limit, idx, local)
        largest = jnp.max(scores, axis=0, keepdims=True)
        powers = jnp.exp(scores - largest)
        total = jnp.sum(powers, axis=0, keepdims=True)
        cross_totals[idx] = largest + jnp.log(total)
        cross[:, pl.ds(column, PAIR)] = fold_heads(tn(value, (powers / total).astype(BF))).astype(BF)
        return 0

    lax.fori_loop(0, all_pairs, cross_forward, 0)
    small[2].finish()
    second[...] = nn(cross[...], co_full[...].reshape(n * local, width))

    def second_norm(chunk):
        value = first[chunk, :] + second[chunk, :]
        second[chunk, :] = value
        n3_pair[0, chunk, :] = (norm_parts(value)[0] * gain3[...] + shift3[...]).astype(BF)

    in_chunks(size, ROWS_AT_ONCE, second_norm)

    n3_copy = remote(n3_pair.at[0], n3_pair.at[1], pair_send.at[0], pair_recv.at[0], mate)
    n3_copy.start()
    for load in loads:
        load.wait()
    for k in range(1, half):
        bias_copy(k).wait()
    for item in wide:
        item.local().wait()
    step = min(256, hidden)

    def feed(p, slot):
        grads = grad_pair[p]

        def chunk(c, _):
            columns = pl.ds(pl.multiple_of(c * step, step), step)
            value = nn(n3_pair[p], mi_full[slot, :, columns]) + bias_full[slot, :, columns]
            inner = 0.5 * (1.0 + lax.erf(value * (0.5**0.5)))
            slope = inner + value * jnp.exp(-0.5 * value * value) * ((2.0 * jnp.pi) ** -0.5)
            active[slot, p, :, columns] = (value * inner).astype(BF)
            dhidden[slot, p, :, columns] = (nt(grads, mo_full[slot, columns, :]) * slope).astype(BF)
            return 0

        lax.fori_loop(0, hidden // step, chunk, 0)

    def sum_slots(term):
        total = term(0)
        for slot in range(1, half):
            total += term(slot)
        return total

    feed(0, mine)
    n3_copy.wait()
    feed(1, mine)
    for item in wide:
        item.step(2)
    for item in wide:
        item.step(3)
    others = [lax.rem(mine + k, half) for k in range(1, half)]
    for slot in others:
        feed(1, slot)
    dn3_send[...] = sum_slots(lambda slot: nt(dhidden[slot, 1], mi_full[slot])).astype(BF)
    dn3_copy = remote(dn3_send, dn3_recv, pair_send.at[1], pair_recv.at[1], mate)
    dn3_copy.start()
    out_send[...] = sum_slots(lambda slot: nn(active[slot, 1], mo_full[slot])).astype(BF)
    out_copy = remote(out_send, out_recv, pair_send.at[2], pair_recv.at[2], mate)
    out_copy.start()
    for slot in others:
        feed(0, slot)
    work[...] = sum_slots(lambda slot: nt(dhidden[slot, 0], mi_full[slot]))
    out_part[...] = sum_slots(lambda slot: nn(active[slot, 0], mo_full[slot]))
    dn3_copy.wait()

    vectors[...] = jnp.zeros_like(vectors)

    def third_back(chunk):
        grad = work[chunk, :] + dn3_recv[chunk, :].astype(F32)
        normal, inverse = norm_parts(second[chunk, :])
        above = grad_pair[0, chunk, :].astype(F32)
        add_rows(vectors, 4, grad * normal)
        add_rows(vectors, 5, grad)
        add_rows(vectors, 6, above)
        value = above + norm_back(grad, normal, inverse, gain3[...])
        work[chunk, :] = value
        r2[chunk, :] = value.astype(BF)

    in_chunks(size, ROWS_AT_ONCE, third_back)
    dcross[...] = nt(r2[...], co_full[...].reshape(n * local, width)).astype(BF)

    def cross_back(idx, _):
        g, near, column, stacked, key, value, scores = cross_pair(query, text_proj, limit, idx, local)
        weights = jnp.exp(scores - cross_totals[idx])
        above = stack_heads(dcross[:, pl.ds(column, PAIR)])
        dweights = nt(value, above)
        dscores = (weights * (dweights - jnp.sum(weights * dweights, axis=0, keepdims=True))).astype(BF)
        dquery[:, pl.ds(column, PAIR)] = (fold_heads(tn(key, dscores)) * SCALE).astype(BF)
        dtext_send[g, :, pl.ds(near, PAIR)] = nn(dscores, stacked).astype(BF)
        dtext_send[g, :, pl.ds(near + local, PAIR)] = nn(weights.astype(BF), above).astype(BF)
        return 0

    lax.fori_loop(0, all_pairs, cross_back, 0)

    def dtext_copy(k):
        return remote(dtext_send.at[place.along(k)], dtext_recv.at[place.m], dtext_ssem.at[k], dtext_rsem.at[k], place.peer(k))

    for k in offsets:
        dtext_copy(k).start()
    def both(term):
        total = term(0)
        for g in range(1, n):
            total += term(g)
        return total

    grad2[...] = both(lambda g: nt(dquery[:, g * local : (g + 1) * local], cq_full[g]))

    def second_back(chunk):
        grad = grad2[chunk, :]
        normal, inverse = norm_parts(first[chunk, :])
        add_rows(vectors, 2, grad * normal)
        add_rows(vectors, 3, grad)
        value = work[chunk, :] + norm_back(grad, normal, inverse, gain2[...])
        residual[chunk, :] = value
        r1[chunk, :] = value.astype(BF)

    in_chunks(size, ROWS_AT_ONCE, second_back)

    def dmix_copy(k):
        return remote(dmixed_send.at[k], dmixed.at[own_rows, :], dmix_send.at[k], dmix_recv.at[k], place.peer(k))

    for k in offsets:
        dmixed_send[k] = nt(r1[...], so_full[place.along(k)]).astype(BF)
        dmix_copy(k).start()
    dmixed[own_rows, :] = nt(r1[...], so_full[place.m]).astype(BF)

    tile = min(256, width)

    def wide_grads(slot):
        inner = n3_pair.shape[0] * size
        hidden_grad = dhidden[slot].reshape(inner, hidden)
        grads = grad_pair[...].reshape(inner, width)
        bias_grad[slot] = jnp.sum(hidden_grad.astype(F32), axis=0, keepdims=True)

        def into(t, _):
            at = pl.ds(pl.multiple_of(t * tile, tile), tile)
            mi_full[slot, at, :] = tn(n3_pair[:, :, at].reshape(inner, tile), hidden_grad).astype(BF)
            return 0

        lax.fori_loop(0, width // tile, into, 0)

        def back(t, _):
            at = pl.ds(pl.multiple_of(t * step, step), step)
            mo_full[slot, at, :] = tn(active[slot, :, :, at].reshape(inner, step), grads).astype(BF)
            return 0

        lax.fori_loop(0, hidden // step, back, 0)

    for slot in range(half):
        wide_grads(slot)
    stores = [
        pltpu.make_async_copy(mi_full, mi_grad, store_sem.at[0]),
        pltpu.make_async_copy(mo_full, mo_grad, store_sem.at[1]),
    ]
    for store in stores:
        store.start()

    def small_grad(left, right, keep, target, index):
        def into(t, _):
            at = pl.ds(pl.multiple_of(t * tile, tile), tile)
            turned = left[:, at]
            for g in range(n):
                keep[g, at, :] = tn(turned, right[:, g * local : (g + 1) * local]).astype(BF)
            return 0

        lax.fori_loop(0, width // tile, into, 0)
        copy = pltpu.make_async_copy(keep, target, store_sem.at[index])
        copy.start()
        stores.append(copy)

    small_grad(n2, dquery, cq_full, cq_grad, 2)
    small_grad(r1, mixed_all, so_keep, so_grad, 3)
    small_grad(r2, cross, co_keep, co_grad, 4)

    out_copy.wait()

    def finish_out(chunk):
        value = second[chunk, :] + out_part[chunk, :] + out_recv[chunk, :].astype(F32) + out_bias[...]
        out[chunk, :] = value.astype(BF)

    in_chunks(size, ROWS_AT_ONCE, finish_out)
    for k in offsets:
        dtext_copy(k).wait()
    total = dtext_send[place.m].astype(F32)
    for k in offsets:
        total += dtext_recv[place.along(k)].astype(F32)
    dtext[...] = total.astype(BF)
    for k in offsets:
        dmix_copy(k).wait()
    for store in stores:
        store.wait()


def layer(sizes, image, gain1, shift1, qkv, text, kv, length, gain2, shift2, gain3, shift3, in_bias, out_bias,
          so, cq, co, mi, mo, grad_out):
    n, share = sizes["mp"], sizes["share"]
    rows, width = image.shape
    slots = text.shape[0]
    local, hidden = so.shape[0], mi.shape[1]
    size = rows // n
    pairs = local // PAIR
    hops = share // 2 + 1
    half = n // 2
    vmem, hbm = pl.BlockSpec(memory_space=pltpu.VMEM), pl.BlockSpec(memory_space=pl.ANY)
    dma, mem = pltpu.SemaphoreType.DMA, pltpu.VMEM
    shape = jax.ShapeDtypeStruct
    few = max(half - 1, 1)
    return pl.pallas_call(
        partial(layer_kernel, sizes),
        out_shape=[
            shape((rows, 3 * local), BF), shape((rows, width), BF), shape((rows, local), BF),
            shape((pairs, n, 1, 2 * size), F32), shape((size, width), BF), shape((size, width), F32),
            shape((rows, local), BF), shape((slots, 2 * local), BF),
            shape((n, width, local), BF), shape((n, width, local), BF), shape((n, width, local), BF),
            shape((half, width, hidden), BF), shape((half, hidden, width), BF),
            shape((half, 1, hidden), F32), shape((8, width), F32),
        ],
        in_specs=[vmem] * 6 + [pl.BlockSpec(memory_space=pltpu.SMEM)] + [vmem] * 6 + [hbm] * 6,
        out_specs=[vmem] * 8 + [hbm] * 5 + [vmem] * 2,
        scratch_shapes=[
            mem((n, size, local), BF), mem((n, slots, 2 * local), BF),
            mem((n, local, width), BF), mem((n, width, local), BF), mem((n, local, width), BF),
            mem((half, width, hidden), BF), mem((half, hidden, width), BF), mem((half, 1, hidden), F32),
            mem((2, size, width), BF), mem((size, n * local), BF),
            mem((size, width), F32), mem((size, width), F32), mem((size, width), F32), mem((size, width), F32),
            mem((size, width), F32),
            mem((size, width), BF), mem((size, n * local), BF), mem((size, n * local), BF),
            mem((n * pairs, 1, 2 * size), F32), mem((size, n * local), BF),
            mem((2, size, width), BF), mem((half, 2, size, hidden), BF), mem((half, 2, size, hidden), BF),
            mem((size, width), BF), mem((size, width), BF), mem((size, width), BF), mem((size, width), BF),
            mem((size, width), BF), mem((size, n * local), BF), mem((size, width), BF),
            mem((n, size, local), BF), mem((n, slots, 2 * local), BF), mem((n, slots, 2 * local), BF),
            mem((slots, 2 * local), BF), mem((n, width, local), BF), mem((n, width, local), BF),
            dma((3, n - 1, hops)), dma((3, n - 1, hops)), dma((3,)),
            dma((2, few, hops)), dma((2, few, hops)), dma((2,)),
            dma((n,)), dma((n,)), dma(()),
            dma((n,)), dma((n,)), dma((half,)), dma((half,)), dma((2,)),
            dma((3,)), dma((3,)), dma((n,)), dma((n,)), dma((n,)), dma((n,)), dma((5,)),
        ],
        compiler_params=pltpu.CompilerParams(collective_id=1, has_side_effects=True, vmem_limit_bytes=VMEM_LIMIT),
        cost_estimate=pl.CostEstimate(flops=22 << 30, bytes_accessed=48 << 20, transcendentals=8 << 20),
    )(image, gain1, shift1, qkv, text, kv, length, gain2, shift2, gain3, shift3, in_bias, out_bias,
      so, cq, co, mi, mo, grad_out)


class Reduce:
    def __init__(self, place, ref, recv, pieces, other, final, whole, rule, sems):
        self.place, self.ref, self.recv, self.pieces, self.other, self.final, self.whole = (
            place, ref, recv, pieces, other, final, whole)
        self.slots, self.rows, self.columns = ref.shape
        self.half = self.rows // 2
        self.part = self.half // 2
        self.bits = (place.dp // 2).bit_length() - 1
        self.count = self.part >> self.bits
        self.rule, (self.send, self.recv_sem, self.keep) = rule, sems
        self.chip = place.d // 2
        if rule == "all":
            self.hops = [(k, place.along(k)) for k in range(1, place.n)]
            self.slot = place.m
        elif rule == "parity":
            half = place.n // 2
            self.hops = [(2 * k, lax.rem(place.m // 2 + k, half)) for k in range(1, half)]
            self.slot = place.m // 2
        else:
            self.hops, self.slot = [], 0

    def bit(self, p, k):
        b = k if p == 0 else self.bits - 1 - k
        value = lax.rem(self.chip // (1 << b), 2)
        chip = self.chip + (1 - 2 * value) * (1 << b)
        return value, (2 * chip + self.place.core, self.place.m)

    def region(self, p, k):
        start = self.place.core * self.half + p * self.part
        for t in range(k):
            start = start + self.bit(p, t)[0] * (self.part >> (t + 1))
        return start

    def span(self, start, count):
        return pl.ds(pl.multiple_of(start, self.count), count)

    def copy(self, src, dst, index, device):
        return pltpu.make_async_remote_copy(
            src_ref=src, dst_ref=dst, send_sem=self.send.at[index], recv_sem=self.recv_sem.at[index],
            device_id=device, device_id_type=MESH,
        )

    def core_copy(self):
        away = self.span((1 - self.place.core) * self.half, self.half)
        return self.copy(self.ref.at[:, away, :], self.recv.at[:, pl.ds(0, self.half), :], 0, self.place.partner)

    def offset(self, p, k):
        return self.half + p * (self.part - self.count) + sum(self.part >> (t + 1) for t in range(k))

    def chip_copy(self, p, k):
        value, device = self.bit(p, k)
        count = self.part >> (k + 1)
        away = self.span(self.region(p, k) + (1 - value) * count, count)
        return self.copy(
            self.ref.at[:, away, :], self.recv.at[:, pl.ds(self.offset(p, k), count), :], 1 + p * self.bits + k, device)

    def far_copy(self, index):
        hop, slot = self.hops[index]
        return self.copy(self.pieces.at[slot], self.other.at[self.slot], 1 + 4 * self.bits + index, self.place.peer(hop))

    def spread_copy(self, p, k):
        _, device = self.bit(p, k)
        count = self.part >> (k + 1)
        rows = self.span(self.region(p, k + 1), count)
        block = self.whole.at[rows, :]
        src = self.final.at[pl.ds(p * self.count, self.count), :] if k == self.bits - 1 else block
        return self.copy(src, block, 1 + 2 * self.bits + p * self.bits + k, device)

    def keep_copy(self, p):
        rows = self.span(self.region(p, self.bits), self.count)
        return pltpu.make_async_copy(self.final.at[pl.ds(p * self.count, self.count), :], self.whole.at[rows, :], self.keep.at[p])

    def core_spread(self):
        block = self.whole.at[self.span(self.place.core * self.half, self.half), :]
        return self.copy(block, block, 1 + 4 * self.bits + self.place.n, self.place.partner)

    def add(self, start, offset, count, target, target_start):
        chunk = min(32, count)

        def run(t, _):
            at = t * chunk
            for s in range(self.slots):
                mine = self.ref[s, self.span_of(start + at, chunk), :].astype(F32)
                theirs = self.recv[s, self.span_of(offset + at, chunk), :].astype(F32)
                target[s, self.span_of(target_start + at, chunk), :] = (mine + theirs).astype(BF)
            return 0

        lax.fori_loop(0, count // chunk, run, 0)

    def span_of(self, start, chunk):
        return pl.ds(pl.multiple_of(start, 16), chunk)

    def phases(self):
        bits = self.bits

        def begin():
            self.core_copy().start()

        def core_sum():
            self.core_copy().wait()
            self.add(self.place.core * self.half, 0, self.half, self.ref, self.place.core * self.half)
            for p in range(2):
                self.chip_copy(p, 0).start()

        def chip_sum(k):
            for p in range(2):
                self.chip_copy(p, k).wait()
                last = k == bits - 1
                start = self.region(p, k + 1)
                self.add(start, self.offset(p, k), self.part >> (k + 1), self.pieces if last else self.ref,
                         p * self.count if last else start)
                if not last:
                    self.chip_copy(p, k + 1).start()
            if k == bits - 1:
                for index in range(len(self.hops)):
                    self.far_copy(index).start()

        def far_sum():
            total = self.pieces[self.slot].astype(F32)
            for index, (hop, _) in enumerate(self.hops):
                self.far_copy(index).wait()
                source = self.place.along(self.place.n - hop)
                total += self.other[source if self.rule == "all" else source // 2].astype(F32)
            self.final[...] = total.astype(BF)
            for p in range(2):
                self.keep_copy(p).start()
                self.spread_copy(p, bits - 1).start()
            for p in range(2):
                self.keep_copy(p).wait()

        def spread(k):
            for p in range(2):
                self.spread_copy(p, k).wait()
                if k > 0:
                    self.spread_copy(p, k - 1).start()
            if k == 0:
                self.core_spread().start()

        def end():
            self.core_spread().wait()

        steps = [begin, core_sum] + [partial(chip_sum, k) for k in range(bits)] + [far_sum]
        return steps + [partial(spread, k) for k in reversed(range(bits))] + [end]


def back_kernel(
    sizes,
    gain1, qkv, kv, text, residual, projected, normed, mixed, totals, dmixed, dtext, early,
    image, mi_grad, mo_grad, so_grad, cq_grad, co_grad,
    image_grad, text_grad, early_out, late_out, mi_out, mo_out, small_out, joint_out,
    image_rows, stacked, above, delta, dquery, dprojected, dn1_send, dn1_recv, dn1_own,
    mi_ref, mi_recv, mi_pieces, mi_other, mi_final, mo_ref, mo_recv, mo_pieces, mo_other, mo_final,
    small_ref, small_recv, small_pieces, small_other, small_final, joint_ref, joint_recv, joint_pieces, joint_final,
    early_dp, early_mp, early_own, late, late_dp, late_mp, late_own, text_send, text_recv,
    reduce_send, reduce_recv, reduce_keep, load_sem, dn1_ssem, dn1_rsem, text_ssem, text_rsem,
    vec_ssem, vec_rsem, vec_zsend, vec_zrecv,
):
    place = Place(sizes)
    n, dp = place.n, place.dp
    rows, width = normed.shape
    local = mixed.shape[1]
    size = rows // n
    pairs = local // PAIR
    offsets = list(range(1, n))
    everyone = [lax.rem(place.d + k, dp) for k in range(1, dp)]
    barrier([place.peer(k) for k in offsets] + [(device, place.m) for device in everyone])

    def remote(src, dst, send, recv, device):
        return pltpu.make_async_remote_copy(
            src_ref=src, dst_ref=dst, send_sem=send, recv_sem=recv, device_id=device, device_id_type=MESH
        )

    def block_of(index):
        return pl.ds(pl.multiple_of(index * size, size), size)

    loads = [
        pltpu.make_async_copy(src, dst, load_sem.at[t])
        for t, (src, dst) in enumerate((
            (mi_grad, mi_ref), (mo_grad, mo_ref), (so_grad, small_ref.at[:, :, 0:local]),
            (cq_grad, small_ref.at[:, :, local : 2 * local]), (co_grad, small_ref.at[:, :, 2 * local : 3 * local]),
            (image.at[block_of(place.m), :], image_rows),
        ))
    ]
    for load in loads:
        load.start()

    def unit(t, ref, recv, pieces, other, final, whole, rule):
        sems = (reduce_send.at[t], reduce_recv.at[t], reduce_keep.at[t])
        return Reduce(place, ref, recv, pieces, other, final, whole, rule, sems).phases()

    mi_steps = unit(0, mi_ref, mi_recv, mi_pieces, mi_other, mi_final, mi_out, "parity")
    mo_steps = unit(1, mo_ref, mo_recv, mo_pieces, mo_other, mo_final, mo_out, "parity")
    small_steps = unit(2, small_ref, small_recv, small_pieces, small_other, small_final, small_out, "all")
    joint_steps = unit(3, joint_ref, joint_recv, joint_pieces, None, joint_final, joint_out, "own")

    class Vectors:
        def __init__(self, value, over_dp, own, over_mp, base):
            self.value, self.over_dp, self.own, self.over_mp, self.base = value, over_dp, own, over_mp, base

        def first(self, k):
            return remote(self.value, self.over_dp.at[place.d], vec_ssem.at[self.base, k], vec_rsem.at[self.base, k],
                          (everyone[k - 1], place.m))

        def second(self, k):
            return remote(self.own, self.over_mp.at[place.m], vec_zsend.at[self.base, k], vec_zrecv.at[self.base, k],
                          place.peer(k))

        def begin(self):
            self.over_dp[place.d] = self.value[...]
            for k in range(1, dp):
                self.first(k).start()

        def turn(self):
            for k in range(1, dp):
                self.first(k).wait()
            total = self.over_dp[0]
            for j in range(1, dp):
                total += self.over_dp[j]
            self.own[...] = total
            self.over_mp[place.m] = total
            for k in offsets:
                self.second(k).start()

        def end(self):
            for k in offsets:
                self.second(k).wait()

        def total(self):
            value = self.over_mp[0]
            for j in range(1, n):
                value += self.over_mp[j]
            return value

    early_sum = Vectors(early, early_dp, early_own, early_mp, 0)
    late_sum = Vectors(late, late_dp, late_own, late_mp, 1)
    early_sum.begin()

    part = text_grad.shape[0]
    spread_text = nt(dtext[...], kv[...]).astype(BF)
    for g in range(n):
        text_send[g] = spread_text[g * part : (g + 1) * part, :]

    def text_copy(k):
        return remote(text_send.at[place.along(k)], text_recv.at[place.m], text_ssem.at[k], text_rsem.at[k], place.peer(k))

    for k in offsets:
        text_copy(k).start()
    joint_ref[0, :, 3 * local :] = tn(text[...], dtext[...]).astype(BF)

    loads[0].wait()
    mi_steps[0]()
    loads[1].wait()
    mo_steps[0]()
    for load in loads[2:5]:
        load.wait()
    small_steps[0]()

    def prepare(i, _):
        block = block_of(i)
        for hp in range(pairs):
            columns = slice(hp * PAIR, (hp + 1) * PAIR)
            stacked[hp, i] = stack_heads(projected[block, columns], SCALE)
            above[hp, i] = stack_heads(dmixed[block, columns])
            product = (dmixed[block, columns].astype(F32) * mixed[block, columns].astype(F32)).T
            delta[hp, i] = jnp.concatenate(
                [jnp.sum(product[:HEAD_DIM], axis=0, keepdims=True), jnp.sum(product[HEAD_DIM:], axis=0, keepdims=True)],
                axis=1,
            )
            dquery[hp, i] = jnp.zeros_like(dquery[hp, i])
        return 0

    lax.fori_loop(0, n, prepare, 0)
    plan = [mi_steps[1], mo_steps[1], small_steps[1], mi_steps[2], mo_steps[2], early_sum.turn, small_steps[2], mi_steps[3]]
    each = -(-len(plan) // (n * pairs))

    def dn1_copy(j):
        gap = lax.rem(j - place.m + n, n)
        return remote(dn1_send.at[j], dn1_recv.at[place.m], dn1_ssem.at[gap], dn1_rsem.at[gap], (place.d, j))

    point = 0
    for j in range(n):
        keys = slice(j * size, (j + 1) * size)
        for hp in range(pairs):
            columns = slice(hp * PAIR, (hp + 1) * PAIR)
            key = projected[keys, local + hp * PAIR : local + (hp + 1) * PAIR]
            value = projected[keys, 2 * local + hp * PAIR : 2 * local + (hp + 1) * PAIR]

            def tile(i, carry, diagonal):
                dkey, dvalue = carry
                query, over = stacked[hp, i], above[hp, i]
                scores = nt(key, query)
                if diagonal:
                    scores = jnp.where(causal(size, size), scores, MASKED)
                weights = jnp.exp(scores - totals[hp, i])
                dscores = (weights * (nt(value, over) - delta[hp, i])).astype(BF)
                dvalue = dvalue + nn(weights.astype(BF), over)
                dkey = dkey + nn(dscores, query)
                turned = tn(key, dscores)
                dquery[hp, i] += jnp.concatenate([turned[:HEAD_DIM, :size], turned[HEAD_DIM:, size:]], axis=0)
                return dkey, dvalue

            carry = (jnp.zeros((size, PAIR), F32), jnp.zeros((size, PAIR), F32))
            carry = tile(j, carry, True)
            dkey, dvalue = lax.fori_loop(j + 1, n, lambda i, c: tile(i, c, False), carry)
            dprojected[keys, columns] = (dquery[hp, j].T * SCALE).astype(BF)
            dprojected[keys, local + hp * PAIR : local + (hp + 1) * PAIR] = dkey.astype(BF)
            dprojected[keys, 2 * local + hp * PAIR : 2 * local + (hp + 1) * PAIR] = dvalue.astype(BF)
            for phase in plan[point * each : (point + 1) * each]:
                phase()
            point += 1
        partial_sum = nt(dprojected[keys, :], qkv[...])

        @pl.when(place.m == j)
        def _():
            dn1_own[...] = partial_sum

        @pl.when(place.m != j)
        def _():
            dn1_send[j] = partial_sum.astype(BF)
            dn1_copy(j).start()

    tile_rows = min(256, width)

    def qkv_grad(t, _):
        at = pl.ds(pl.multiple_of(t * tile_rows, tile_rows), tile_rows)
        joint_ref[0, at, 0 : 3 * local] = tn(normed[:, at], dprojected[...]).astype(BF)
        return 0

    lax.fori_loop(0, width // tile_rows, qkv_grad, 0)
    done = 3 + (len(mi_steps) - 8)
    joint_steps[0]()
    mo_steps[3]()
    small_steps[3]()
    joint_steps[1]()
    for k in range(4, len(mi_steps) - 1):
        mi_steps[k]()
        mo_steps[k]()
        small_steps[k]()
        joint_steps[k - 2]()

    for k in offsets:
        dn1_copy(place.along(k)).wait()
        dn1_own[...] += dn1_recv[place.along(n - k)].astype(F32)
    loads[5].wait()
    late[...] = jnp.zeros_like(late)

    def last_back(chunk):
        grad = dn1_own[chunk, :]
        normal, inverse = norm_parts(image_rows[chunk, :].astype(F32))
        add_rows(late, 0, grad * normal)
        add_rows(late, 1, grad)
        image_grad[chunk, :] = residual[chunk, :] + norm_back(grad, normal, inverse, gain1[...])

    in_chunks(size, ROWS_AT_ONCE, last_back)
    late_sum.begin()
    for k in range(len(mi_steps) - 3, len(mi_steps) - 1):
        joint_steps[k]()
    for k in offsets:
        text_copy(k).wait()
    total = text_send[place.m].astype(F32)
    for k in offsets:
        total += text_recv[place.along(k)].astype(F32)
    text_grad[...] = total
    late_sum.turn()
    early_sum.end()
    early_out[...] = early_sum.total()
    shared = early_out[pl.ds(8 + place.m // 2, 1), :] * 0.0
    for j in range(n):
        take = jnp.where(lax.rem(place.m + j, 2) == 0, 1.0, 0.0)
        shared += early_mp[j, pl.ds(8 + place.m // 2, 1), :] * take
    early_out[7:8, :] = shared
    late_sum.end()
    late_out[...] = late_sum.total()
    for steps in (mi_steps, mo_steps, small_steps, joint_steps):
        steps[-1]()


def back(sizes, gain1, qkv, kv, text, residual, projected, normed, mixed, totals, dmixed, dtext, early,
         image, mi_grad, mo_grad, so_grad, cq_grad, co_grad):
    n, dp = sizes["mp"], sizes["dp"]
    rows, width = normed.shape
    slots = text.shape[0]
    local, hidden = mixed.shape[1], mi_grad.shape[2]
    size, pairs, half = rows // n, local // PAIR, n // 2
    bits = (dp // 2).bit_length() - 1
    vmem, hbm = pl.BlockSpec(memory_space=pltpu.VMEM), pl.BlockSpec(memory_space=pl.ANY)
    dma, mem = pltpu.SemaphoreType.DMA, pltpu.VMEM
    shape = jax.ShapeDtypeStruct

    def unit(count, height, columns, rule):
        piece = 2 * (height // 4 >> bits)
        scratch = [mem((count, height, columns), BF), mem((count, height - piece, columns), BF), mem((count, piece, columns), BF)]
        if rule != "own":
            scratch.append(mem((count, piece, columns), BF))
        return scratch + [mem((piece, columns), BF)]

    few = early.shape[0]
    each = 2 + 4 * bits + n
    return pl.pallas_call(
        partial(back_kernel, sizes),
        out_shape=[
            shape((size, width), F32), shape((slots // n, width), F32), shape((few, width), F32), shape((2, width), F32),
            shape((width, hidden), BF), shape((hidden, width), BF), shape((width, 3 * local), BF), shape((width, 5 * local), BF),
        ],
        in_specs=[vmem] * 12 + [hbm] * 6,
        out_specs=[vmem] * 4 + [hbm] * 4,
        scratch_shapes=[
            mem((size, width), BF), mem((pairs, n, 2 * size, PAIR), BF), mem((pairs, n, 2 * size, PAIR), BF),
            mem((pairs, n, 1, 2 * size), F32), mem((pairs, n, PAIR, size), F32), mem((rows, 3 * local), BF),
            mem((n, size, width), BF), mem((n, size, width), BF), mem((size, width), F32),
            *unit(half, width, hidden, "parity"), *unit(half, hidden, width, "parity"),
            *unit(n, width, 3 * local, "all"), *unit(1, width, 5 * local, "own"),
            mem((dp, few, width), F32), mem((n, few, width), F32), mem((few, width), F32),
            mem((2, width), F32), mem((dp, 2, width), F32), mem((n, 2, width), F32), mem((2, width), F32),
            mem((n, slots // n, width), BF), mem((n, slots // n, width), BF),
            dma((4, each)), dma((4, each)), dma((4, 2)), dma((6,)), dma((n,)), dma((n,)), dma((n,)), dma((n,)),
            dma((2, dp)), dma((2, dp)), dma((2, n)), dma((2, n)),
        ],
        compiler_params=pltpu.CompilerParams(collective_id=2, has_side_effects=True, vmem_limit_bytes=60 << 20),
        cost_estimate=pl.CostEstimate(flops=8 << 30, bytes_accessed=48 << 20, transcendentals=4 << 20),
    )(gain1, qkv, kv, text, residual, projected, normed, mixed, totals, dmixed, dtext, early,
      image, mi_grad, mo_grad, so_grad, cq_grad, co_grad)


def body(sizes, image, text, grad_out, lengths, gain1, shift1, qkv, so, gain2, shift2, cq, kv, co, gain3, shift3, mi,
         in_bias, mo, out_bias):
    n = sizes["mp"]
    image, text, grad_out = image[0], text[0], grad_out[0]
    rows, width = image.shape
    local = so.shape[0]
    sizes = dict(sizes, share=share_of(local, sizes["dp"]))
    qkv, kv = qkv.reshape(width, 3 * local), kv.reshape(width, 2 * local)
    row = lambda value: value[None]
    (projected, normed1, mixed, totals, out, residual, dmixed, dtext, so_grad, cq_grad, co_grad, mi_grad, mo_grad,
     in_bias_grad, vectors) = layer(
        sizes, image, row(gain1), row(shift1), qkv, text, kv, row(lengths), row(gain2), row(shift2), row(gain3),
        row(shift3), row(in_bias), row(out_bias), so, cq, co, mi, mo, grad_out)
    early = jnp.zeros((8 + -(-n // 2 // 8) * 8, width), F32)
    early = lax.dynamic_update_slice(early, vectors, (0, 0))
    early = lax.dynamic_update_slice(early, in_bias_grad[:, 0], (8, 0))
    image_grad, text_grad, early, late, mi_sum, mo_sum, small_sum, joint_sum = back(
        sizes, row(gain1), qkv, kv, text, residual, projected, normed1, mixed, totals, dmixed, dtext, early,
        image, mi_grad, mo_grad, so_grad, cq_grad, co_grad)
    hidden = mi.shape[1]
    small = lambda t: small_sum[:, t * local : (t + 1) * local].astype(F32)
    return (
        out[None], image_grad[None], text_grad[None], late[0], late[1],
        joint_sum[:, : 3 * local].astype(F32).reshape(width, 3, local), small(0).T, early[2], early[3], small(1),
        joint_sum[:, 3 * local :].astype(F32).reshape(width, 2, local), small(2).T, early[4], early[5],
        mi_sum.astype(F32), early[7, :hidden], mo_sum.astype(F32), early[6],
    )


def solution(mesh):
    rows3, rows2, rows1 = P(None, None, "mp"), P(None, "mp"), P("mp")
    item = P("dp", None, None)
    in_specs = (item, item, item, P("dp"), P(), P(), rows3, P("mp", None), P(), P(), rows2, rows3, P("mp", None), P(), P(),
                rows2, rows1, P("mp", None), P())
    split = P("dp", "mp", None)
    out_specs = (split, split, split, P(), P(), rows3, P("mp", None), P(), P(), rows2, rows3, P("mp", None), P(), P(),
                 rows2, rows1, P("mp", None), P())
    sizes = dict(mesh.shape)
    return jax.shard_map(partial(body, sizes), mesh=mesh, in_specs=in_specs, out_specs=out_specs, check_vma=False)
```

```python
from functools import partial

import jax
import jax.numpy as jnp
from jax import lax
from jax.experimental import pallas as pl
from jax.experimental.pallas import tpu as pltpu
from jax.sharding import PartitionSpec as P

HEAD_DIM = 64
PAIR = 2 * HEAD_DIM
EPSILON = 1e-05
SCALE = HEAD_DIM ** (-0.5)
MASKED = -1e30
BF = jnp.bfloat16
F32 = jnp.float32
MESH = pl.DeviceIdType.MESH
VMEM_LIMIT = 60 << 20


def nn(a, b):
    return lax.dot_general(a, b, (((1,), (0,)), ((), ())), preferred_element_type=F32)


def nt(a, b):
    return lax.dot_general(a, b, (((1,), (1,)), ((), ())), preferred_element_type=F32)


def tn(a, b):
    return lax.dot_general(a, b, (((0,), (0,)), ((), ())), preferred_element_type=F32)


def norm_parts(value):
    center = value - jnp.mean(value, axis=-1, keepdims=True)
    inverse = lax.rsqrt(jnp.mean(center * center, axis=-1, keepdims=True) + EPSILON)
    return center * inverse, inverse


def half_masks():
    lane = lax.broadcasted_iota(jnp.int32, (1, PAIR), 1)
    first = jnp.where(lane < HEAD_DIM, 1.0, 0.0)
    return first, 1.0 - first


def stack_heads(pair, scale=None):
    first, second = half_masks()
    if scale is not None:
        first, second = first * scale, second * scale
    wide = pair.astype(F32)
    return jnp.concatenate([wide * first, wide * second], axis=0).astype(BF)


def fold_heads(stacked):
    rows = stacked.shape[1] // 2
    both = jnp.concatenate([stacked[:HEAD_DIM, :rows], stacked[HEAD_DIM:, rows:]], axis=0)
    return both.T


def causal(tile_keys, tile_rows):
    key = lax.broadcasted_iota(jnp.int32, (tile_keys, tile_rows), 0)
    row = lax.broadcasted_iota(jnp.int32, (tile_keys, tile_rows), 1)
    both = key <= row
    return jnp.concatenate([both, both], axis=1)


class Place:
    def __init__(self, sizes):
        self.n = sizes["mp"]
        self.dp = sizes["dp"]
        self.share = sizes["share"]
        self.d = lax.axis_index("dp")
        self.m = lax.axis_index("mp")
        self.core = lax.rem(self.d, 2)
        self.mate = self.m + 1 - 2 * lax.rem(self.m, 2)
        self.partner = (self.d + 1 - 2 * self.core, self.m)
        self.member = lax.rem(self.d, self.share)
        self.chip = self.member // 2
        self.base = self.d - self.member
        self.piece = self.core * (self.share // 2) + self.chip

    def along(self, offset):
        return lax.rem(self.m + offset, self.n)

    def mate_along(self, offset):
        return lax.rem(self.mate + offset, self.n)

    def peer(self, offset):
        return (self.d, self.along(offset))

    def chip_peer(self, offset):
        chip = lax.rem(self.chip + offset, self.share // 2)
        return (self.base + 2 * chip + self.core, self.m), self.core * (self.share // 2) + chip


def barrier(devices):
    sem = pltpu.get_barrier_semaphore()
    for device in devices:
        pl.semaphore_signal(sem, inc=1, device_id=device, device_id_type=MESH)
    pl.semaphore_wait(sem, len(devices))


class Gather:
    def __init__(self, place, own, full, everyone, slot_of, sems):
        self.place, self.own, self.full, self.slot_of = place, own, full, slot_of
        self.count = own.shape[0] // place.share
        self.sems = sems
        self.even = list(range(2, place.n, 2))
        self.sources = [place.along(place.n - k) for k in self.even]
        if everyone:
            self.sources.append(place.mate)
            self.sources += [place.mate_along(place.n - k) for k in self.even]
        self.everyone = everyone

    def rows_of(self, slot, piece, pieces=1):
        start = pl.multiple_of(piece * self.count, self.count)
        return self.full.at[slot, pl.ds(start, pieces * self.count), :]

    def copy(self, src, dst, index, hop, device):
        return pltpu.make_async_remote_copy(
            src_ref=src, dst_ref=dst, send_sem=self.sems[0].at[index, hop], recv_sem=self.sems[1].at[index, hop],
            device_id=device, device_id_type=MESH,
        )

    def first(self, index):
        place, parity = self.place, len(self.even)
        mine = self.own.at[pl.ds(pl.multiple_of(place.piece * self.count, self.count), self.count), :]
        slot = self.slot_of(place.m)
        if index < parity:
            device = place.peer(self.even[index])
        else:
            device = (place.d, place.mate)
        if index > parity:
            slot = self.slot_of(self.sources[index - parity - 1])
            mine = self.rows_of(slot, place.piece)
        return self.copy(mine, self.rows_of(slot, place.piece), index, 0, device)

    def second(self, index, hop):
        block = self.rows_of(self.slot_of(self.sources[index]), self.place.piece)
        return self.copy(block, block, index, hop, self.place.chip_peer(hop)[0])

    def third(self, index):
        half = self.place.share // 2
        block = self.rows_of(self.slot_of(self.sources[index]), self.place.core * half, half)
        return self.copy(block, block, index, half, self.place.partner)

    def local(self):
        return pltpu.make_async_copy(self.own, self.full.at[self.slot_of(self.place.m)], self.sems[2])

    def step(self, number):
        hops = range(1, self.place.share // 2)
        parity = len(self.even)
        everything = range(len(self.sources))
        if number == 0:
            for index in everything:
                if index <= parity:
                    self.first(index).start()
        elif number == 1:
            for index in range(parity):
                self.first(index).wait_recv()
                if self.everyone:
                    self.first(parity + 1 + index).start()
                for hop in hops:
                    self.second(index, hop).start()
        elif number == 2:
            for index in everything[parity:]:
                self.first(index).wait_recv()
                for hop in hops:
                    self.second(index, hop).start()
        elif number == 3:
            for index in everything:
                for hop in hops:
                    self.second(index, hop).wait_recv()
                self.third(index).start()
        else:
            for index in everything:
                self.third(index).wait()
                self.first(index).wait_send()
                for hop in hops:
                    self.second(index, hop).wait_send()

    def finish(self):
        self.step(4)
        self.local().wait()


def attend_block(projected, mixed, totals, i, hp, size, local):
    rows = pl.ds(pl.multiple_of(i * size, size), size)
    column = pl.multiple_of(hp * PAIR, PAIR)
    query = stack_heads(projected[rows, pl.ds(column, PAIR)], SCALE)

    def tile(j, carry, diagonal):
        largest, total, acc = carry
        keys = pl.ds(pl.multiple_of(j * size, size), size)
        key = projected[keys, pl.ds(column + local, PAIR)]
        value = projected[keys, pl.ds(column + 2 * local, PAIR)]
        scores = nt(key, query)
        if diagonal:
            scores = jnp.where(causal(size, size), scores, MASKED)
        top = jnp.maximum(largest, jnp.max(scores, axis=0, keepdims=True))
        powers = jnp.exp(scores - top)
        shrink = jnp.exp(largest - top)
        total = total * shrink + jnp.sum(powers, axis=0, keepdims=True)
        acc = acc * shrink + tn(value, powers.astype(BF))
        return top, total, acc

    carry = (
        jnp.full((1, 2 * size), MASKED, F32),
        jnp.zeros((1, 2 * size), F32),
        jnp.zeros((PAIR, 2 * size), F32),
    )
    carry = tile(i, carry, True)
    largest, total, acc = lax.fori_loop(0, i, lambda j, c: tile(j, c, False), carry)
    mixed[rows, pl.ds(column, PAIR)] = fold_heads(acc / total).astype(BF)
    totals[hp, i] = largest + jnp.log(total)


def share_of(local, dp):
    share = dp
    while (local // share) % 16:
        share //= 2
    return share


def halvings(rows, bits):
    left = [rows // 4]
    for _ in range(bits):
        left.append(left[-1] // 2 if left[-1] % 32 == 0 else left[-1])
    return left


def arrivals(rows, bits):
    left = halvings(rows, bits)
    return left[1:]


class Rows:
    def __init__(self, place, rows):
        self.place = place
        self.half = rows // 2
        self.bits = (place.dp // 2).bit_length() - 1
        self.left = halvings(rows, self.bits)
        self.count = self.left[-1]
        self.chip = place.d // 2

    def bit(self, p, k):
        b = k if p == 0 else self.bits - 1 - k
        value = lax.rem(self.chip // (1 << b), 2)
        chip = self.chip + (1 - 2 * value) * (1 << b)
        return value, (2 * chip + self.place.core, self.place.m)

    def cut(self, k):
        return self.left[k + 1] < self.left[k]

    def region(self, p, k):
        start = self.place.core * self.half + p * self.left[0]
        for t in range(k):
            if self.cut(t):
                start = start + self.bit(p, t)[0] * self.left[t + 1]
        return start

    def span(self, start, count):
        return pl.ds(pl.multiple_of(start, 16), count)


class Reduce:
    def __init__(self, place, ref, recv, pieces, sems):
        self.place, self.ref, self.recv, self.pieces = place, ref, recv, pieces
        self.rows = Rows(place, ref.shape[1])
        self.send, self.recv_sem = sems

    def copy(self, src, dst, index, device):
        return pltpu.make_async_remote_copy(
            src_ref=src, dst_ref=dst, send_sem=self.send.at[index], recv_sem=self.recv_sem.at[index],
            device_id=device, device_id_type=MESH,
        )

    def core_copy(self):
        half = self.rows.half
        away = self.rows.span((1 - self.place.core) * half, half)
        return self.copy(self.ref.at[:, away, :], self.recv.at[:, pl.ds(0, half), :], 0, self.place.partner)

    def offset(self, p, k):
        into = self.rows.left[1:]
        return self.rows.half + p * sum(into) + sum(into[:k])

    def chip_copy(self, p, k):
        rows = self.rows
        value, device = rows.bit(p, k)
        count = rows.left[k + 1]
        start = rows.region(p, k)
        if rows.cut(k):
            start = start + (1 - value) * count
        return self.copy(
            self.ref.at[:, rows.span(start, count), :], self.recv.at[:, pl.ds(self.offset(p, k), count), :],
            1 + p * rows.bits + k, device)

    def add(self, start, offset, count, target, target_start):
        chunk = min(32, count)
        span = self.rows.span

        def run(t, _):
            at = t * chunk
            for s in range(self.ref.shape[0]):
                mine = self.ref[s, span(start + at, chunk), :].astype(F32)
                theirs = self.recv[s, span(offset + at, chunk), :].astype(F32)
                target[s, span(target_start + at, chunk), :] = (mine + theirs).astype(BF)
            return 0

        lax.fori_loop(0, count // chunk, run, 0)

    def phases(self):
        rows = self.rows

        def begin():
            self.core_copy().start()

        def core_sum():
            self.core_copy().wait()
            self.add(self.place.core * rows.half, 0, rows.half, self.ref, self.place.core * rows.half)
            for p in range(2):
                self.chip_copy(p, 0).start()

        def chip_sum(k):
            last = k == rows.bits - 1
            for p in range(2):
                self.chip_copy(p, k).wait()
                start = rows.region(p, k + 1)
                self.add(start, self.offset(p, k), rows.left[k + 1], self.pieces if last else self.ref,
                         p * rows.count if last else start)
                if not last:
                    self.chip_copy(p, k + 1).start()

        return [begin, core_sum] + [partial(chip_sum, k) for k in range(rows.bits)]


class Spread:
    def __init__(self, place, rows, pieces, other, final, whole, rule, sems):
        self.place, self.pieces, self.other, self.final, self.whole = place, pieces, other, final, whole
        self.rows = Rows(place, rows)
        self.rule, (self.send, self.recv_sem, self.keep) = rule, sems
        if rule == "all":
            self.hops = [(k, place.along(k)) for k in range(1, place.n)]
            self.slot = place.m
        elif rule == "parity":
            half = place.n // 2
            self.hops = [(2 * k, lax.rem(place.m // 2 + k, half)) for k in range(1, half)]
            self.slot = place.m // 2
        else:
            self.hops, self.slot = [], 0

    def copy(self, src, dst, index, device):
        return pltpu.make_async_remote_copy(
            src_ref=src, dst_ref=dst, send_sem=self.send.at[index], recv_sem=self.recv_sem.at[index],
            device_id=device, device_id_type=MESH,
        )

    def far_copy(self, index):
        hop, slot = self.hops[index]
        return self.copy(self.pieces.at[slot], self.other.at[self.slot], 1 + 2 * self.rows.bits + index, self.place.peer(hop))

    def spread_copy(self, p, k):
        rows = self.rows
        count = rows.left[k + 1]
        block = self.whole.at[rows.span(rows.region(p, k + 1), count), :]
        first = not any(rows.cut(t) for t in range(k + 1, rows.bits))
        src = self.final.at[pl.ds(p * rows.count, rows.count), :] if first else block
        return self.copy(src, block, 1 + p * rows.bits + k, rows.bit(p, k)[1])

    def keep_copy(self, p):
        rows = self.rows
        block = self.whole.at[rows.span(rows.region(p, rows.bits), rows.count), :]
        return pltpu.make_async_copy(self.final.at[pl.ds(p * rows.count, rows.count), :], block, self.keep.at[p])

    def core_spread(self):
        half = self.rows.half
        block = self.whole.at[self.rows.span(self.place.core * half, half), :]
        return self.copy(block, block, 0, self.place.partner)

    def phases(self):
        rows = self.rows
        cuts = [k for k in reversed(range(rows.bits)) if rows.cut(k)]

        def far():
            for index in range(len(self.hops)):
                self.far_copy(index).start()

        def far_sum():
            total = self.pieces[self.slot].astype(F32)
            for index, (hop, _) in enumerate(self.hops):
                self.far_copy(index).wait()
                source = self.place.along(self.place.n - hop)
                total += self.other[source if self.rule == "all" else source // 2].astype(F32)
            self.final[...] = total.astype(BF)
            for p in range(2):
                self.keep_copy(p).start()
                self.spread_copy(p, cuts[0]).start()
            for p in range(2):
                self.keep_copy(p).wait()

        def spread(t):
            for p in range(2):
                self.spread_copy(p, cuts[t]).wait()
                if t + 1 < len(cuts):
                    self.spread_copy(p, cuts[t + 1]).start()
            if t + 1 == len(cuts):
                self.core_spread().start()

        def end():
            self.core_spread().wait()

        nothing = [lambda: None] * (rows.bits - len(cuts))
        return [far, far_sum] + [partial(spread, t) for t in range(len(cuts))] + nothing + [end]


def recv_space(count, rows, columns, bits):
    return pltpu.VMEM((count, rows // 2 + 2 * sum(arrivals(rows, bits)), columns), BF)


def piece_shape(count, rows, columns, bits):
    return jax.ShapeDtypeStruct((count, 2 * halvings(rows, bits)[-1], columns), BF)


def norm_back(grad, normal, inverse, gain):
    scaled = grad * gain
    return inverse * (
        scaled
        - jnp.mean(scaled, axis=-1, keepdims=True)
        - normal * jnp.mean(scaled * normal, axis=-1, keepdims=True)
    )


def add_rows(ref, index, value):
    ref[pl.ds(index, 1), :] += jnp.sum(value, axis=0, keepdims=True)


def in_chunks(total, chunk, step):
    def run(i, _):
        step(pl.ds(pl.multiple_of(i * chunk, chunk), chunk))
        return 0

    lax.fori_loop(0, total // chunk, run, 0)


def cross_pair(query, text_proj, length, idx, local):
    per = local // PAIR
    g, hp = idx // per, lax.rem(idx, per)
    near = pl.multiple_of(hp * PAIR, PAIR)
    column = pl.multiple_of(idx * PAIR, PAIR)
    stacked = stack_heads(query[:, pl.ds(column, PAIR)], SCALE)
    key = text_proj[g, :, pl.ds(near, PAIR)]
    value = text_proj[g, :, pl.ds(near + local, PAIR)]
    scores = nt(key, stacked)
    slot = lax.broadcasted_iota(jnp.int32, scores.shape, 0)
    return g, near, column, stacked, key, value, jnp.where(slot < length, scores, MASKED)


ROWS_AT_ONCE = 32


def layer_kernel(
    sizes,
    image, gain1, shift1, qkv, text, kv, length, gain2, shift2, gain3, shift3, in_bias, out_bias,
    so, cq, co, mi, mo, grad_out,
    projected, normed, mixed, totals, out, residual, dmixed, dtext, so_grad, cq_grad, co_grad, mi_pieces, mo_pieces,
    bias_grad, vectors,
    mixed_rows, text_proj, so_full, cq_full, co_full, mi_full, mo_full, bias_full,
    grad_pair, mixed_all, first, second, work, grad2, out_part,
    n2, query, cross, cross_totals, dquery, n3_pair, active, dhidden,
    dn3_send, dn3_recv, out_send, out_recv, r2, dcross, r1, dmixed_send, dtext_send, dtext_recv,
    text_own, mi_recv, mo_recv, small_send, small_recv, small_own, wide_send, wide_recv, wide_own,
    mix_send, mix_recv, mix_own, text_send, text_recv, bias_send, bias_recv, load_sem,
    pair_send, pair_recv, dmix_send, dmix_recv, dtext_ssem, dtext_rsem, store_sem, reduce_send, reduce_recv,
):
    place = Place(sizes)
    n, share = place.n, place.share
    rows, width = image.shape
    size = rows // n
    local, hidden = so.shape[0], mi.shape[1]
    half = n // 2
    offsets = list(range(1, n))
    mate = (place.d, place.mate)
    mine = place.m // 2
    chips = place.dp // 2
    greet = [place.peer(k) for k in offsets] + [place.partner]
    greet += [(2 * lax.rem(place.d // 2 + k, chips) + place.core, place.m) for k in range(1, chips)]
    barrier(greet)

    def remote(src, dst, send, recv, device):
        return pltpu.make_async_remote_copy(
            src_ref=src, dst_ref=dst, send_sem=send, recv_sem=recv, device_id=device, device_id_type=MESH
        )

    small = [
        Gather(place, own, full, True, lambda s: s, (small_send.at[t], small_recv.at[t], small_own.at[t]))
        for t, (own, full) in enumerate(((so, so_full), (cq, cq_full), (co, co_full)))
    ]
    wide = [
        Gather(place, own, full, False, lambda s: s // 2, (wide_send.at[t], wide_recv.at[t], wide_own.at[t]))
        for t, (own, full) in enumerate(((mi, mi_full), (mo, mo_full)))
    ]
    for item in small:
        item.step(0)
    for item in small + wide:
        item.local().start()

    def block_of(index):
        return pl.ds(pl.multiple_of(index * size, size), size)

    own_rows = block_of(place.m)
    loads = [
        pltpu.make_async_copy(grad_out.at[own_rows, :], grad_pair.at[0], load_sem.at[0]),
        pltpu.make_async_copy(grad_out.at[block_of(mate[1]), :], grad_pair.at[1], load_sem.at[1]),
    ]
    for load in loads:
        load.start()
    bias_full[mine] = in_bias[...]

    def bias_copy(k):
        return remote(in_bias, bias_full.at[mine], bias_send.at[k], bias_recv.at[k], place.peer(2 * k))

    for k in range(1, half):
        bias_copy(k).start()

    def project(i, _):
        block = block_of(i)

        def norm(chunk):
            at = pl.ds(pl.multiple_of(i * size + chunk.start, ROWS_AT_ONCE), ROWS_AT_ONCE)
            normal, _ = norm_parts(image[at, :].astype(F32))
            normed[at, :] = (normal * gain1[...] + shift1[...]).astype(BF)

        in_chunks(size, ROWS_AT_ONCE, norm)
        projected[block, :] = nn(normed[block, :], qkv[...]).astype(BF)
        return 0

    lax.fori_loop(0, n, project, 0)
    text_own[...] = nn(text[...], kv[...]).astype(BF)
    text_proj[place.m] = text_own[...]

    even = list(range(2, n, 2))

    def text_copy(k):
        return remote(text_own, text_proj.at[place.m], text_send.at[k], text_recv.at[k], place.peer(k) if k else mate)

    def text_pass(k):
        block = text_proj.at[place.along(n - k)]
        return remote(block, block, text_send.at[k + 1], text_recv.at[k + 1], mate)

    for k in [0] + even:
        text_copy(k).start()

    def mix_copy(i):
        gap = lax.rem(i - place.m + n, n)
        return remote(mixed.at[block_of(i), :], mixed_rows.at[place.m], mix_send.at[gap], mix_recv.at[gap], (place.d, i))

    mix_keep = pltpu.make_async_copy(mixed.at[own_rows, :], mixed_rows.at[place.m], mix_own)
    for item in small:
        item.step(1)
    plan = [[] for _ in range(n)]
    plan[1] = [small[0]]
    plan[2] = [small[1]]
    plan[n - 1] += [small[2]]
    for i in range(n):
        lax.fori_loop(0, local // PAIR, lambda hp, _: (attend_block(projected, mixed, totals, i, hp, size, local), 0)[1], 0)

        @pl.when(place.m != i)
        def _():
            mix_copy(i).start()

        @pl.when(place.m == i)
        def _():
            mix_keep.start()

        for item in plan[i]:
            item.step(2)

    for item in wide:
        item.step(0)
    for k in even:
        text_copy(k).wait_recv()
        text_pass(k).start()
    small[0].step(3)

    for k in offsets:
        mix_copy(place.along(k)).wait()
    mix_keep.wait()
    small[0].finish()
    small[1].step(3)
    for g in range(n):
        mixed_all[:, g * local : (g + 1) * local] = mixed_rows[g]
    first[...] = nn(mixed_all[...], so_full[...].reshape(n * local, width))

    def first_norm(chunk):
        at = pl.ds(pl.multiple_of(place.m * size + chunk.start, ROWS_AT_ONCE), ROWS_AT_ONCE)
        value = image[at, :].astype(F32) + first[chunk, :]
        first[chunk, :] = value
        n2[chunk, :] = (norm_parts(value)[0] * gain2[...] + shift2[...]).astype(BF)

    in_chunks(size, ROWS_AT_ONCE, first_norm)
    small[1].finish()
    small[2].step(3)
    for g in range(n):
        query[:, g * local : (g + 1) * local] = nn(n2[...], cq_full[g]).astype(BF)
    text_copy(0).wait()
    for k in even:
        text_copy(k).wait_send()
        text_pass(k).wait()
    for item in wide:
        item.step(1)
    limit = length[0, 0]
    all_pairs = n * local // PAIR

    def cross_forward(idx, _):
        g, near, column, stacked, key, value, scores = cross_pair(query, text_proj, limit, idx, local)
        largest = jnp.max(scores, axis=0, keepdims=True)
        powers = jnp.exp(scores - largest)
        total = jnp.sum(powers, axis=0, keepdims=True)
        cross_totals[idx] = largest + jnp.log(total)
        cross[:, pl.ds(column, PAIR)] = fold_heads(tn(value, (powers / total).astype(BF))).astype(BF)
        return 0

    lax.fori_loop(0, all_pairs, cross_forward, 0)
    small[2].finish()
    second[...] = nn(cross[...], co_full[...].reshape(n * local, width))

    def second_norm(chunk):
        value = first[chunk, :] + second[chunk, :]
        second[chunk, :] = value
        n3_pair[0, chunk, :] = (norm_parts(value)[0] * gain3[...] + shift3[...]).astype(BF)

    in_chunks(size, ROWS_AT_ONCE, second_norm)

    n3_copy = remote(n3_pair.at[0], n3_pair.at[1], pair_send.at[0], pair_recv.at[0], mate)
    n3_copy.start()
    for load in loads:
        load.wait()
    for k in range(1, half):
        bias_copy(k).wait()
    for item in wide:
        item.local().wait()
    step = min(256, hidden)

    def feed(p, slot):
        grads = grad_pair[p]

        def chunk(c, _):
            columns = pl.ds(pl.multiple_of(c * step, step), step)
            value = nn(n3_pair[p], mi_full[slot, :, columns]) + bias_full[slot, :, columns]
            inner = 0.5 * (1.0 + lax.erf(value * (0.5**0.5)))
            slope = inner + value * jnp.exp(-0.5 * value * value) * ((2.0 * jnp.pi) ** -0.5)
            active[slot, p, :, columns] = (value * inner).astype(BF)
            dhidden[slot, p, :, columns] = (nt(grads, mo_full[slot, columns, :]) * slope).astype(BF)
            return 0

        lax.fori_loop(0, hidden // step, chunk, 0)

    def sum_slots(term):
        total = term(0)
        for slot in range(1, half):
            total += term(slot)
        return total

    feed(0, mine)
    n3_copy.wait()
    feed(1, mine)
    for item in wide:
        item.step(3)
    for item in wide:
        item.step(4)
    others = [lax.rem(mine + k, half) for k in range(1, half)]
    for slot in others:
        feed(1, slot)
    dn3_send[...] = sum_slots(lambda slot: nt(dhidden[slot, 1], mi_full[slot])).astype(BF)
    dn3_copy = remote(dn3_send, dn3_recv, pair_send.at[1], pair_recv.at[1], mate)
    dn3_copy.start()
    out_send[...] = sum_slots(lambda slot: nn(active[slot, 1], mo_full[slot])).astype(BF)
    out_copy = remote(out_send, out_recv, pair_send.at[2], pair_recv.at[2], mate)
    out_copy.start()
    for slot in others:
        feed(0, slot)
    work[...] = sum_slots(lambda slot: nt(dhidden[slot, 0], mi_full[slot]))
    out_part[...] = sum_slots(lambda slot: nn(active[slot, 0], mo_full[slot]))
    tile = min(256, width)

    def wide_grads(slot):
        inner = n3_pair.shape[0] * size
        hidden_grad = dhidden[slot].reshape(inner, hidden)
        grads = grad_pair[...].reshape(inner, width)
        bias_grad[slot] = jnp.sum(hidden_grad.astype(F32), axis=0, keepdims=True)

        def into(t, _):
            at = pl.ds(pl.multiple_of(t * tile, tile), tile)
            mi_full[slot, at, :] = tn(n3_pair[:, :, at].reshape(inner, tile), hidden_grad).astype(BF)
            return 0

        lax.fori_loop(0, width // tile, into, 0)

        def back(t, _):
            at = pl.ds(pl.multiple_of(t * step, step), step)
            mo_full[slot, at, :] = tn(active[slot, :, :, at].reshape(inner, step), grads).astype(BF)
            return 0

        lax.fori_loop(0, hidden // step, back, 0)

    for slot in range(half):
        wide_grads(slot)
    mi_steps = Reduce(place, mi_full, mi_recv, mi_pieces, (reduce_send.at[0], reduce_recv.at[0])).phases()
    mo_steps = Reduce(place, mo_full, mo_recv, mo_pieces, (reduce_send.at[1], reduce_recv.at[1])).phases()
    wide_steps = [step for pair in zip(mi_steps, mo_steps) for step in pair]
    for run in wide_steps[:2]:
        run()
    dn3_copy.wait()

    vectors[...] = jnp.zeros_like(vectors)

    def third_back(chunk):
        grad = work[chunk, :] + dn3_recv[chunk, :].astype(F32)
        normal, inverse = norm_parts(second[chunk, :])
        above = grad_pair[0, chunk, :].astype(F32)
        add_rows(vectors, 4, grad * normal)
        add_rows(vectors, 5, grad)
        add_rows(vectors, 6, above)
        value = above + norm_back(grad, normal, inverse, gain3[...])
        work[chunk, :] = value
        r2[chunk, :] = value.astype(BF)

    in_chunks(size, ROWS_AT_ONCE, third_back)
    wide_steps[2]()
    dcross[...] = nt(r2[...], co_full[...].reshape(n * local, width)).astype(BF)

    def cross_back(idx, _):
        g, near, column, stacked, key, value, scores = cross_pair(query, text_proj, limit, idx, local)
        weights = jnp.exp(scores - cross_totals[idx])
        above = stack_heads(dcross[:, pl.ds(column, PAIR)])
        dweights = nt(value, above)
        dscores = (weights * (dweights - jnp.sum(weights * dweights, axis=0, keepdims=True))).astype(BF)
        dquery[:, pl.ds(column, PAIR)] = (fold_heads(tn(key, dscores)) * SCALE).astype(BF)
        dtext_send[g, :, pl.ds(near, PAIR)] = nn(dscores, stacked).astype(BF)
        dtext_send[g, :, pl.ds(near + local, PAIR)] = nn(weights.astype(BF), above).astype(BF)
        return 0

    lax.fori_loop(0, all_pairs, cross_back, 0)
    wide_steps[3]()

    def dtext_copy(k):
        return remote(dtext_send.at[place.along(k)], dtext_recv.at[place.m], dtext_ssem.at[k], dtext_rsem.at[k], place.peer(k))

    for k in offsets:
        dtext_copy(k).start()
    def both(term):
        total = term(0)
        for g in range(1, n):
            total += term(g)
        return total

    grad2[...] = both(lambda g: nt(dquery[:, g * local : (g + 1) * local], cq_full[g]))

    def second_back(chunk):
        grad = grad2[chunk, :]
        normal, inverse = norm_parts(first[chunk, :])
        add_rows(vectors, 2, grad * normal)
        add_rows(vectors, 3, grad)
        value = work[chunk, :] + norm_back(grad, normal, inverse, gain2[...])
        residual[chunk, :] = value
        r1[chunk, :] = value.astype(BF)

    in_chunks(size, ROWS_AT_ONCE, second_back)

    def dmix_copy(k):
        return remote(dmixed_send.at[k], dmixed.at[own_rows, :], dmix_send.at[k], dmix_recv.at[k], place.peer(k))

    for k in offsets:
        dmixed_send[k] = nt(r1[...], so_full[place.along(k)]).astype(BF)
        dmix_copy(k).start()
    dmixed[own_rows, :] = nt(r1[...], so_full[place.m]).astype(BF)
    wide_steps[4]()

    stores = []

    def small_grad(left, right, keep, target, index):
        for g in range(n):
            heads = slice(g * local, (g + 1) * local)
            if keep.shape[1] == local:
                keep[g] = tn(left[:, heads], right[...]).astype(BF)
            else:
                keep[g] = tn(left[...], right[:, heads]).astype(BF)
        copy = pltpu.make_async_copy(keep, target, store_sem.at[index])
        copy.start()
        stores.append(copy)

    small_grad(n2, dquery, cq_full, cq_grad, 0)
    small_grad(mixed_all, r1, so_full, so_grad, 1)
    small_grad(cross, r2, co_full, co_grad, 2)

    wide_steps[5]()
    out_copy.wait()

    def finish_out(chunk):
        value = second[chunk, :] + out_part[chunk, :] + out_recv[chunk, :].astype(F32) + out_bias[...]
        out[chunk, :] = value.astype(BF)

    in_chunks(size, ROWS_AT_ONCE, finish_out)
    for run in wide_steps[6:]:
        run()
    for k in offsets:
        dtext_copy(k).wait()
    total = dtext_send[place.m].astype(F32)
    for k in offsets:
        total += dtext_recv[place.along(k)].astype(F32)
    dtext[...] = total.astype(BF)
    for k in offsets:
        dmix_copy(k).wait()
    for store in stores:
        store.wait()


def layer(sizes, image, gain1, shift1, qkv, text, kv, length, gain2, shift2, gain3, shift3, in_bias, out_bias,
          so, cq, co, mi, mo, grad_out):
    n, share = sizes["mp"], sizes["share"]
    rows, width = image.shape
    slots = text.shape[0]
    local, hidden = so.shape[0], mi.shape[1]
    size = rows // n
    pairs = local // PAIR
    hops = share // 2 + 1
    half = n // 2
    vmem, hbm = pl.BlockSpec(memory_space=pltpu.VMEM), pl.BlockSpec(memory_space=pl.ANY)
    dma, mem = pltpu.SemaphoreType.DMA, pltpu.VMEM
    shape = jax.ShapeDtypeStruct
    few = max(half - 1, 1)
    bits = (sizes["dp"] // 2).bit_length() - 1
    return pl.pallas_call(
        partial(layer_kernel, sizes),
        out_shape=[
            shape((rows, 3 * local), BF), shape((rows, width), BF), shape((rows, local), BF),
            shape((pairs, n, 1, 2 * size), F32), shape((size, width), BF), shape((size, width), F32),
            shape((rows, local), BF), shape((slots, 2 * local), BF),
            shape((n, local, width), BF), shape((n, width, local), BF), shape((n, local, width), BF),
            piece_shape(half, width, hidden, bits), piece_shape(half, hidden, width, bits),
            shape((half, 1, hidden), F32), shape((8, width), F32),
        ],
        in_specs=[vmem] * 6 + [pl.BlockSpec(memory_space=pltpu.SMEM)] + [vmem] * 6 + [hbm] * 6,
        out_specs=[vmem] * 8 + [hbm] * 3 + [vmem] * 4,
        scratch_shapes=[
            mem((n, size, local), BF), mem((n, slots, 2 * local), BF),
            mem((n, local, width), BF), mem((n, width, local), BF), mem((n, local, width), BF),
            mem((half, width, hidden), BF), mem((half, hidden, width), BF), mem((half, 1, hidden), F32),
            mem((2, size, width), BF), mem((size, n * local), BF),
            mem((size, width), F32), mem((size, width), F32), mem((size, width), F32), mem((size, width), F32),
            mem((size, width), F32),
            mem((size, width), BF), mem((size, n * local), BF), mem((size, n * local), BF),
            mem((n * pairs, 1, 2 * size), F32), mem((size, n * local), BF),
            mem((2, size, width), BF), mem((half, 2, size, hidden), BF), mem((half, 2, size, hidden), BF),
            mem((size, width), BF), mem((size, width), BF), mem((size, width), BF), mem((size, width), BF),
            mem((size, width), BF), mem((size, n * local), BF), mem((size, width), BF),
            mem((n, size, local), BF), mem((n, slots, 2 * local), BF), mem((n, slots, 2 * local), BF),
            mem((slots, 2 * local), BF), recv_space(half, width, hidden, bits), recv_space(half, hidden, width, bits),
            dma((3, n - 1, hops)), dma((3, n - 1, hops)), dma((3,)),
            dma((2, few, hops)), dma((2, few, hops)), dma((2,)),
            dma((n,)), dma((n,)), dma(()),
            dma((n + 1,)), dma((n + 1,)), dma((half,)), dma((half,)), dma((2,)),
            dma((3,)), dma((3,)), dma((n,)), dma((n,)), dma((n,)), dma((n,)), dma((3,)), dma((2, 1 + 2 * bits)), dma((2, 1 + 2 * bits)),
        ],
        compiler_params=pltpu.CompilerParams(collective_id=1, has_side_effects=True, vmem_limit_bytes=VMEM_LIMIT),
        cost_estimate=pl.CostEstimate(flops=22 << 30, bytes_accessed=48 << 20, transcendentals=8 << 20),
    )(image, gain1, shift1, qkv, text, kv, length, gain2, shift2, gain3, shift3, in_bias, out_bias,
      so, cq, co, mi, mo, grad_out)


def back_kernel(
    sizes,
    gain1, qkv, kv, text, residual, projected, normed, mixed, totals, dmixed, dtext, early, mi_pieces, mo_pieces,
    image, so_grad, cq_grad, co_grad,
    image_grad, text_grad, early_out, late_out, mi_out, mo_out, so_out, cq_out, co_out, joint_out,
    image_rows, stacked, above, delta, dquery, dprojected,
    near_hold, near_send, near_recv, far_send, far_recv, dn1_own,
    mi_other, mi_final, mo_other, mo_final,
    so_ref, so_recv, so_pieces, so_other, so_final, cq_ref, cq_recv, cq_pieces, cq_other, cq_final,
    co_ref, co_recv, co_pieces, co_other, co_final, joint_ref, joint_recv, joint_pieces, joint_final,
    early_dp, early_mp, early_own, late, late_dp, late_mp, late_own, text_send, text_recv,
    reduce_send, reduce_recv, spread_send, spread_recv, spread_keep, load_sem,
    near_ssem, near_rsem, far_ssem, far_rsem, text_ssem, text_rsem, vec_ssem, vec_rsem, vec_zsend, vec_zrecv,
):
    place = Place(sizes)
    n, dp = place.n, place.dp
    rows, width = normed.shape
    local = mixed.shape[1]
    size = rows // n
    half = n // 2
    pairs = local // PAIR
    offsets = list(range(1, n))
    everyone = [lax.rem(place.d + k, dp) for k in range(1, dp)]
    barrier([place.peer(k) for k in offsets] + [(device, place.m) for device in everyone])

    def remote(src, dst, send, recv, device):
        return pltpu.make_async_remote_copy(
            src_ref=src, dst_ref=dst, send_sem=send, recv_sem=recv, device_id=device, device_id_type=MESH
        )

    def block_of(index):
        return pl.ds(pl.multiple_of(index * size, size), size)

    loads = [
        pltpu.make_async_copy(src, dst, load_sem.at[t])
        for t, (src, dst) in enumerate((
            (so_grad, so_ref), (cq_grad, cq_ref), (co_grad, co_ref), (image.at[block_of(place.m), :], image_rows),
        ))
    ]
    for load in loads:
        load.start()

    def reduce(t, ref, recv, pieces):
        return Reduce(place, ref, recv, pieces, (reduce_send.at[t], reduce_recv.at[t])).phases()

    def spread(t, rows, pieces, other, final, whole, rule):
        sems = (spread_send.at[t], spread_recv.at[t], spread_keep.at[t])
        return Spread(place, rows, pieces, other, final, whole, rule, sems).phases()

    mi_steps = spread(0, width, mi_pieces, mi_other, mi_final, mi_out, "parity")
    mo_steps = spread(1, mo_out.shape[0], mo_pieces, mo_other, mo_final, mo_out, "parity")
    so_steps = reduce(0, so_ref, so_recv, so_pieces) + spread(2, local, so_pieces, so_other, so_final, so_out, "all")
    cq_steps = reduce(1, cq_ref, cq_recv, cq_pieces) + spread(3, width, cq_pieces, cq_other, cq_final, cq_out, "all")
    co_steps = reduce(2, co_ref, co_recv, co_pieces) + spread(4, local, co_pieces, co_other, co_final, co_out, "all")
    joint_steps = reduce(3, joint_ref, joint_recv, joint_pieces)
    joint_steps += spread(5, width, joint_pieces, None, joint_final, joint_out, "own")
    mi_steps[0]()
    mo_steps[0]()

    class Vectors:
        def __init__(self, value, over_dp, own, over_mp, base):
            self.value, self.over_dp, self.own, self.over_mp, self.base = value, over_dp, own, over_mp, base

        def first(self, k):
            return remote(self.value, self.over_dp.at[place.d], vec_ssem.at[self.base, k], vec_rsem.at[self.base, k],
                          (everyone[k - 1], place.m))

        def second(self, k):
            return remote(self.own, self.over_mp.at[place.m], vec_zsend.at[self.base, k], vec_zrecv.at[self.base, k],
                          place.peer(k))

        def begin(self):
            self.over_dp[place.d] = self.value[...]
            for k in range(1, dp):
                self.first(k).start()

        def turn(self):
            for k in range(1, dp):
                self.first(k).wait()
            total = self.over_dp[0]
            for j in range(1, dp):
                total += self.over_dp[j]
            self.own[...] = total
            self.over_mp[place.m] = total
            for k in offsets:
                self.second(k).start()

        def end(self):
            for k in offsets:
                self.second(k).wait()

        def total(self):
            value = self.over_mp[0]
            for j in range(1, n):
                value += self.over_mp[j]
            return value

    early_sum = Vectors(early, early_dp, early_own, early_mp, 0)
    late_sum = Vectors(late, late_dp, late_own, late_mp, 1)
    early_sum.begin()

    part = text_grad.shape[0]
    spread_text = nt(dtext[...], kv[...]).astype(BF)
    for g in range(n):
        text_send[g] = spread_text[g * part : (g + 1) * part, :]

    def text_copy(k):
        return remote(text_send.at[place.along(k)], text_recv.at[place.m], text_ssem.at[k], text_rsem.at[k], place.peer(k))

    for k in offsets:
        text_copy(k).start()
    joint_ref[0, :, 3 * local :] = tn(text[...], dtext[...]).astype(BF)

    for load, steps in zip(loads, (so_steps, cq_steps, co_steps)):
        load.wait()
        steps[0]()

    def prepare(i, _):
        block = block_of(i)
        for hp in range(pairs):
            columns = slice(hp * PAIR, (hp + 1) * PAIR)
            stacked[hp, i] = stack_heads(projected[block, columns], SCALE)
            above[hp, i] = stack_heads(dmixed[block, columns])
            product = (dmixed[block, columns].astype(F32) * mixed[block, columns].astype(F32)).T
            delta[hp, i] = jnp.concatenate(
                [jnp.sum(product[:HEAD_DIM], axis=0, keepdims=True), jnp.sum(product[HEAD_DIM:], axis=0, keepdims=True)],
                axis=1,
            )
            dquery[hp, i] = jnp.zeros_like(dquery[hp, i])
        return 0

    lax.fori_loop(0, n, prepare, 0)
    plan = [[so_steps[1]], [cq_steps[1]], [co_steps[1]], [mi_steps[1]], [so_steps[2]], [mo_steps[1]], [cq_steps[2]], [co_steps[2]]]
    each = -(-len(plan) // (n * pairs))
    parity = lax.rem(place.m, 2)
    mine = place.m // 2

    def near_copy(t):
        return remote(near_send.at[t], near_recv.at[t], near_ssem.at[t], near_rsem.at[t], (place.d, place.mate))

    def far_copy(t):
        gap = lax.rem(t - mine + half, half)
        return remote(far_send.at[t], far_recv.at[mine], far_ssem.at[gap], far_rsem.at[gap], (place.d, 2 * t + parity))

    def pass_on(t):
        near_copy(t).wait()
        total = near_hold[t] + near_recv[t].astype(F32)

        @pl.when(mine == t)
        def _():
            dn1_own[...] = total

        @pl.when(mine != t)
        def _():
            far_send[t] = total.astype(BF)
            far_copy(t).start()

    point = 0
    for j in range(n):
        keys = slice(j * size, (j + 1) * size)
        for hp in range(pairs):
            columns = slice(hp * PAIR, (hp + 1) * PAIR)
            key = projected[keys, local + hp * PAIR : local + (hp + 1) * PAIR]
            value = projected[keys, 2 * local + hp * PAIR : 2 * local + (hp + 1) * PAIR]

            def tile(i, carry, diagonal):
                dkey, dvalue = carry
                query, over = stacked[hp, i], above[hp, i]
                scores = nt(key, query)
                if diagonal:
                    scores = jnp.where(causal(size, size), scores, MASKED)
                weights = jnp.exp(scores - totals[hp, i])
                dscores = (weights * (nt(value, over) - delta[hp, i])).astype(BF)
                dvalue = dvalue + nn(weights.astype(BF), over)
                dkey = dkey + nn(dscores, query)
                turned = tn(key, dscores)
                dquery[hp, i] += jnp.concatenate([turned[:HEAD_DIM, :size], turned[HEAD_DIM:, size:]], axis=0)
                return dkey, dvalue

            carry = (jnp.zeros((size, PAIR), F32), jnp.zeros((size, PAIR), F32))
            carry = tile(j, carry, True)
            dkey, dvalue = lax.fori_loop(j + 1, n, lambda i, c: tile(i, c, False), carry)
            dprojected[keys, columns] = (dquery[hp, j].T * SCALE).astype(BF)
            dprojected[keys, local + hp * PAIR : local + (hp + 1) * PAIR] = dkey.astype(BF)
            dprojected[keys, 2 * local + hp * PAIR : 2 * local + (hp + 1) * PAIR] = dvalue.astype(BF)
            for phases in plan[point * each : (point + 1) * each]:
                for phase in phases:
                    phase()
            point += 1
        partial_sum = nt(dprojected[keys, :], qkv[...])

        @pl.when(parity == j % 2)
        def _():
            near_hold[j // 2] = partial_sum

        @pl.when(parity != j % 2)
        def _():
            near_send[j // 2] = partial_sum.astype(BF)
            near_copy(j // 2).start()

        if j % 2 and j > 1:
            pass_on(j // 2 - 1)

    tile_rows = min(256, width)

    def qkv_grad(t, _):
        at = pl.ds(pl.multiple_of(t * tile_rows, tile_rows), tile_rows)
        joint_ref[0, at, 0 : 3 * local] = tn(normed[:, at], dprojected[...]).astype(BF)
        return 0

    lax.fori_loop(0, width // tile_rows, qkv_grad, 0)
    bits = (dp // 2).bit_length() - 1
    joint_steps[0]()
    early_sum.turn()
    pass_on(half - 1)
    mi_steps[2]()
    small_steps = (so_steps, cq_steps, co_steps)
    for k in range(1, bits):
        for steps in small_steps:
            steps[2 + k]()
    for steps in small_steps:
        steps[2 + bits]()
    joint_steps[1]()
    mo_steps[2]()
    for k in range(1, bits):
        mi_steps[2 + k]()
        mo_steps[2 + k]()
    for k in range(bits):
        joint_steps[2 + k]()
        if k == 0:
            for steps in small_steps:
                steps[3 + bits]()
    joint_steps[2 + bits]()
    joint_steps[3 + bits]()
    for k in range(bits - 1):
        for steps in small_steps:
            steps[4 + bits + k]()

    for k in range(1, half):
        far_copy(lax.rem(mine + k, half)).wait()
        dn1_own[...] += far_recv[lax.rem(mine + half - k, half)].astype(F32)
    loads[3].wait()
    late[...] = jnp.zeros_like(late)

    def last_back(chunk):
        grad = dn1_own[chunk, :]
        normal, inverse = norm_parts(image_rows[chunk, :].astype(F32))
        add_rows(late, 0, grad * normal)
        add_rows(late, 1, grad)
        image_grad[chunk, :] = residual[chunk, :] + norm_back(grad, normal, inverse, gain1[...])

    in_chunks(size, ROWS_AT_ONCE, last_back)
    late_sum.begin()
    for steps in small_steps:
        steps[3 + 2 * bits]()
    joint_steps[4 + bits]()
    for k in offsets:
        text_copy(k).wait()
    total = text_send[place.m].astype(F32)
    for k in offsets:
        total += text_recv[place.along(k)].astype(F32)
    text_grad[...] = total
    late_sum.turn()
    early_sum.end()
    early_out[...] = early_sum.total()
    shared = early_out[pl.ds(8 + place.m // 2, 1), :] * 0.0
    for j in range(n):
        take = jnp.where(lax.rem(place.m + j, 2) == 0, 1.0, 0.0)
        shared += early_mp[j, pl.ds(8 + place.m // 2, 1), :] * take
    early_out[7:8, :] = shared
    for k in range(1, bits):
        joint_steps[4 + bits + k]()
    late_sum.end()
    late_out[...] = late_sum.total()
    for steps in (mi_steps, mo_steps, *small_steps, joint_steps):
        steps[-1]()


def back(sizes, gain1, qkv, kv, text, residual, projected, normed, mixed, totals, dmixed, dtext, early, mi_pieces, mo_pieces,
         image, so_grad, cq_grad, co_grad, hidden):
    n, dp = sizes["mp"], sizes["dp"]
    rows, width = normed.shape
    slots = text.shape[0]
    local = mixed.shape[1]
    size, pairs, half = rows // n, local // PAIR, n // 2
    bits = (dp // 2).bit_length() - 1
    vmem, hbm = pl.BlockSpec(memory_space=pltpu.VMEM), pl.BlockSpec(memory_space=pl.ANY)
    dma, mem = pltpu.SemaphoreType.DMA, pltpu.VMEM
    shape = jax.ShapeDtypeStruct

    def unit(count, height, columns, rule):
        pieces = piece_shape(count, height, columns, bits).shape
        scratch = []
        if rule != "parity":
            scratch += [mem((count, height, columns), BF), recv_space(count, height, columns, bits), mem(pieces, BF)]
        if rule != "own":
            scratch.append(mem(pieces, BF))
        return scratch + [mem(pieces[1:], BF)]

    few = early.shape[0]
    whole = [(width, hidden), (hidden, width), (local, width), (width, local), (local, width), (width, 5 * local)]
    block = mem((half, size, width), BF)
    return pl.pallas_call(
        partial(back_kernel, sizes),
        out_shape=[
            shape((size, width), F32), shape((slots // n, width), F32), shape((few, width), F32), shape((2, width), F32),
        ] + [shape(extent, BF) for extent in whole],
        in_specs=[vmem] * 14 + [hbm] * 4,
        out_specs=[vmem] * 4 + [hbm] * 6,
        scratch_shapes=[
            mem((size, width), BF), mem((pairs, n, 2 * size, PAIR), BF), mem((pairs, n, 2 * size, PAIR), BF),
            mem((pairs, n, 1, 2 * size), F32), mem((pairs, n, PAIR, size), F32), mem((rows, 3 * local), BF),
            mem((half, size, width), F32), block, block, block, block, mem((size, width), F32),
            *unit(half, width, hidden, "parity"), *unit(half, hidden, width, "parity"),
            *unit(n, local, width, "all"), *unit(n, width, local, "all"), *unit(n, local, width, "all"),
            *unit(1, width, 5 * local, "own"),
            mem((dp, few, width), F32), mem((n, few, width), F32), mem((few, width), F32),
            mem((2, width), F32), mem((dp, 2, width), F32), mem((n, 2, width), F32), mem((2, width), F32),
            mem((n, slots // n, width), BF), mem((n, slots // n, width), BF),
            dma((4, 1 + 2 * bits)), dma((4, 1 + 2 * bits)), dma((6, 1 + 2 * bits + n)), dma((6, 1 + 2 * bits + n)), dma((6, 2)),
            dma((4,)), dma((half,)), dma((half,)), dma((half,)), dma((half,)), dma((n,)), dma((n,)),
            dma((2, dp)), dma((2, dp)), dma((2, n)), dma((2, n)),
        ],
        compiler_params=pltpu.CompilerParams(collective_id=2, has_side_effects=True, vmem_limit_bytes=VMEM_LIMIT),
        cost_estimate=pl.CostEstimate(flops=8 << 30, bytes_accessed=48 << 20, transcendentals=4 << 20),
    )(gain1, qkv, kv, text, residual, projected, normed, mixed, totals, dmixed, dtext, early, mi_pieces, mo_pieces,
      image, so_grad, cq_grad, co_grad)


def body(sizes, image, text, grad_out, lengths, gain1, shift1, qkv, so, gain2, shift2, cq, kv, co, gain3, shift3, mi,
         in_bias, mo, out_bias):
    n = sizes["mp"]
    image, text, grad_out = image[0], text[0], grad_out[0]
    rows, width = image.shape
    local = so.shape[0]
    sizes = dict(sizes, share=share_of(local, sizes["dp"]))
    qkv, kv = qkv.reshape(width, 3 * local), kv.reshape(width, 2 * local)
    row = lambda value: value[None]
    (projected, normed1, mixed, totals, out, residual, dmixed, dtext, so_grad, cq_grad, co_grad, mi_pieces, mo_pieces,
     in_bias_grad, vectors) = layer(
        sizes, image, row(gain1), row(shift1), qkv, text, kv, row(lengths), row(gain2), row(shift2), row(gain3),
        row(shift3), row(in_bias), row(out_bias), so, cq, co, mi, mo, grad_out)
    early = jnp.zeros((8 + -(-n // 2 // 8) * 8, width), F32)
    early = lax.dynamic_update_slice(early, vectors, (0, 0))
    early = lax.dynamic_update_slice(early, in_bias_grad[:, 0], (8, 0))
    hidden = mi.shape[1]
    image_grad, text_grad, early, late, mi_sum, mo_sum, so_sum, cq_sum, co_sum, joint_sum = back(
        sizes, row(gain1), qkv, kv, text, residual, projected, normed1, mixed, totals, dmixed, dtext, early,
        mi_pieces, mo_pieces, image, so_grad, cq_grad, co_grad, hidden)
    return (
        out[None], image_grad[None], text_grad[None], late[0], late[1],
        joint_sum[:, : 3 * local].astype(F32).reshape(width, 3, local), so_sum.astype(F32), early[2], early[3],
        cq_sum.astype(F32), joint_sum[:, 3 * local :].astype(F32).reshape(width, 2, local), co_sum.astype(F32),
        early[4], early[5], mi_sum.astype(F32), early[7, :hidden], mo_sum.astype(F32), early[6],
    )


def solution(mesh):
    rows3, rows2, rows1 = P(None, None, "mp"), P(None, "mp"), P("mp")
    item = P("dp", None, None)
    in_specs = (item, item, item, P("dp"), P(), P(), rows3, P("mp", None), P(), P(), rows2, rows3, P("mp", None), P(), P(),
                rows2, rows1, P("mp", None), P())
    split = P("dp", "mp", None)
    out_specs = (split, split, split, P(), P(), rows3, P("mp", None), P(), P(), rows2, rows3, P("mp", None), P(), P(),
                 rows2, rows1, P("mp", None), P())
    sizes = dict(mesh.shape)
    return jax.shard_map(partial(body, sizes), mesh=mesh, in_specs=in_specs, out_specs=out_specs, check_vma=False)
```

```python
from functools import partial

import jax
import jax.numpy as jnp
from jax import lax
from jax.experimental import pallas as pl
from jax.experimental.pallas import tpu as pltpu
from jax.sharding import PartitionSpec as P

HEAD_DIM = 64
PAIR = 2 * HEAD_DIM
EPSILON = 1e-05
SCALE = HEAD_DIM ** (-0.5)
MASKED = -1e30
BF = jnp.bfloat16
F32 = jnp.float32
MESH = pl.DeviceIdType.MESH
VMEM_LIMIT = 60 << 20


def nn(a, b):
    return lax.dot_general(a, b, (((1,), (0,)), ((), ())), preferred_element_type=F32)


def nt(a, b):
    return lax.dot_general(a, b, (((1,), (1,)), ((), ())), preferred_element_type=F32)


def tn(a, b):
    return lax.dot_general(a, b, (((0,), (0,)), ((), ())), preferred_element_type=F32)


def norm_parts(value):
    center = value - jnp.mean(value, axis=-1, keepdims=True)
    inverse = lax.rsqrt(jnp.mean(center * center, axis=-1, keepdims=True) + EPSILON)
    return center * inverse, inverse


def half_masks():
    lane = lax.broadcasted_iota(jnp.int32, (1, PAIR), 1)
    first = jnp.where(lane < HEAD_DIM, 1.0, 0.0)
    return first, 1.0 - first


def stack_heads(pair, scale=None):
    first, second = half_masks()
    if scale is not None:
        first, second = first * scale, second * scale
    wide = pair.astype(F32)
    return jnp.concatenate([wide * first, wide * second], axis=0).astype(BF)


def fold_heads(stacked):
    rows = stacked.shape[1] // 2
    both = jnp.concatenate([stacked[:HEAD_DIM, :rows], stacked[HEAD_DIM:, rows:]], axis=0)
    return both.T


def causal(tile_keys, tile_rows):
    key = lax.broadcasted_iota(jnp.int32, (tile_keys, tile_rows), 0)
    row = lax.broadcasted_iota(jnp.int32, (tile_keys, tile_rows), 1)
    both = key <= row
    return jnp.concatenate([both, both], axis=1)


class Place:
    def __init__(self, sizes):
        self.n = sizes["mp"]
        self.dp = sizes["dp"]
        self.share = sizes["share"]
        self.d = lax.axis_index("dp")
        self.m = lax.axis_index("mp")
        self.core = lax.rem(self.d, 2)
        self.mate = self.m + 1 - 2 * lax.rem(self.m, 2)
        self.partner = (self.d + 1 - 2 * self.core, self.m)
        self.member = lax.rem(self.d, self.share)
        self.chip = self.member // 2
        self.base = self.d - self.member
        self.piece = self.core * (self.share // 2) + self.chip

    def along(self, offset):
        return lax.rem(self.m + offset, self.n)

    def mate_along(self, offset):
        return lax.rem(self.mate + offset, self.n)

    def peer(self, offset):
        return (self.d, self.along(offset))

    def chip_peer(self, offset):
        chip = lax.rem(self.chip + offset, self.share // 2)
        return (self.base + 2 * chip + self.core, self.m), self.core * (self.share // 2) + chip


def greet(devices):
    for device in devices:
        pl.semaphore_signal(pltpu.get_barrier_semaphore(), inc=1, device_id=device, device_id_type=MESH)


def meet(devices):
    pl.semaphore_wait(pltpu.get_barrier_semaphore(), len(devices))


class Gather:
    def __init__(self, place, own, full, everyone, slot_of, sems):
        self.place, self.own, self.full, self.slot_of = place, own, full, slot_of
        self.count = own.shape[0] // place.share
        self.sems = sems
        self.even = list(range(2, place.n, 2))
        self.sources = [place.along(place.n - k) for k in self.even]
        if everyone:
            self.sources.append(place.mate)
            self.sources += [place.mate_along(place.n - k) for k in self.even]
        self.everyone = everyone

    def rows_of(self, slot, piece, pieces=1):
        start = pl.multiple_of(piece * self.count, self.count)
        return self.full.at[slot, pl.ds(start, pieces * self.count), :]

    def copy(self, src, dst, index, hop, device):
        return pltpu.make_async_remote_copy(
            src_ref=src, dst_ref=dst, send_sem=self.sems[0].at[index, hop], recv_sem=self.sems[1].at[index, hop],
            device_id=device, device_id_type=MESH,
        )

    def first(self, index):
        place, parity = self.place, len(self.even)
        mine = self.own.at[pl.ds(pl.multiple_of(place.piece * self.count, self.count), self.count), :]
        slot = self.slot_of(place.m)
        if index < parity:
            device = place.peer(self.even[index])
        else:
            device = (place.d, place.mate)
        if index > parity:
            slot = self.slot_of(self.sources[index - parity - 1])
            mine = self.rows_of(slot, place.piece)
        return self.copy(mine, self.rows_of(slot, place.piece), index, 0, device)

    def second(self, index, hop):
        block = self.rows_of(self.slot_of(self.sources[index]), self.place.piece)
        return self.copy(block, block, index, hop, self.place.chip_peer(hop)[0])

    def third(self, index):
        half = self.place.share // 2
        block = self.rows_of(self.slot_of(self.sources[index]), self.place.core * half, half)
        return self.copy(block, block, index, half, self.place.partner)

    def local(self):
        return pltpu.make_async_copy(self.own, self.full.at[self.slot_of(self.place.m)], self.sems[2])

    def step(self, number):
        hops = range(1, self.place.share // 2)
        parity = len(self.even)
        everything = range(len(self.sources))
        if number == 0:
            for index in everything:
                if index <= parity:
                    self.first(index).start()
        elif number == 1:
            for index in range(parity):
                self.first(index).wait_recv()
                if self.everyone:
                    self.first(parity + 1 + index).start()
                for hop in hops:
                    self.second(index, hop).start()
        elif number == 2:
            for index in everything[parity:]:
                self.first(index).wait_recv()
                for hop in hops:
                    self.second(index, hop).start()
        elif number == 3:
            for index in everything:
                for hop in hops:
                    self.second(index, hop).wait_recv()
                self.third(index).start()
        else:
            for index in everything:
                self.third(index).wait()
                self.first(index).wait_send()
                for hop in hops:
                    self.second(index, hop).wait_send()

    def finish(self):
        self.step(4)
        self.local().wait()


def attend_block(projected, mixed, totals, i, hp, size, local):
    rows = pl.ds(pl.multiple_of(i * size, size), size)
    column = pl.multiple_of(hp * PAIR, PAIR)
    query = stack_heads(projected[rows, pl.ds(column, PAIR)], SCALE)

    def tile(j, carry, diagonal):
        largest, total, acc = carry
        keys = pl.ds(pl.multiple_of(j * size, size), size)
        key = projected[keys, pl.ds(column + local, PAIR)]
        value = projected[keys, pl.ds(column + 2 * local, PAIR)]
        scores = nt(key, query)
        if diagonal:
            scores = jnp.where(causal(size, size), scores, MASKED)
        top = jnp.maximum(largest, jnp.max(scores, axis=0, keepdims=True))
        powers = jnp.exp(scores - top)
        shrink = jnp.exp(largest - top)
        total = total * shrink + jnp.sum(powers, axis=0, keepdims=True)
        acc = acc * shrink + tn(value, powers.astype(BF))
        return top, total, acc

    carry = (
        jnp.full((1, 2 * size), MASKED, F32),
        jnp.zeros((1, 2 * size), F32),
        jnp.zeros((PAIR, 2 * size), F32),
    )
    carry = tile(i, carry, True)
    largest, total, acc = lax.fori_loop(0, i, lambda j, c: tile(j, c, False), carry)
    mixed[rows, pl.ds(column, PAIR)] = fold_heads(acc / total).astype(BF)
    totals[hp, i] = largest + jnp.log(total)


def share_of(local, dp):
    share = dp
    while (local // share) % 16:
        share //= 2
    return share


def halvings(rows, bits):
    left = [rows // 4]
    for _ in range(bits):
        left.append(left[-1] // 2 if left[-1] % 32 == 0 else left[-1])
    return left


def arrivals(rows, bits):
    left = halvings(rows, bits)
    return left[1:]


class Rows:
    def __init__(self, place, rows):
        self.place = place
        self.half = rows // 2
        self.bits = (place.dp // 2).bit_length() - 1
        self.left = halvings(rows, self.bits)
        self.count = self.left[-1]
        self.chip = place.d // 2

    def bit(self, p, k):
        b = k if p == 0 else self.bits - 1 - k
        value = lax.rem(self.chip // (1 << b), 2)
        chip = self.chip + (1 - 2 * value) * (1 << b)
        return value, (2 * chip + self.place.core, self.place.m)

    def cut(self, k):
        return self.left[k + 1] < self.left[k]

    def region(self, p, k):
        start = self.place.core * self.half + p * self.left[0]
        for t in range(k):
            if self.cut(t):
                start = start + self.bit(p, t)[0] * self.left[t + 1]
        return start

    def span(self, start, count):
        return pl.ds(pl.multiple_of(start, 16), count)


class Reduce:
    def __init__(self, place, ref, recv, pieces, sems):
        self.place, self.ref, self.recv, self.pieces = place, ref, recv, pieces
        self.rows = Rows(place, ref.shape[1])
        self.send, self.recv_sem = sems

    def copy(self, src, dst, index, device):
        return pltpu.make_async_remote_copy(
            src_ref=src, dst_ref=dst, send_sem=self.send.at[index], recv_sem=self.recv_sem.at[index],
            device_id=device, device_id_type=MESH,
        )

    def core_copy(self):
        half = self.rows.half
        away = self.rows.span((1 - self.place.core) * half, half)
        return self.copy(self.ref.at[:, away, :], self.recv.at[:, pl.ds(0, half), :], 0, self.place.partner)

    def offset(self, p, k):
        into = self.rows.left[1:]
        return self.rows.half + p * sum(into) + sum(into[:k])

    def chip_copy(self, p, k):
        rows = self.rows
        value, device = rows.bit(p, k)
        count = rows.left[k + 1]
        start = rows.region(p, k)
        if rows.cut(k):
            start = start + (1 - value) * count
        return self.copy(
            self.ref.at[:, rows.span(start, count), :], self.recv.at[:, pl.ds(self.offset(p, k), count), :],
            1 + p * rows.bits + k, device)

    def add(self, start, offset, count, target, target_start):
        chunk = min(32, count)
        span = self.rows.span

        def run(t, _):
            at = t * chunk
            for s in range(self.ref.shape[0]):
                mine = self.ref[s, span(start + at, chunk), :].astype(F32)
                theirs = self.recv[s, span(offset + at, chunk), :].astype(F32)
                target[s, span(target_start + at, chunk), :] = (mine + theirs).astype(BF)
            return 0

        lax.fori_loop(0, count // chunk, run, 0)

    def phases(self):
        rows = self.rows

        def begin():
            self.core_copy().start()

        def core_sum():
            self.core_copy().wait()
            self.add(self.place.core * rows.half, 0, rows.half, self.ref, self.place.core * rows.half)
            for p in range(2):
                self.chip_copy(p, 0).start()

        def chip_sum(k):
            last = k == rows.bits - 1
            for p in range(2):
                self.chip_copy(p, k).wait()
                start = rows.region(p, k + 1)
                self.add(start, self.offset(p, k), rows.left[k + 1], self.pieces if last else self.ref,
                         p * rows.count if last else start)
                if not last:
                    self.chip_copy(p, k + 1).start()

        return [begin, core_sum] + [partial(chip_sum, k) for k in range(rows.bits)]


class Spread:
    def __init__(self, place, rows, pieces, other, final, whole, rule, sems):
        self.place, self.pieces, self.other, self.final, self.whole = place, pieces, other, final, whole
        self.rows = Rows(place, rows)
        self.rule, (self.send, self.recv_sem, self.keep) = rule, sems
        if rule == "all":
            self.hops = [(k, place.along(k)) for k in range(1, place.n)]
            self.slot = place.m
        elif rule == "parity":
            half = place.n // 2
            self.hops = [(2 * k, lax.rem(place.m // 2 + k, half)) for k in range(1, half)]
            self.slot = place.m // 2
        else:
            self.hops, self.slot = [], 0

    def copy(self, src, dst, index, device):
        return pltpu.make_async_remote_copy(
            src_ref=src, dst_ref=dst, send_sem=self.send.at[index], recv_sem=self.recv_sem.at[index],
            device_id=device, device_id_type=MESH,
        )

    def far_copy(self, index):
        hop, slot = self.hops[index]
        return self.copy(self.pieces.at[slot], self.other.at[self.slot], 1 + 2 * self.rows.bits + index, self.place.peer(hop))

    def view(self, ref, start, count):
        span = self.rows.span(start, count)
        return ref.at[:, span, :] if self.rule == "own" else ref.at[span, :]

    def spread_copy(self, p, k):
        rows = self.rows
        count = rows.left[k + 1]
        block = self.view(self.whole, rows.region(p, k + 1), count)
        first = not any(rows.cut(t) for t in range(k + 1, rows.bits))
        src = self.view(self.final, p * rows.count, rows.count) if first else block
        return self.copy(src, block, 1 + p * rows.bits + k, rows.bit(p, k)[1])

    def keep_copy(self, p):
        rows = self.rows
        block = self.view(self.whole, rows.region(p, rows.bits), rows.count)
        return pltpu.make_async_copy(self.view(self.final, p * rows.count, rows.count), block, self.keep.at[p])

    def core_spread(self):
        half = self.rows.half
        block = self.view(self.whole, self.place.core * half, half)
        return self.copy(block, block, 0, self.place.partner)

    def phases(self):
        rows = self.rows
        cuts = [k for k in reversed(range(rows.bits)) if rows.cut(k)]

        def far():
            for index in range(len(self.hops)):
                self.far_copy(index).start()

        def far_sum():
            if self.hops:
                total = self.pieces[self.slot].astype(F32)
                for index, (hop, _) in enumerate(self.hops):
                    self.far_copy(index).wait()
                    source = self.place.along(self.place.n - hop)
                    total += self.other[source if self.rule == "all" else source // 2].astype(F32)
                self.final[...] = total.astype(BF)
            for p in range(2):
                self.keep_copy(p).start()
                self.spread_copy(p, cuts[0]).start()
            for p in range(2):
                self.keep_copy(p).wait()

        def spread(t):
            for p in range(2):
                self.spread_copy(p, cuts[t]).wait()
                if t + 1 < len(cuts):
                    self.spread_copy(p, cuts[t + 1]).start()
            if t + 1 == len(cuts):
                self.core_spread().start()

        def end():
            self.core_spread().wait()

        nothing = [lambda: None] * (rows.bits - len(cuts))
        return [far, far_sum] + [partial(spread, t) for t in range(len(cuts))] + nothing + [end]


def recv_space(count, rows, columns, bits):
    return pltpu.VMEM((count, rows // 2 + 2 * sum(arrivals(rows, bits)), columns), BF)


def piece_shape(count, rows, columns, bits):
    return jax.ShapeDtypeStruct((count, 2 * halvings(rows, bits)[-1], columns), BF)


def norm_back(grad, normal, inverse, gain):
    scaled = grad * gain
    return inverse * (
        scaled
        - jnp.mean(scaled, axis=-1, keepdims=True)
        - normal * jnp.mean(scaled * normal, axis=-1, keepdims=True)
    )


def add_rows(ref, index, value):
    ref[pl.ds(index, 1), :] += jnp.sum(value, axis=0, keepdims=True)


def in_chunks(total, chunk, step):
    def run(i, _):
        step(pl.ds(pl.multiple_of(i * chunk, chunk), chunk))
        return 0

    lax.fori_loop(0, total // chunk, run, 0)


def cross_pair(query, text_proj, length, idx, local):
    per = local // PAIR
    g, hp = idx // per, lax.rem(idx, per)
    near = pl.multiple_of(hp * PAIR, PAIR)
    column = pl.multiple_of(idx * PAIR, PAIR)
    stacked = stack_heads(query[:, pl.ds(column, PAIR)], SCALE)
    key = text_proj[g, :, pl.ds(near, PAIR)]
    value = text_proj[g, :, pl.ds(near + local, PAIR)]
    scores = nt(key, stacked)
    slot = lax.broadcasted_iota(jnp.int32, scores.shape, 0)
    return g, near, column, stacked, key, value, jnp.where(slot < length, scores, MASKED)


ROWS_AT_ONCE = 32


def layer_kernel(
    sizes,
    image, gain1, shift1, qkv, text, kv, length, gain2, shift2, gain3, shift3, in_bias, out_bias,
    so, cq, co, mi, mo, grad_out,
    projected, normed, mixed, totals, out, residual, dmixed, dtext, so_grad, cq_grad, co_grad, mi_pieces, mo_pieces,
    vectors,
    mixed_rows, text_proj, so_full, cq_full, co_full, mi_full, mo_full, bias_full,
    grad_pair, mixed_all, first, second, work, grad2, out_part,
    n2, query, cross, cross_totals, dquery, n3_pair, active, dhidden,
    dn3_send, dn3_recv, out_send, out_recv, r2, dcross, r1, dmixed_send, dtext_send, dtext_recv,
    text_own, mi_recv, mo_recv, small_send, small_recv, small_own, wide_send, wide_recv, wide_own,
    mix_send, mix_recv, mix_own, text_send, text_recv, bias_send, bias_recv, load_sem,
    pair_send, pair_recv, dmix_send, dmix_recv, dtext_ssem, dtext_rsem, store_sem, reduce_send, reduce_recv,
):
    place = Place(sizes)
    n, share = place.n, place.share
    rows, width = image.shape
    size = rows // n
    local, hidden = so.shape[0], mi.shape[1]
    half = n // 2
    offsets = list(range(1, n))
    mate = (place.d, place.mate)
    mine = place.m // 2
    chips = place.dp // 2
    partners = [place.peer(k) for k in offsets] + [place.partner]
    partners += [(2 * lax.rem(place.d // 2 + k, chips) + place.core, place.m) for k in range(1, chips)]
    greet(partners)
    meet(partners)

    def remote(src, dst, send, recv, device):
        return pltpu.make_async_remote_copy(
            src_ref=src, dst_ref=dst, send_sem=send, recv_sem=recv, device_id=device, device_id_type=MESH
        )

    small = [
        Gather(place, own, full, True, lambda s: s, (small_send.at[t], small_recv.at[t], small_own.at[t]))
        for t, (own, full) in enumerate(((so, so_full), (cq, cq_full), (co, co_full)))
    ]
    wide = [
        Gather(place, own, full, False, lambda s: s // 2, (wide_send.at[t], wide_recv.at[t], wide_own.at[t]))
        for t, (own, full) in enumerate(((mi, mi_full), (mo, mo_full)))
    ]
    for item in small:
        item.step(0)
    for item in small + wide:
        item.local().start()
    wide[0].step(0)

    def block_of(index):
        return pl.ds(pl.multiple_of(index * size, size), size)

    own_rows = block_of(place.m)
    loads = [
        pltpu.make_async_copy(grad_out.at[own_rows, :], grad_pair.at[0], load_sem.at[0]),
        pltpu.make_async_copy(grad_out.at[block_of(mate[1]), :], grad_pair.at[1], load_sem.at[1]),
    ]
    for load in loads:
        load.start()
    bias_full[mine] = in_bias[...]

    def bias_copy(k):
        return remote(in_bias, bias_full.at[mine], bias_send.at[k], bias_recv.at[k], place.peer(2 * k))

    for k in range(1, half):
        bias_copy(k).start()

    def project(i, _):
        block = block_of(i)

        def norm(chunk):
            at = pl.ds(pl.multiple_of(i * size + chunk.start, ROWS_AT_ONCE), ROWS_AT_ONCE)
            normal, _ = norm_parts(image[at, :].astype(F32))
            normed[at, :] = (normal * gain1[...] + shift1[...]).astype(BF)

        in_chunks(size, ROWS_AT_ONCE, norm)
        for t in range(3):
            projected[block, t * local : (t + 1) * local] = nn(normed[block, :], qkv[t]).astype(BF)
        return 0

    lax.fori_loop(0, n, project, 0)
    text_own[...] = nn(text[...], kv[...]).astype(BF)
    text_proj[place.m] = text_own[...]

    even = list(range(2, n, 2))

    def text_copy(k):
        return remote(text_own, text_proj.at[place.m], text_send.at[k], text_recv.at[k], place.peer(k) if k else mate)

    def text_pass(k):
        block = text_proj.at[place.along(n - k)]
        return remote(block, block, text_send.at[k + 1], text_recv.at[k + 1], mate)

    for k in [0] + even:
        text_copy(k).start()

    def mix_copy(i):
        gap = lax.rem(i - place.m + n, n)
        return remote(mixed.at[block_of(i), :], mixed_rows.at[place.m], mix_send.at[gap], mix_recv.at[gap], (place.d, i))

    mix_keep = pltpu.make_async_copy(mixed.at[own_rows, :], mixed_rows.at[place.m], mix_own)
    for item in small:
        item.step(1)
    plan = [[] for _ in range(n)]
    plan[1] = [small[0]]
    plan[2] = [small[1]]
    plan[n - 1] += [small[2]]
    for i in range(n):
        lax.fori_loop(0, local // PAIR, lambda hp, _: (attend_block(projected, mixed, totals, i, hp, size, local), 0)[1], 0)

        @pl.when(place.m != i)
        def _():
            mix_copy(i).start()

        @pl.when(place.m == i)
        def _():
            mix_keep.start()

        for item in plan[i]:
            item.step(2)

    wide[1].step(0)
    for k in even:
        text_copy(k).wait_recv()
        text_pass(k).start()
    small[0].step(3)

    for k in offsets:
        mix_copy(place.along(k)).wait()
    mix_keep.wait()
    small[0].finish()
    small[1].step(3)
    for g in range(n):
        mixed_all[:, g * local : (g + 1) * local] = mixed_rows[g]
    first[...] = nn(mixed_all[...], so_full[...].reshape(n * local, width))

    def first_norm(chunk):
        at = pl.ds(pl.multiple_of(place.m * size + chunk.start, ROWS_AT_ONCE), ROWS_AT_ONCE)
        value = image[at, :].astype(F32) + first[chunk, :]
        first[chunk, :] = value
        n2[chunk, :] = (norm_parts(value)[0] * gain2[...] + shift2[...]).astype(BF)

    in_chunks(size, ROWS_AT_ONCE, first_norm)
    small[1].finish()
    small[2].step(3)
    for g in range(n):
        query[:, g * local : (g + 1) * local] = nn(n2[...], cq_full[g]).astype(BF)
    text_copy(0).wait()
    for k in even:
        text_copy(k).wait_send()
        text_pass(k).wait()
    for item in wide:
        item.step(1)
    limit = length[0, 0]
    all_pairs = n * local // PAIR

    def cross_forward(idx, _):
        g, near, column, stacked, key, value, scores = cross_pair(query, text_proj, limit, idx, local)
        largest = jnp.max(scores, axis=0, keepdims=True)
        powers = jnp.exp(scores - largest)
        total = jnp.sum(powers, axis=0, keepdims=True)
        cross_totals[idx] = largest + jnp.log(total)
        cross[:, pl.ds(column, PAIR)] = fold_heads(tn(value, (powers / total).astype(BF))).astype(BF)
        return 0

    lax.fori_loop(0, all_pairs, cross_forward, 0)
    small[2].finish()
    second[...] = nn(cross[...], co_full[...].reshape(n * local, width))

    def second_norm(chunk):
        value = first[chunk, :] + second[chunk, :]
        second[chunk, :] = value
        n3_pair[0, chunk, :] = (norm_parts(value)[0] * gain3[...] + shift3[...]).astype(BF)

    in_chunks(size, ROWS_AT_ONCE, second_norm)

    n3_copy = remote(n3_pair.at[0], n3_pair.at[1], pair_send.at[0], pair_recv.at[0], mate)
    n3_copy.start()
    for load in loads:
        load.wait()
    for k in range(1, half):
        bias_copy(k).wait()
    for item in wide:
        item.local().wait()
    step = min(256, hidden)

    def feed(p, slot):
        grads = grad_pair[p]

        def chunk(c, _):
            columns = pl.ds(pl.multiple_of(c * step, step), step)
            value = nn(n3_pair[p], mi_full[slot, :, columns]) + bias_full[slot, :, columns]
            inner = 0.5 * (1.0 + lax.erf(value * (0.5**0.5)))
            slope = inner + value * jnp.exp(-0.5 * value * value) * ((2.0 * jnp.pi) ** -0.5)
            active[slot, p, :, columns] = (value * inner).astype(BF)
            dhidden[slot, p, :, columns] = (nt(grads, mo_full[slot, columns, :]) * slope).astype(BF)
            return 0

        lax.fori_loop(0, hidden // step, chunk, 0)

    def sum_slots(term):
        total = term(0)
        for slot in range(1, half):
            total += term(slot)
        return total

    feed(0, mine)
    n3_copy.wait()
    feed(1, mine)
    for item in wide:
        item.step(3)
    for item in wide:
        item.step(4)
    others = [lax.rem(mine + k, half) for k in range(1, half)]
    for slot in others:
        feed(1, slot)
    dn3_send[...] = sum_slots(lambda slot: nt(dhidden[slot, 1], mi_full[slot])).astype(BF)
    dn3_copy = remote(dn3_send, dn3_recv, pair_send.at[1], pair_recv.at[1], mate)
    dn3_copy.start()
    out_send[...] = sum_slots(lambda slot: nn(active[slot, 1], mo_full[slot])).astype(BF)
    out_copy = remote(out_send, out_recv, pair_send.at[2], pair_recv.at[2], mate)
    out_copy.start()
    for slot in others:
        feed(0, slot)
    work[...] = sum_slots(lambda slot: nt(dhidden[slot, 0], mi_full[slot]))
    out_part[...] = sum_slots(lambda slot: nn(active[slot, 0], mo_full[slot]))
    tile = min(256, width)

    def wide_grads(slot):
        inner = n3_pair.shape[0] * size
        hidden_grad = dhidden[slot].reshape(inner, hidden)
        grads = grad_pair[...].reshape(inner, width)
        vectors[8 + slot : 9 + slot, 0:hidden] = jnp.sum(hidden_grad.astype(F32), axis=0, keepdims=True)

        def into(t, _):
            at = pl.ds(pl.multiple_of(t * tile, tile), tile)
            mi_full[slot, at, :] = tn(n3_pair[:, :, at].reshape(inner, tile), hidden_grad).astype(BF)
            return 0

        lax.fori_loop(0, width // tile, into, 0)

        def back(t, _):
            at = pl.ds(pl.multiple_of(t * step, step), step)
            mo_full[slot, at, :] = tn(active[slot, :, :, at].reshape(inner, step), grads).astype(BF)
            return 0

        lax.fori_loop(0, hidden // step, back, 0)

    vectors[...] = jnp.zeros_like(vectors)
    for slot in range(half):
        wide_grads(slot)
    mi_steps = Reduce(place, mi_full, mi_recv, mi_pieces, (reduce_send.at[0], reduce_recv.at[0])).phases()
    mo_steps = Reduce(place, mo_full, mo_recv, mo_pieces, (reduce_send.at[1], reduce_recv.at[1])).phases()
    wide_steps = [step for pair in zip(mi_steps, mo_steps) for step in pair]
    for run in wide_steps[:2]:
        run()
    dn3_copy.wait()


    def third_back(chunk):
        grad = work[chunk, :] + dn3_recv[chunk, :].astype(F32)
        normal, inverse = norm_parts(second[chunk, :])
        above = grad_pair[0, chunk, :].astype(F32)
        add_rows(vectors, 4, grad * normal)
        add_rows(vectors, 5, grad)
        add_rows(vectors, 6, above)
        value = above + norm_back(grad, normal, inverse, gain3[...])
        work[chunk, :] = value
        r2[chunk, :] = value.astype(BF)

    in_chunks(size, ROWS_AT_ONCE, third_back)
    wide_steps[2]()
    dcross[...] = nt(r2[...], co_full[...].reshape(n * local, width)).astype(BF)

    def cross_back(idx, _):
        g, near, column, stacked, key, value, scores = cross_pair(query, text_proj, limit, idx, local)
        weights = jnp.exp(scores - cross_totals[idx])
        above = stack_heads(dcross[:, pl.ds(column, PAIR)])
        dweights = nt(value, above)
        dscores = (weights * (dweights - jnp.sum(weights * dweights, axis=0, keepdims=True))).astype(BF)
        dquery[:, pl.ds(column, PAIR)] = (fold_heads(tn(key, dscores)) * SCALE).astype(BF)
        dtext_send[g, :, pl.ds(near, PAIR)] = nn(dscores, stacked).astype(BF)
        dtext_send[g, :, pl.ds(near + local, PAIR)] = nn(weights.astype(BF), above).astype(BF)
        return 0

    lax.fori_loop(0, all_pairs, cross_back, 0)
    wide_steps[3]()

    def dtext_copy(k):
        return remote(dtext_send.at[place.along(k)], dtext_recv.at[place.m], dtext_ssem.at[k], dtext_rsem.at[k], place.peer(k))

    for k in offsets:
        dtext_copy(k).start()
    def both(term):
        total = term(0)
        for g in range(1, n):
            total += term(g)
        return total

    grad2[...] = both(lambda g: nt(dquery[:, g * local : (g + 1) * local], cq_full[g]))

    def second_back(chunk):
        grad = grad2[chunk, :]
        normal, inverse = norm_parts(first[chunk, :])
        add_rows(vectors, 2, grad * normal)
        add_rows(vectors, 3, grad)
        value = work[chunk, :] + norm_back(grad, normal, inverse, gain2[...])
        residual[chunk, :] = value
        r1[chunk, :] = value.astype(BF)

    in_chunks(size, ROWS_AT_ONCE, second_back)

    def dmix_copy(k):
        return remote(dmixed_send.at[k], dmixed.at[own_rows, :], dmix_send.at[k], dmix_recv.at[k], place.peer(k))

    for k in offsets:
        dmixed_send[k] = nt(r1[...], so_full[place.along(k)]).astype(BF)
        dmix_copy(k).start()
    dmixed[own_rows, :] = nt(r1[...], so_full[place.m]).astype(BF)
    wide_steps[4]()

    stores = []

    def small_grad(left, right, keep, target, index):
        for g in range(n):
            heads = slice(g * local, (g + 1) * local)
            if keep.shape[1] == local:
                keep[g] = tn(left[:, heads], right[...]).astype(BF)
            else:
                keep[g] = tn(left[...], right[:, heads]).astype(BF)
        copy = pltpu.make_async_copy(keep, target, store_sem.at[index])
        copy.start()
        stores.append(copy)

    small_grad(n2, dquery, cq_full, cq_grad, 0)
    small_grad(mixed_all, r1, so_full, so_grad, 1)
    small_grad(cross, r2, co_full, co_grad, 2)

    wide_steps[5]()
    out_copy.wait()

    def finish_out(chunk):
        value = second[chunk, :] + out_part[chunk, :] + out_recv[chunk, :].astype(F32) + out_bias[...]
        out[chunk, :] = value.astype(BF)

    in_chunks(size, ROWS_AT_ONCE, finish_out)
    for run in wide_steps[6:]:
        run()
    for k in offsets:
        dtext_copy(k).wait()
    total = dtext_send[place.m].astype(F32)
    for k in offsets:
        total += dtext_recv[place.along(k)].astype(F32)
    dtext[...] = total.astype(BF)
    for k in offsets:
        dmix_copy(k).wait()
    for store in stores:
        store.wait()


def layer(sizes, image, gain1, shift1, qkv, text, kv, length, gain2, shift2, gain3, shift3, in_bias, out_bias,
          so, cq, co, mi, mo, grad_out):
    n, share = sizes["mp"], sizes["share"]
    rows, width = image.shape
    slots = text.shape[0]
    local, hidden = so.shape[0], mi.shape[1]
    size = rows // n
    pairs = local // PAIR
    hops = share // 2 + 1
    half = n // 2
    vmem, hbm = pl.BlockSpec(memory_space=pltpu.VMEM), pl.BlockSpec(memory_space=pl.ANY)
    dma, mem = pltpu.SemaphoreType.DMA, pltpu.VMEM
    shape = jax.ShapeDtypeStruct
    few = max(half - 1, 1)
    bits = (sizes["dp"] // 2).bit_length() - 1
    return pl.pallas_call(
        partial(layer_kernel, sizes),
        out_shape=[
            shape((rows, 3 * local), BF), shape((rows, width), BF), shape((rows, local), BF),
            shape((pairs, n, 1, 2 * size), F32), shape((size, width), BF), shape((size, width), F32),
            shape((rows, local), BF), shape((slots, 2 * local), BF),
            shape((n, local, width), BF), shape((n, width, local), BF), shape((n, local, width), BF),
            piece_shape(half, width, hidden, bits), piece_shape(half, hidden, width, bits),
            shape((8 + -(-half // 8) * 8, width), F32),
        ],
        in_specs=[vmem] * 6 + [pl.BlockSpec(memory_space=pltpu.SMEM)] + [vmem] * 6 + [hbm] * 6,
        out_specs=[vmem] * 8 + [hbm] * 3 + [vmem] * 3,
        scratch_shapes=[
            mem((n, size, local), BF), mem((n, slots, 2 * local), BF),
            mem((n, local, width), BF), mem((n, width, local), BF), mem((n, local, width), BF),
            mem((half, width, hidden), BF), mem((half, hidden, width), BF), mem((half, 1, hidden), F32),
            mem((2, size, width), BF), mem((size, n * local), BF),
            mem((size, width), F32), mem((size, width), F32), mem((size, width), F32), mem((size, width), F32),
            mem((size, width), F32),
            mem((size, width), BF), mem((size, n * local), BF), mem((size, n * local), BF),
            mem((n * pairs, 1, 2 * size), F32), mem((size, n * local), BF),
            mem((2, size, width), BF), mem((half, 2, size, hidden), BF), mem((half, 2, size, hidden), BF),
            mem((size, width), BF), mem((size, width), BF), mem((size, width), BF), mem((size, width), BF),
            mem((size, width), BF), mem((size, n * local), BF), mem((size, width), BF),
            mem((n, size, local), BF), mem((n, slots, 2 * local), BF), mem((n, slots, 2 * local), BF),
            mem((slots, 2 * local), BF), recv_space(half, width, hidden, bits), recv_space(half, hidden, width, bits),
            dma((3, n - 1, hops)), dma((3, n - 1, hops)), dma((3,)),
            dma((2, few, hops)), dma((2, few, hops)), dma((2,)),
            dma((n,)), dma((n,)), dma(()),
            dma((n + 1,)), dma((n + 1,)), dma((half,)), dma((half,)), dma((2,)),
            dma((3,)), dma((3,)), dma((n,)), dma((n,)), dma((n,)), dma((n,)), dma((3,)), dma((2, 1 + 2 * bits)), dma((2, 1 + 2 * bits)),
        ],
        compiler_params=pltpu.CompilerParams(collective_id=1, has_side_effects=True, vmem_limit_bytes=VMEM_LIMIT),
        cost_estimate=pl.CostEstimate(flops=22 << 30, bytes_accessed=48 << 20, transcendentals=8 << 20),
    )(image, gain1, shift1, qkv, text, kv, length, gain2, shift2, gain3, shift3, in_bias, out_bias,
      so, cq, co, mi, mo, grad_out)


def back_kernel(
    sizes,
    gain1, qkv, kv, text, residual, projected, normed, mixed, totals, dmixed, dtext, early, mi_pieces, mo_pieces,
    image, so_grad, cq_grad, co_grad,
    image_grad, text_grad, early_out, late_out, mi_out, mo_out, so_out, cq_out, co_out, joint_out,
    image_rows, stacked, above, delta, dquery, dprojected,
    near_hold, near_send, near_recv, far_send, far_recv, dn1_own,
    mi_other, mi_final, mo_other, mo_final,
    so_ref, so_recv, so_pieces, so_other, so_final, cq_ref, cq_recv, cq_pieces, cq_other, cq_final,
    co_ref, co_recv, co_pieces, co_other, co_final, joint_ref, joint_recv, joint_pieces,
    early_dp, early_mp, early_own, late, late_dp, late_mp, late_own, text_send, text_recv,
    reduce_send, reduce_recv, spread_send, spread_recv, spread_keep, load_sem,
    near_ssem, near_rsem, far_ssem, far_rsem, text_ssem, text_rsem, vec_ssem, vec_rsem, vec_zsend, vec_zrecv,
):
    place = Place(sizes)
    n, dp = place.n, place.dp
    rows, width = normed.shape
    local = mixed.shape[1]
    size = rows // n
    half = n // 2
    pairs = local // PAIR
    offsets = list(range(1, n))
    everyone = [lax.rem(place.d + k, dp) for k in range(1, dp)]
    partners = [place.peer(k) for k in offsets] + [(device, place.m) for device in everyone]
    greet(partners)

    def remote(src, dst, send, recv, device):
        return pltpu.make_async_remote_copy(
            src_ref=src, dst_ref=dst, send_sem=send, recv_sem=recv, device_id=device, device_id_type=MESH
        )

    def block_of(index):
        return pl.ds(pl.multiple_of(index * size, size), size)

    loads = [
        pltpu.make_async_copy(src, dst, load_sem.at[t])
        for t, (src, dst) in enumerate((
            (so_grad, so_ref), (cq_grad, cq_ref), (co_grad, co_ref), (image.at[block_of(place.m), :], image_rows),
        ))
    ]
    for load in loads:
        load.start()

    def reduce(t, ref, recv, pieces):
        return Reduce(place, ref, recv, pieces, (reduce_send.at[t], reduce_recv.at[t])).phases()

    def spread(t, rows, pieces, other, final, whole, rule):
        sems = (spread_send.at[t], spread_recv.at[t], spread_keep.at[t])
        return Spread(place, rows, pieces, other, final, whole, rule, sems).phases()

    mi_steps = spread(0, width, mi_pieces, mi_other, mi_final, mi_out, "parity")
    mo_steps = spread(1, mo_out.shape[0], mo_pieces, mo_other, mo_final, mo_out, "parity")
    so_steps = reduce(0, so_ref, so_recv, so_pieces) + spread(2, local, so_pieces, so_other, so_final, so_out, "all")
    cq_steps = reduce(1, cq_ref, cq_recv, cq_pieces) + spread(3, width, cq_pieces, cq_other, cq_final, cq_out, "all")
    co_steps = reduce(2, co_ref, co_recv, co_pieces) + spread(4, local, co_pieces, co_other, co_final, co_out, "all")
    joint_steps = reduce(3, joint_ref, joint_recv, joint_pieces)
    joint_steps += spread(5, width, joint_pieces, None, joint_pieces, joint_out, "own")
    class Vectors:
        def __init__(self, value, over_dp, own, over_mp, base):
            self.value, self.over_dp, self.own, self.over_mp, self.base = value, over_dp, own, over_mp, base

        def first(self, k):
            return remote(self.value, self.over_dp.at[place.d], vec_ssem.at[self.base, k], vec_rsem.at[self.base, k],
                          (everyone[k - 1], place.m))

        def second(self, k):
            return remote(self.own, self.over_mp.at[place.m], vec_zsend.at[self.base, k], vec_zrecv.at[self.base, k],
                          place.peer(k))

        def begin(self):
            self.over_dp[place.d] = self.value[...]
            for k in range(1, dp):
                self.first(k).start()

        def turn(self):
            for k in range(1, dp):
                self.first(k).wait()
            total = self.over_dp[0]
            for j in range(1, dp):
                total += self.over_dp[j]
            self.own[...] = total
            self.over_mp[place.m] = total
            for k in offsets:
                self.second(k).start()

        def end(self):
            for k in offsets:
                self.second(k).wait()

        def total(self):
            value = self.over_mp[0]
            for j in range(1, n):
                value += self.over_mp[j]
            return value

    early_sum = Vectors(early, early_dp, early_own, early_mp, 0)
    late_sum = Vectors(late, late_dp, late_own, late_mp, 1)
    part = text_grad.shape[0]
    spread_text = nt(dtext[...], kv[...]).astype(BF)
    for g in range(n):
        text_send[g] = spread_text[g * part : (g + 1) * part, :]

    def text_copy(k):
        return remote(text_send.at[place.along(k)], text_recv.at[place.m], text_ssem.at[k], text_rsem.at[k], place.peer(k))

    for t in range(2):
        joint_ref[3 + t] = tn(text[...], dtext[:, t * local : (t + 1) * local]).astype(BF)

    def prepare(i, _):
        block = block_of(i)
        for hp in range(pairs):
            columns = slice(hp * PAIR, (hp + 1) * PAIR)
            stacked[hp, i] = stack_heads(projected[block, columns], SCALE)
            above[hp, i] = stack_heads(dmixed[block, columns])
            product = (dmixed[block, columns].astype(F32) * mixed[block, columns].astype(F32)).T
            delta[hp, i] = jnp.concatenate(
                [jnp.sum(product[:HEAD_DIM], axis=0, keepdims=True), jnp.sum(product[HEAD_DIM:], axis=0, keepdims=True)],
                axis=1,
            )
            dquery[hp, i] = jnp.zeros_like(dquery[hp, i])
        return 0

    lax.fori_loop(0, n, prepare, 0)
    meet(partners)
    mi_steps[0]()
    mo_steps[0]()
    for load, steps in zip(loads, (so_steps, cq_steps, co_steps)):
        load.wait()
        steps[0]()
    early_sum.begin()
    for k in offsets:
        text_copy(k).start()

    plan = [[so_steps[1]], [cq_steps[1]], [co_steps[1]]]
    each = -(-len(plan) // (n * pairs))
    parity = lax.rem(place.m, 2)
    mine = place.m // 2

    def near_copy(t):
        return remote(near_send.at[t], near_recv.at[t], near_ssem.at[t], near_rsem.at[t], (place.d, place.mate))

    def far_copy(t):
        gap = lax.rem(t - mine + half, half)
        return remote(far_send.at[t], far_recv.at[mine], far_ssem.at[gap], far_rsem.at[gap], (place.d, 2 * t + parity))

    def pass_on(t):
        near_copy(t).wait()
        total = near_hold[t] + near_recv[t].astype(F32)

        @pl.when(mine == t)
        def _():
            dn1_own[...] = total

        @pl.when(mine != t)
        def _():
            far_send[t] = total.astype(BF)
            far_copy(t).start()

    point = 0
    for j in range(n):
        keys = slice(j * size, (j + 1) * size)
        for hp in range(pairs):
            columns = slice(hp * PAIR, (hp + 1) * PAIR)
            key = projected[keys, local + hp * PAIR : local + (hp + 1) * PAIR]
            value = projected[keys, 2 * local + hp * PAIR : 2 * local + (hp + 1) * PAIR]

            def tile(i, carry, diagonal):
                dkey, dvalue = carry
                query, over = stacked[hp, i], above[hp, i]
                scores = nt(key, query)
                if diagonal:
                    scores = jnp.where(causal(size, size), scores, MASKED)
                weights = jnp.exp(scores - totals[hp, i])
                dscores = (weights * (nt(value, over) - delta[hp, i])).astype(BF)
                dvalue = dvalue + nn(weights.astype(BF), over)
                dkey = dkey + nn(dscores, query)
                turned = tn(key, dscores)
                dquery[hp, i] += jnp.concatenate([turned[:HEAD_DIM, :size], turned[HEAD_DIM:, size:]], axis=0)
                return dkey, dvalue

            carry = (jnp.zeros((size, PAIR), F32), jnp.zeros((size, PAIR), F32))
            carry = tile(j, carry, True)
            dkey, dvalue = lax.fori_loop(j + 1, n, lambda i, c: tile(i, c, False), carry)
            dprojected[keys, columns] = (dquery[hp, j].T * SCALE).astype(BF)
            dprojected[keys, local + hp * PAIR : local + (hp + 1) * PAIR] = dkey.astype(BF)
            dprojected[keys, 2 * local + hp * PAIR : 2 * local + (hp + 1) * PAIR] = dvalue.astype(BF)
            for phases in plan[point * each : (point + 1) * each]:
                for phase in phases:
                    phase()
            point += 1
        partial_sum = sum(nt(dprojected[keys, t * local : (t + 1) * local], qkv[t]) for t in range(3))

        @pl.when(parity == j % 2)
        def _():
            near_hold[j // 2] = partial_sum

        @pl.when(parity != j % 2)
        def _():
            near_send[j // 2] = partial_sum.astype(BF)
            near_copy(j // 2).start()

    tile_rows = min(256, width)

    def qkv_grad(t, _):
        at = pl.ds(pl.multiple_of(t * tile_rows, tile_rows), tile_rows)
        total = tn(normed[:, at], dprojected[...]).astype(BF)
        for t in range(3):
            joint_ref[t, at, :] = total[:, t * local : (t + 1) * local]
        return 0

    lax.fori_loop(0, width // tile_rows, qkv_grad, 0)
    bits = (dp // 2).bit_length() - 1
    small_steps = (so_steps, cq_steps, co_steps)
    joint_steps[0]()
    early_sum.turn()
    for steps in small_steps:
        steps[2]()
    joint_steps[1]()
    for t in range(half - 1):
        pass_on(t)
    mi_steps[1]()
    mo_steps[1]()
    pass_on(half - 1)
    for k in range(1, bits):
        for steps in small_steps:
            steps[2 + k]()
    for steps in small_steps:
        steps[2 + bits]()
    for k in range(bits):
        joint_steps[2 + k]()
    joint_steps[2 + bits]()
    joint_steps[3 + bits]()
    mi_steps[2]()
    mo_steps[2]()
    for steps in small_steps:
        steps[3 + bits]()
    for k in range(1, bits):
        mi_steps[2 + k]()
        mo_steps[2 + k]()
    joint_steps[4 + bits]()
    for k in range(bits - 1):
        for steps in small_steps:
            steps[4 + bits + k]()

    for k in range(1, half):
        far_copy(lax.rem(mine + k, half)).wait()
        dn1_own[...] += far_recv[lax.rem(mine + half - k, half)].astype(F32)
    loads[3].wait()
    late[...] = jnp.zeros_like(late)

    def last_back(chunk):
        grad = dn1_own[chunk, :]
        normal, inverse = norm_parts(image_rows[chunk, :].astype(F32))
        add_rows(late, 0, grad * normal)
        add_rows(late, 1, grad)
        image_grad[chunk, :] = residual[chunk, :] + norm_back(grad, normal, inverse, gain1[...])

    in_chunks(size, ROWS_AT_ONCE, last_back)
    late_sum.begin()
    for steps in small_steps:
        steps[3 + 2 * bits]()
    for k in offsets:
        text_copy(k).wait()
    total = text_send[place.m].astype(F32)
    for k in offsets:
        total += text_recv[place.along(k)].astype(F32)
    text_grad[...] = total
    late_sum.turn()
    early_sum.end()
    early_out[...] = early_sum.total()
    shared = early_out[pl.ds(8 + place.m // 2, 1), :] * 0.0
    for j in range(n):
        take = jnp.where(lax.rem(place.m + j, 2) == 0, 1.0, 0.0)
        shared += early_mp[j, pl.ds(8 + place.m // 2, 1), :] * take
    early_out[7:8, :] = shared
    for k in range(1, bits):
        joint_steps[4 + bits + k]()
    late_sum.end()
    late_out[...] = late_sum.total()
    for steps in (mi_steps, mo_steps, *small_steps, joint_steps):
        steps[-1]()


def back(sizes, gain1, qkv, kv, text, residual, projected, normed, mixed, totals, dmixed, dtext, early, mi_pieces, mo_pieces,
         image, so_grad, cq_grad, co_grad, hidden):
    n, dp = sizes["mp"], sizes["dp"]
    rows, width = normed.shape
    slots = text.shape[0]
    local = mixed.shape[1]
    size, pairs, half = rows // n, local // PAIR, n // 2
    bits = (dp // 2).bit_length() - 1
    vmem, hbm = pl.BlockSpec(memory_space=pltpu.VMEM), pl.BlockSpec(memory_space=pl.ANY)
    dma, mem = pltpu.SemaphoreType.DMA, pltpu.VMEM
    shape = jax.ShapeDtypeStruct

    def unit(count, height, columns, rule):
        pieces = piece_shape(count, height, columns, bits).shape
        scratch = []
        if rule != "parity":
            scratch += [mem((count, height, columns), BF), recv_space(count, height, columns, bits), mem(pieces, BF)]
        if rule != "own":
            scratch += [mem(pieces, BF), mem(pieces[1:], BF)]
        return scratch

    few = early.shape[0]
    whole = [(width, hidden), (hidden, width), (local, width), (width, local), (local, width), (5, width, local)]
    block = mem((half, size, width), BF)
    return pl.pallas_call(
        partial(back_kernel, sizes),
        out_shape=[
            shape((size, width), F32), shape((slots // n, width), F32), shape((few, width), F32), shape((2, width), F32),
        ] + [shape(extent, BF) for extent in whole],
        in_specs=[vmem] * 14 + [hbm] * 4,
        out_specs=[vmem] * 4 + [hbm] * 6,
        scratch_shapes=[
            mem((size, width), BF), mem((pairs, n, 2 * size, PAIR), BF), mem((pairs, n, 2 * size, PAIR), BF),
            mem((pairs, n, 1, 2 * size), F32), mem((pairs, n, PAIR, size), F32), mem((rows, 3 * local), BF),
            mem((half, size, width), F32), block, block, block, block, mem((size, width), F32),
            *unit(half, width, hidden, "parity"), *unit(half, hidden, width, "parity"),
            *unit(n, local, width, "all"), *unit(n, width, local, "all"), *unit(n, local, width, "all"),
            *unit(5, width, local, "own"),
            mem((dp, few, width), F32), mem((n, few, width), F32), mem((few, width), F32),
            mem((2, width), F32), mem((dp, 2, width), F32), mem((n, 2, width), F32), mem((2, width), F32),
            mem((n, slots // n, width), BF), mem((n, slots // n, width), BF),
            dma((4, 1 + 2 * bits)), dma((4, 1 + 2 * bits)), dma((6, 1 + 2 * bits + n)), dma((6, 1 + 2 * bits + n)), dma((6, 2)),
            dma((4,)), dma((half,)), dma((half,)), dma((half,)), dma((half,)), dma((n,)), dma((n,)),
            dma((2, dp)), dma((2, dp)), dma((2, n)), dma((2, n)),
        ],
        compiler_params=pltpu.CompilerParams(collective_id=2, has_side_effects=True, vmem_limit_bytes=VMEM_LIMIT),
        cost_estimate=pl.CostEstimate(flops=8 << 30, bytes_accessed=48 << 20, transcendentals=4 << 20),
    )(gain1, qkv, kv, text, residual, projected, normed, mixed, totals, dmixed, dtext, early, mi_pieces, mo_pieces,
      image, so_grad, cq_grad, co_grad)


def finish_kernel(slots, out, image_grad, text_grad, early, late, mi, mo, so, cq, co, joint,
                  to_out, to_image, to_text, to_mi, to_mo, to_so, to_cq, to_co, to_qkv, to_kv, to_bias, *to_vectors):
    to_out[...] = out[...]
    to_image[...] = image_grad[...]
    to_text[...] = text_grad[...]
    for source, target in ((mi, to_mi), (mo, to_mo), (so, to_so), (cq, to_cq), (co, to_co)):
        target[...] = source[...].astype(F32)
    for t in range(3):
        to_qkv[t] = joint[t].astype(F32)
    for t in range(2):
        to_kv[:, t, :] = joint[3 + t].astype(F32)
    for t in range(2):
        to_vectors[t][...] = late[t : t + 1, :]
    for t in range(2, 7):
        to_vectors[t][...] = early[t : t + 1, :]
    to_bias[...] = early[7:8, 0 : to_bias.shape[1]]


def finish(out, image_grad, text_grad, early, late, mi, mo, so, cq, co, joint):
    steps = 8
    width, hidden = mi.shape
    local = so.shape[0]

    def cut(value, axis=0):
        shape = list(value.shape)
        shape[axis] //= steps
        return pl.BlockSpec(tuple(shape), lambda i: tuple(i if t == axis else 0 for t in range(len(shape))))

    def whole(shape):
        return pl.BlockSpec(tuple(shape), lambda i: (0,) * len(shape))

    shape = jax.ShapeDtypeStruct
    sums = [shape(value.shape, F32) for value in (mi, mo, so, cq, co)]
    qkv, kv = shape((3, width, local), F32), shape((width, 2, local), F32)
    return pl.pallas_call(
        partial(finish_kernel, steps),
        grid=(steps,),
        out_shape=[shape(out.shape, BF), shape(image_grad.shape, F32), shape(text_grad.shape, F32), *sums, qkv, kv,
                   shape((1, hidden), F32)] + [shape((1, width), F32)] * 7,
        in_specs=[cut(out), cut(image_grad), whole(text_grad.shape), whole(early.shape), whole(late.shape)]
        + [cut(value) for value in (mi, mo, so, cq, co)] + [cut(joint, 1)],
        out_specs=[cut(out), cut(image_grad), whole(text_grad.shape)] + [cut(value) for value in sums]
        + [cut(qkv, 1), cut(kv), whole((1, hidden))] + [whole((1, width))] * 7,
        compiler_params=pltpu.CompilerParams(vmem_limit_bytes=VMEM_LIMIT),
        cost_estimate=pl.CostEstimate(flops=1 << 22, bytes_accessed=28 << 20, transcendentals=0),
    )(out, image_grad, text_grad, early, late, mi, mo, so, cq, co, joint)


def body(sizes, image, text, grad_out, lengths, gain1, shift1, qkv, so, gain2, shift2, cq, kv, co, gain3, shift3, mi,
         in_bias, mo, out_bias):
    n = sizes["mp"]
    image, text, grad_out = image[0], text[0], grad_out[0]
    rows, width = image.shape
    local = so.shape[0]
    sizes = dict(sizes, share=share_of(local, sizes["dp"]))
    qkv, kv = jnp.transpose(qkv, (1, 0, 2)), kv.reshape(width, 2 * local)
    row = lambda value: value[None]
    (projected, normed1, mixed, totals, out, residual, dmixed, dtext, so_grad, cq_grad, co_grad, mi_pieces, mo_pieces,
     early) = layer(
        sizes, image, row(gain1), row(shift1), qkv, text, kv, row(lengths), row(gain2), row(shift2), row(gain3),
        row(shift3), row(in_bias), row(out_bias), so, cq, co, mi, mo, grad_out)
    image_grad, text_grad, early, late, mi_sum, mo_sum, so_sum, cq_sum, co_sum, joint_sum = back(
        sizes, row(gain1), qkv, kv, text, residual, projected, normed1, mixed, totals, dmixed, dtext, early,
        mi_pieces, mo_pieces, image, so_grad, cq_grad, co_grad, mi.shape[1])
    (out, image_grad, text_grad, mi_sum, mo_sum, so_sum, cq_sum, co_sum, qkv_sum, kv_sum, bias_sum, *vectors) = finish(
        out, image_grad, text_grad, early, late, mi_sum, mo_sum, so_sum, cq_sum, co_sum, joint_sum)
    g1, s1, g2, s2, g3, s3, ob = (value[0] for value in vectors)
    return (
        out[None], image_grad[None], text_grad[None], g1, s1, jnp.transpose(qkv_sum, (1, 0, 2)), so_sum, g2, s2, cq_sum,
        kv_sum, co_sum, g3, s3, mi_sum, bias_sum[0], mo_sum, ob,
    )


def solution(mesh):
    rows3, rows2, rows1 = P(None, None, "mp"), P(None, "mp"), P("mp")
    item = P("dp", None, None)
    in_specs = (item, item, item, P("dp"), P(), P(), rows3, P("mp", None), P(), P(), rows2, rows3, P("mp", None), P(), P(),
                rows2, rows1, P("mp", None), P())
    split = P("dp", "mp", None)
    out_specs = (split, split, split, P(), P(), rows3, P("mp", None), P(), P(), rows2, rows3, P("mp", None), P(), P(),
                 rows2, rows1, P("mp", None), P())
    sizes = dict(mesh.shape)
    return jax.shard_map(partial(body, sizes), mesh=mesh, in_specs=in_specs, out_specs=out_specs, check_vma=False)
```

```python
from functools import partial

import jax
import jax.numpy as jnp
from jax import lax
from jax.experimental import pallas as pl
from jax.experimental.pallas import tpu as pltpu
from jax.sharding import PartitionSpec as P

HEAD_DIM = 64
PAIR = 2 * HEAD_DIM
EPSILON = 1e-05
SCALE = HEAD_DIM ** (-0.5)
MASKED = -1e30
BF = jnp.bfloat16
F32 = jnp.float32
MESH = pl.DeviceIdType.MESH
VMEM_LIMIT = 60 << 20


def nn(a, b):
    return lax.dot_general(a, b, (((1,), (0,)), ((), ())), preferred_element_type=F32)


def nt(a, b):
    return lax.dot_general(a, b, (((1,), (1,)), ((), ())), preferred_element_type=F32)


def tn(a, b):
    return lax.dot_general(a, b, (((0,), (0,)), ((), ())), preferred_element_type=F32)


def norm_parts(value):
    center = value - jnp.mean(value, axis=-1, keepdims=True)
    inverse = lax.rsqrt(jnp.mean(center * center, axis=-1, keepdims=True) + EPSILON)
    return center * inverse, inverse


def half_masks():
    lane = lax.broadcasted_iota(jnp.int32, (1, PAIR), 1)
    first = jnp.where(lane < HEAD_DIM, 1.0, 0.0)
    return first, 1.0 - first


def stack_heads(pair, scale=None):
    first, second = half_masks()
    if scale is not None:
        first, second = first * scale, second * scale
    wide = pair.astype(F32)
    return jnp.concatenate([wide * first, wide * second], axis=0).astype(BF)


def fold_heads(stacked):
    rows = stacked.shape[1] // 2
    both = jnp.concatenate([stacked[:HEAD_DIM, :rows], stacked[HEAD_DIM:, rows:]], axis=0)
    return both.T


def causal(tile_keys, tile_rows):
    key = lax.broadcasted_iota(jnp.int32, (tile_keys, tile_rows), 0)
    row = lax.broadcasted_iota(jnp.int32, (tile_keys, tile_rows), 1)
    both = key <= row
    return jnp.concatenate([both, both], axis=1)


class Place:
    def __init__(self, sizes):
        self.n = sizes["mp"]
        self.dp = sizes["dp"]
        self.share = sizes["share"]
        self.d = lax.axis_index("dp")
        self.m = lax.axis_index("mp")
        self.core = lax.rem(self.d, 2)
        self.mate = self.m + 1 - 2 * lax.rem(self.m, 2)
        self.partner = (self.d + 1 - 2 * self.core, self.m)
        self.member = lax.rem(self.d, self.share)
        self.chip = self.member // 2
        self.base = self.d - self.member
        self.piece = self.core * (self.share // 2) + self.chip

    def along(self, offset):
        return lax.rem(self.m + offset, self.n)

    def mate_along(self, offset):
        return lax.rem(self.mate + offset, self.n)

    def peer(self, offset):
        return (self.d, self.along(offset))

    def chip_peer(self, offset):
        chip = lax.rem(self.chip + offset, self.share // 2)
        return (self.base + 2 * chip + self.core, self.m), self.core * (self.share // 2) + chip


def greet(devices):
    for device in devices:
        pl.semaphore_signal(pltpu.get_barrier_semaphore(), inc=1, device_id=device, device_id_type=MESH)


def meet(devices):
    pl.semaphore_wait(pltpu.get_barrier_semaphore(), len(devices))


class Gather:
    def __init__(self, place, own, full, everyone, slot_of, sems):
        self.place, self.own, self.full, self.slot_of = place, own, full, slot_of
        self.count = own.shape[0] // place.share
        self.sems = sems
        self.even = list(range(2, place.n, 2))
        self.sources = [place.along(place.n - k) for k in self.even]
        if everyone:
            self.sources.append(place.mate)
            self.sources += [place.mate_along(place.n - k) for k in self.even]
        self.everyone = everyone

    def rows_of(self, slot, piece, pieces=1):
        start = pl.multiple_of(piece * self.count, self.count)
        return self.full.at[slot, pl.ds(start, pieces * self.count), :]

    def copy(self, src, dst, index, hop, device):
        return pltpu.make_async_remote_copy(
            src_ref=src, dst_ref=dst, send_sem=self.sems[0].at[index, hop], recv_sem=self.sems[1].at[index, hop],
            device_id=device, device_id_type=MESH,
        )

    def first(self, index):
        place, parity = self.place, len(self.even)
        mine = self.own.at[pl.ds(pl.multiple_of(place.piece * self.count, self.count), self.count), :]
        slot = self.slot_of(place.m)
        if index < parity:
            device = place.peer(self.even[index])
        else:
            device = (place.d, place.mate)
        if index > parity:
            slot = self.slot_of(self.sources[index - parity - 1])
            mine = self.rows_of(slot, place.piece)
        return self.copy(mine, self.rows_of(slot, place.piece), index, 0, device)

    def second(self, index, hop):
        block = self.rows_of(self.slot_of(self.sources[index]), self.place.piece)
        return self.copy(block, block, index, hop, self.place.chip_peer(hop)[0])

    def third(self, index):
        half = self.place.share // 2
        block = self.rows_of(self.slot_of(self.sources[index]), self.place.core * half, half)
        return self.copy(block, block, index, half, self.place.partner)

    def local(self):
        return pltpu.make_async_copy(self.own, self.full.at[self.slot_of(self.place.m)], self.sems[2])

    def step(self, number):
        hops = range(1, self.place.share // 2)
        parity = len(self.even)
        everything = range(len(self.sources))
        if number == 0:
            for index in everything:
                if index <= parity:
                    self.first(index).start()
        elif number == 1:
            for index in range(parity):
                self.first(index).wait_recv()
                if self.everyone:
                    self.first(parity + 1 + index).start()
                for hop in hops:
                    self.second(index, hop).start()
        elif number == 2:
            for index in everything[parity:]:
                self.first(index).wait_recv()
                for hop in hops:
                    self.second(index, hop).start()
        elif number == 3:
            for index in everything:
                for hop in hops:
                    self.second(index, hop).wait_recv()
                self.third(index).start()
        else:
            for index in everything:
                self.third(index).wait()
                self.first(index).wait_send()
                for hop in hops:
                    self.second(index, hop).wait_send()

    def finish(self):
        self.step(4)
        self.local().wait()


def attend_block(projected, mixed, totals, i, hp, size, local):
    rows = pl.ds(pl.multiple_of(i * size, size), size)
    column = pl.multiple_of(hp * PAIR, PAIR)
    query = stack_heads(projected[rows, pl.ds(column, PAIR)], SCALE)

    def tile(j, carry, diagonal):
        largest, total, acc = carry
        keys = pl.ds(pl.multiple_of(j * size, size), size)
        key = projected[keys, pl.ds(column + local, PAIR)]
        value = projected[keys, pl.ds(column + 2 * local, PAIR)]
        scores = nt(key, query)
        if diagonal:
            scores = jnp.where(causal(size, size), scores, MASKED)
        top = jnp.maximum(largest, jnp.max(scores, axis=0, keepdims=True))
        powers = jnp.exp(scores - top)
        shrink = jnp.exp(largest - top)
        total = total * shrink + jnp.sum(powers, axis=0, keepdims=True)
        acc = acc * shrink + tn(value, powers.astype(BF))
        return top, total, acc

    carry = (
        jnp.full((1, 2 * size), MASKED, F32),
        jnp.zeros((1, 2 * size), F32),
        jnp.zeros((PAIR, 2 * size), F32),
    )
    carry = tile(i, carry, True)
    largest, total, acc = lax.fori_loop(0, i, lambda j, c: tile(j, c, False), carry)
    mixed[rows, pl.ds(column, PAIR)] = fold_heads(acc / total).astype(BF)
    totals[hp, i] = largest + jnp.log(total)


def share_of(local, dp):
    share = dp
    while (local // share) % 16:
        share //= 2
    return share


def halvings(rows, bits):
    left = [rows // 4]
    for _ in range(bits):
        left.append(left[-1] // 2 if left[-1] % 32 == 0 else left[-1])
    return left


def arrivals(rows, bits):
    left = halvings(rows, bits)
    return left[1:]


class Rows:
    def __init__(self, place, rows):
        self.place = place
        self.half = rows // 2
        self.bits = (place.dp // 2).bit_length() - 1
        self.left = halvings(rows, self.bits)
        self.count = self.left[-1]
        self.chip = place.d // 2

    def bit(self, p, k):
        b = k if p == 0 else self.bits - 1 - k
        value = lax.rem(self.chip // (1 << b), 2)
        chip = self.chip + (1 - 2 * value) * (1 << b)
        return value, (2 * chip + self.place.core, self.place.m)

    def cut(self, k):
        return self.left[k + 1] < self.left[k]

    def region(self, p, k):
        start = self.place.core * self.half + p * self.left[0]
        for t in range(k):
            if self.cut(t):
                start = start + self.bit(p, t)[0] * self.left[t + 1]
        return start

    def span(self, start, count):
        return pl.ds(pl.multiple_of(start, 16), count)


class Reduce:
    def __init__(self, place, ref, recv, pieces, sems):
        self.place, self.ref, self.recv, self.pieces = place, ref, recv, pieces
        self.rows = Rows(place, ref.shape[1])
        self.send, self.recv_sem = sems

    def copy(self, src, dst, index, device):
        return pltpu.make_async_remote_copy(
            src_ref=src, dst_ref=dst, send_sem=self.send.at[index], recv_sem=self.recv_sem.at[index],
            device_id=device, device_id_type=MESH,
        )

    def core_copy(self):
        half = self.rows.half
        away = self.rows.span((1 - self.place.core) * half, half)
        return self.copy(self.ref.at[:, away, :], self.recv.at[:, pl.ds(0, half), :], 0, self.place.partner)

    def offset(self, p, k):
        into = self.rows.left[1:]
        return self.rows.half + p * sum(into) + sum(into[:k])

    def chip_copy(self, p, k):
        rows = self.rows
        value, device = rows.bit(p, k)
        count = rows.left[k + 1]
        start = rows.region(p, k)
        if rows.cut(k):
            start = start + (1 - value) * count
        return self.copy(
            self.ref.at[:, rows.span(start, count), :], self.recv.at[:, pl.ds(self.offset(p, k), count), :],
            1 + p * rows.bits + k, device)

    def add(self, start, offset, count, target, target_start):
        chunk = min(32, count)
        span = self.rows.span

        def run(t, _):
            at = t * chunk
            for s in range(self.ref.shape[0]):
                mine = self.ref[s, span(start + at, chunk), :].astype(F32)
                theirs = self.recv[s, span(offset + at, chunk), :].astype(F32)
                target[s, span(target_start + at, chunk), :] = (mine + theirs).astype(BF)
            return 0

        lax.fori_loop(0, count // chunk, run, 0)

    def phases(self):
        rows = self.rows

        def begin():
            self.core_copy().start()

        def core_sum():
            self.core_copy().wait()
            self.add(self.place.core * rows.half, 0, rows.half, self.ref, self.place.core * rows.half)
            for p in range(2):
                self.chip_copy(p, 0).start()

        def chip_sum(k):
            last = k == rows.bits - 1
            for p in range(2):
                self.chip_copy(p, k).wait()
                start = rows.region(p, k + 1)
                self.add(start, self.offset(p, k), rows.left[k + 1], self.pieces if last else self.ref,
                         p * rows.count if last else start)
                if not last:
                    self.chip_copy(p, k + 1).start()

        return [begin, core_sum] + [partial(chip_sum, k) for k in range(rows.bits)]


class Spread:
    def __init__(self, place, rows, pieces, other, final, whole, rule, sems):
        self.place, self.pieces, self.other, self.final, self.whole = place, pieces, other, final, whole
        self.rows = Rows(place, rows)
        self.rule, (self.send, self.recv_sem, self.keep) = rule, sems
        if rule == "all":
            self.hops = [(k, place.along(k)) for k in range(1, place.n)]
            self.slot = place.m
        elif rule == "parity":
            half = place.n // 2
            self.hops = [(2 * k, lax.rem(place.m // 2 + k, half)) for k in range(1, half)]
            self.slot = place.m // 2
        else:
            self.hops, self.slot = [], 0

    def copy(self, src, dst, index, device):
        return pltpu.make_async_remote_copy(
            src_ref=src, dst_ref=dst, send_sem=self.send.at[index], recv_sem=self.recv_sem.at[index],
            device_id=device, device_id_type=MESH,
        )

    def far_copy(self, index):
        hop, slot = self.hops[index]
        return self.copy(self.pieces.at[slot], self.other.at[self.slot], 1 + 2 * self.rows.bits + index, self.place.peer(hop))

    def view(self, ref, start, count):
        span = self.rows.span(start, count)
        return ref.at[:, span, :] if self.rule == "own" else ref.at[span, :]

    def spread_copy(self, p, k):
        rows = self.rows
        count = rows.left[k + 1]
        block = self.view(self.whole, rows.region(p, k + 1), count)
        first = not any(rows.cut(t) for t in range(k + 1, rows.bits))
        src = self.view(self.final, p * rows.count, rows.count) if first else block
        return self.copy(src, block, 1 + p * rows.bits + k, rows.bit(p, k)[1])

    def keep_copy(self, p):
        rows = self.rows
        block = self.view(self.whole, rows.region(p, rows.bits), rows.count)
        return pltpu.make_async_copy(self.view(self.final, p * rows.count, rows.count), block, self.keep.at[p])

    def core_spread(self):
        half = self.rows.half
        block = self.view(self.whole, self.place.core * half, half)
        return self.copy(block, block, 0, self.place.partner)

    def phases(self):
        rows = self.rows
        cuts = [k for k in reversed(range(rows.bits)) if rows.cut(k)]

        def far():
            for index in range(len(self.hops)):
                self.far_copy(index).start()

        def far_sum():
            if self.hops:
                total = self.pieces[self.slot].astype(F32)
                for index, (hop, _) in enumerate(self.hops):
                    self.far_copy(index).wait()
                    source = self.place.along(self.place.n - hop)
                    total += self.other[source if self.rule == "all" else source // 2].astype(F32)
                self.final[...] = total.astype(BF)
            for p in range(2):
                self.keep_copy(p).start()
                self.spread_copy(p, cuts[0]).start()
            for p in range(2):
                self.keep_copy(p).wait()

        def spread(t):
            for p in range(2):
                self.spread_copy(p, cuts[t]).wait()
                if t + 1 < len(cuts):
                    self.spread_copy(p, cuts[t + 1]).start()
            if t + 1 == len(cuts):
                self.core_spread().start()

        def end():
            self.core_spread().wait()

        nothing = [lambda: None] * (rows.bits - len(cuts))
        return [far, far_sum] + [partial(spread, t) for t in range(len(cuts))] + nothing + [end]


def recv_space(count, rows, columns, bits):
    return pltpu.VMEM((count, rows // 2 + 2 * sum(arrivals(rows, bits)), columns), BF)


def piece_shape(count, rows, columns, bits):
    return jax.ShapeDtypeStruct((count, 2 * halvings(rows, bits)[-1], columns), BF)


def norm_back(grad, normal, inverse, gain):
    scaled = grad * gain
    return inverse * (
        scaled
        - jnp.mean(scaled, axis=-1, keepdims=True)
        - normal * jnp.mean(scaled * normal, axis=-1, keepdims=True)
    )


def add_rows(ref, index, value):
    ref[pl.ds(index, 1), :] += jnp.sum(value, axis=0, keepdims=True)


def in_chunks(total, chunk, step):
    def run(i, _):
        step(pl.ds(pl.multiple_of(i * chunk, chunk), chunk))
        return 0

    lax.fori_loop(0, total // chunk, run, 0)


def cross_pair(query, text_proj, length, idx, local):
    per = local // PAIR
    g, hp = idx // per, lax.rem(idx, per)
    near = pl.multiple_of(hp * PAIR, PAIR)
    column = pl.multiple_of(idx * PAIR, PAIR)
    stacked = stack_heads(query[:, pl.ds(column, PAIR)], SCALE)
    key = text_proj[g, :, pl.ds(near, PAIR)]
    value = text_proj[g, :, pl.ds(near + local, PAIR)]
    scores = nt(key, stacked)
    slot = lax.broadcasted_iota(jnp.int32, scores.shape, 0)
    return g, near, column, stacked, key, value, jnp.where(slot < length, scores, MASKED)


ROWS_AT_ONCE = 32


def layer_kernel(
    sizes,
    image, gain1, shift1, qkv, text, kv, length, gain2, shift2, gain3, shift3, in_bias, out_bias,
    so, cq, co, mi, mo, grad_out,
    projected, normed, mixed, totals, out, residual, dmixed, dtext, so_grad, cq_grad, co_grad, mi_pieces, mo_pieces,
    vectors,
    mixed_rows, text_proj, so_full, cq_full, co_full, mi_full, mo_full, bias_full,
    grad_pair, mixed_all, first, second, work, grad2, out_part,
    n2, query, cross, cross_totals, dquery, n3_pair, active, dhidden,
    dn3_send, dn3_recv, out_send, out_recv, r2, dcross, r1, dmixed_send, dtext_send, dtext_recv,
    text_own, mi_recv, mo_recv, small_send, small_recv, small_own, wide_send, wide_recv, wide_own,
    mix_send, mix_recv, mix_own, text_send, text_recv, bias_send, bias_recv, load_sem,
    pair_send, pair_recv, dmix_send, dmix_recv, dtext_ssem, dtext_rsem, store_sem, reduce_send, reduce_recv,
):
    place = Place(sizes)
    n, share = place.n, place.share
    rows, width = image.shape
    size = rows // n
    local, hidden = so.shape[0], mi.shape[1]
    half = n // 2
    offsets = list(range(1, n))
    mate = (place.d, place.mate)
    mine = place.m // 2
    chips = place.dp // 2
    partners = [place.peer(k) for k in offsets] + [place.partner]
    partners += [(2 * lax.rem(place.d // 2 + k, chips) + place.core, place.m) for k in range(1, chips)]
    greet(partners)
    meet(partners)

    def remote(src, dst, send, recv, device):
        return pltpu.make_async_remote_copy(
            src_ref=src, dst_ref=dst, send_sem=send, recv_sem=recv, device_id=device, device_id_type=MESH
        )

    small = [
        Gather(place, own, full, True, lambda s: s, (small_send.at[t], small_recv.at[t], small_own.at[t]))
        for t, (own, full) in enumerate(((so, so_full), (cq, cq_full), (co, co_full)))
    ]
    wide = [
        Gather(place, own, full, False, lambda s: s // 2, (wide_send.at[t], wide_recv.at[t], wide_own.at[t]))
        for t, (own, full) in enumerate(((mi, mi_full), (mo, mo_full)))
    ]
    for item in small:
        item.step(0)
    for item in small + wide:
        item.local().start()
    wide[0].step(0)

    def block_of(index):
        return pl.ds(pl.multiple_of(index * size, size), size)

    own_rows = block_of(place.m)
    loads = [
        pltpu.make_async_copy(grad_out.at[own_rows, :], grad_pair.at[0], load_sem.at[0]),
        pltpu.make_async_copy(grad_out.at[block_of(mate[1]), :], grad_pair.at[1], load_sem.at[1]),
    ]
    for load in loads:
        load.start()
    bias_full[mine] = in_bias[...]

    def bias_copy(k):
        return remote(in_bias, bias_full.at[mine], bias_send.at[k], bias_recv.at[k], place.peer(2 * k))

    for k in range(1, half):
        bias_copy(k).start()

    def project(i, _):
        block = block_of(i)

        def norm(chunk):
            at = pl.ds(pl.multiple_of(i * size + chunk.start, ROWS_AT_ONCE), ROWS_AT_ONCE)
            normal, _ = norm_parts(image[at, :].astype(F32))
            normed[at, :] = (normal * gain1[...] + shift1[...]).astype(BF)

        in_chunks(size, ROWS_AT_ONCE, norm)
        for t in range(3):
            projected[block, t * local : (t + 1) * local] = nn(normed[block, :], qkv[t]).astype(BF)
        return 0

    lax.fori_loop(0, n, project, 0)
    text_own[...] = nn(text[...], kv[...]).astype(BF)
    text_proj[place.m] = text_own[...]

    even = list(range(2, n, 2))

    def text_copy(k):
        return remote(text_own, text_proj.at[place.m], text_send.at[k], text_recv.at[k], place.peer(k) if k else mate)

    def text_pass(k):
        block = text_proj.at[place.along(n - k)]
        return remote(block, block, text_send.at[k + 1], text_recv.at[k + 1], mate)

    for k in [0] + even:
        text_copy(k).start()

    def mix_copy(i):
        gap = lax.rem(i - place.m + n, n)
        return remote(mixed.at[block_of(i), :], mixed_rows.at[place.m], mix_send.at[gap], mix_recv.at[gap], (place.d, i))

    mix_keep = pltpu.make_async_copy(mixed.at[own_rows, :], mixed_rows.at[place.m], mix_own)
    for item in small:
        item.step(1)
    plan = [[] for _ in range(n)]
    plan[1] = [small[0]]
    plan[2] = [small[1]]
    plan[n - 1] += [small[2]]
    for i in range(n):
        lax.fori_loop(0, local // PAIR, lambda hp, _: (attend_block(projected, mixed, totals, i, hp, size, local), 0)[1], 0)

        @pl.when(place.m != i)
        def _():
            mix_copy(i).start()

        @pl.when(place.m == i)
        def _():
            mix_keep.start()

        for item in plan[i]:
            item.step(2)

    wide[1].step(0)
    for k in even:
        text_copy(k).wait_recv()
        text_pass(k).start()
    small[0].step(3)

    for k in offsets:
        mix_copy(place.along(k)).wait()
    mix_keep.wait()
    small[0].finish()
    small[1].step(3)
    for g in range(n):
        mixed_all[:, g * local : (g + 1) * local] = mixed_rows[g]
    first[...] = nn(mixed_all[...], so_full[...].reshape(n * local, width))

    def first_norm(chunk):
        at = pl.ds(pl.multiple_of(place.m * size + chunk.start, ROWS_AT_ONCE), ROWS_AT_ONCE)
        value = image[at, :].astype(F32) + first[chunk, :]
        first[chunk, :] = value
        n2[chunk, :] = (norm_parts(value)[0] * gain2[...] + shift2[...]).astype(BF)

    in_chunks(size, ROWS_AT_ONCE, first_norm)
    small[1].finish()
    small[2].step(3)
    for g in range(n):
        query[:, g * local : (g + 1) * local] = nn(n2[...], cq_full[g]).astype(BF)
    text_copy(0).wait()
    for k in even:
        text_copy(k).wait_send()
        text_pass(k).wait()
    for item in wide:
        item.step(1)
    limit = length[0, 0]
    all_pairs = n * local // PAIR

    def cross_forward(idx, _):
        g, near, column, stacked, key, value, scores = cross_pair(query, text_proj, limit, idx, local)
        largest = jnp.max(scores, axis=0, keepdims=True)
        powers = jnp.exp(scores - largest)
        total = jnp.sum(powers, axis=0, keepdims=True)
        cross_totals[idx] = largest + jnp.log(total)
        cross[:, pl.ds(column, PAIR)] = fold_heads(tn(value, (powers / total).astype(BF))).astype(BF)
        return 0

    lax.fori_loop(0, all_pairs, cross_forward, 0)
    small[2].finish()
    second[...] = nn(cross[...], co_full[...].reshape(n * local, width))

    def second_norm(chunk):
        value = first[chunk, :] + second[chunk, :]
        second[chunk, :] = value
        n3_pair[0, chunk, :] = (norm_parts(value)[0] * gain3[...] + shift3[...]).astype(BF)

    in_chunks(size, ROWS_AT_ONCE, second_norm)

    n3_copy = remote(n3_pair.at[0], n3_pair.at[1], pair_send.at[0], pair_recv.at[0], mate)
    n3_copy.start()
    for load in loads:
        load.wait()
    for k in range(1, half):
        bias_copy(k).wait()
    for item in wide:
        item.local().wait()
    step = min(256, hidden)

    def feed(p, slot):
        grads = grad_pair[p]

        def chunk(c, _):
            columns = pl.ds(pl.multiple_of(c * step, step), step)
            value = nn(n3_pair[p], mi_full[slot, :, columns]) + bias_full[slot, :, columns]
            inner = 0.5 * (1.0 + lax.erf(value * (0.5**0.5)))
            slope = inner + value * jnp.exp(-0.5 * value * value) * ((2.0 * jnp.pi) ** -0.5)
            active[slot, p, :, columns] = (value * inner).astype(BF)
            dhidden[slot, p, :, columns] = (nt(grads, mo_full[slot, columns, :]) * slope).astype(BF)
            return 0

        lax.fori_loop(0, hidden // step, chunk, 0)

    def sum_slots(term):
        total = term(0)
        for slot in range(1, half):
            total += term(slot)
        return total

    feed(0, mine)
    for item in wide:
        item.step(3)
    n3_copy.wait()
    feed(1, mine)
    for item in wide:
        item.step(4)
    others = [lax.rem(mine + k, half) for k in range(1, half)]
    for slot in others:
        feed(1, slot)
    dn3_send[...] = sum_slots(lambda slot: nt(dhidden[slot, 1], mi_full[slot])).astype(BF)
    dn3_copy = remote(dn3_send, dn3_recv, pair_send.at[1], pair_recv.at[1], mate)
    dn3_copy.start()
    out_send[...] = sum_slots(lambda slot: nn(active[slot, 1], mo_full[slot])).astype(BF)
    out_copy = remote(out_send, out_recv, pair_send.at[2], pair_recv.at[2], mate)
    out_copy.start()
    for slot in others:
        feed(0, slot)
    work[...] = sum_slots(lambda slot: nt(dhidden[slot, 0], mi_full[slot]))
    out_part[...] = sum_slots(lambda slot: nn(active[slot, 0], mo_full[slot]))
    tile = min(256, width)

    def wide_grads(slot):
        inner = n3_pair.shape[0] * size
        hidden_grad = dhidden[slot].reshape(inner, hidden)
        grads = grad_pair[...].reshape(inner, width)
        vectors[8 + slot : 9 + slot, 0:hidden] = jnp.sum(hidden_grad.astype(F32), axis=0, keepdims=True)

        def into(t, _):
            at = pl.ds(pl.multiple_of(t * tile, tile), tile)
            mi_full[slot, at, :] = tn(n3_pair[:, :, at].reshape(inner, tile), hidden_grad).astype(BF)
            return 0

        lax.fori_loop(0, width // tile, into, 0)

        def back(t, _):
            at = pl.ds(pl.multiple_of(t * step, step), step)
            mo_full[slot, at, :] = tn(active[slot, :, :, at].reshape(inner, step), grads).astype(BF)
            return 0

        lax.fori_loop(0, hidden // step, back, 0)

    vectors[...] = jnp.zeros_like(vectors)
    for slot in range(half):
        wide_grads(slot)
    mi_steps = Reduce(place, mi_full, mi_recv, mi_pieces, (reduce_send.at[0], reduce_recv.at[0])).phases()
    mo_steps = Reduce(place, mo_full, mo_recv, mo_pieces, (reduce_send.at[1], reduce_recv.at[1])).phases()
    wide_steps = [step for pair in zip(mi_steps, mo_steps) for step in pair]
    for run in wide_steps[:2]:
        run()
    dn3_copy.wait()


    def third_back(chunk):
        grad = work[chunk, :] + dn3_recv[chunk, :].astype(F32)
        normal, inverse = norm_parts(second[chunk, :])
        above = grad_pair[0, chunk, :].astype(F32)
        add_rows(vectors, 4, grad * normal)
        add_rows(vectors, 5, grad)
        add_rows(vectors, 6, above)
        value = above + norm_back(grad, normal, inverse, gain3[...])
        work[chunk, :] = value
        r2[chunk, :] = value.astype(BF)

    in_chunks(size, ROWS_AT_ONCE, third_back)
    wide_steps[2]()
    dcross[...] = nt(r2[...], co_full[...].reshape(n * local, width)).astype(BF)

    def cross_back(idx, _):
        g, near, column, stacked, key, value, scores = cross_pair(query, text_proj, limit, idx, local)
        weights = jnp.exp(scores - cross_totals[idx])
        above = stack_heads(dcross[:, pl.ds(column, PAIR)])
        dweights = nt(value, above)
        dscores = (weights * (dweights - jnp.sum(weights * dweights, axis=0, keepdims=True))).astype(BF)
        dquery[:, pl.ds(column, PAIR)] = (fold_heads(tn(key, dscores)) * SCALE).astype(BF)
        dtext_send[g, :, pl.ds(near, PAIR)] = nn(dscores, stacked).astype(BF)
        dtext_send[g, :, pl.ds(near + local, PAIR)] = nn(weights.astype(BF), above).astype(BF)
        return 0

    lax.fori_loop(0, all_pairs, cross_back, 0)
    wide_steps[3]()

    def dtext_copy(k):
        return remote(dtext_send.at[place.along(k)], dtext_recv.at[place.m], dtext_ssem.at[k], dtext_rsem.at[k], place.peer(k))

    for k in offsets:
        dtext_copy(k).start()
    def both(term):
        total = term(0)
        for g in range(1, n):
            total += term(g)
        return total

    grad2[...] = both(lambda g: nt(dquery[:, g * local : (g + 1) * local], cq_full[g]))

    def second_back(chunk):
        grad = grad2[chunk, :]
        normal, inverse = norm_parts(first[chunk, :])
        add_rows(vectors, 2, grad * normal)
        add_rows(vectors, 3, grad)
        value = work[chunk, :] + norm_back(grad, normal, inverse, gain2[...])
        residual[chunk, :] = value
        r1[chunk, :] = value.astype(BF)

    in_chunks(size, ROWS_AT_ONCE, second_back)

    def dmix_copy(k):
        return remote(dmixed_send.at[k], dmixed.at[own_rows, :], dmix_send.at[k], dmix_recv.at[k], place.peer(k))

    for k in offsets:
        dmixed_send[k] = nt(r1[...], so_full[place.along(k)]).astype(BF)
        dmix_copy(k).start()
    dmixed[own_rows, :] = nt(r1[...], so_full[place.m]).astype(BF)
    wide_steps[4]()

    stores = []

    def small_grad(left, right, keep, target, index):
        for g in range(n):
            heads = slice(g * local, (g + 1) * local)
            if keep.shape[1] == local:
                keep[g] = tn(left[:, heads], right[...]).astype(BF)
            else:
                keep[g] = tn(left[...], right[:, heads]).astype(BF)
        copy = pltpu.make_async_copy(keep, target, store_sem.at[index])
        copy.start()
        stores.append(copy)

    small_grad(n2, dquery, cq_full, cq_grad, 0)
    small_grad(mixed_all, r1, so_full, so_grad, 1)
    small_grad(cross, r2, co_full, co_grad, 2)

    wide_steps[5]()
    out_copy.wait()

    def finish_out(chunk):
        value = second[chunk, :] + out_part[chunk, :] + out_recv[chunk, :].astype(F32) + out_bias[...]
        out[chunk, :] = value.astype(BF)

    in_chunks(size, ROWS_AT_ONCE, finish_out)
    for run in wide_steps[6:]:
        run()
    for k in offsets:
        dtext_copy(k).wait()
    total = dtext_send[place.m].astype(F32)
    for k in offsets:
        total += dtext_recv[place.along(k)].astype(F32)
    dtext[...] = total.astype(BF)
    for k in offsets:
        dmix_copy(k).wait()
    for store in stores:
        store.wait()


def layer(sizes, image, gain1, shift1, qkv, text, kv, length, gain2, shift2, gain3, shift3, in_bias, out_bias,
          so, cq, co, mi, mo, grad_out):
    n, share = sizes["mp"], sizes["share"]
    rows, width = image.shape
    slots = text.shape[0]
    local, hidden = so.shape[0], mi.shape[1]
    size = rows // n
    pairs = local // PAIR
    hops = share // 2 + 1
    half = n // 2
    vmem, hbm = pl.BlockSpec(memory_space=pltpu.VMEM), pl.BlockSpec(memory_space=pl.ANY)
    dma, mem = pltpu.SemaphoreType.DMA, pltpu.VMEM
    shape = jax.ShapeDtypeStruct
    few = max(half - 1, 1)
    bits = (sizes["dp"] // 2).bit_length() - 1
    return pl.pallas_call(
        partial(layer_kernel, sizes),
        out_shape=[
            shape((rows, 3 * local), BF), shape((rows, width), BF), shape((rows, local), BF),
            shape((pairs, n, 1, 2 * size), F32), shape((size, width), BF), shape((size, width), F32),
            shape((rows, local), BF), shape((slots, 2 * local), BF),
            shape((n, local, width), BF), shape((n, width, local), BF), shape((n, local, width), BF),
            piece_shape(half, width, hidden, bits), piece_shape(half, hidden, width, bits),
            shape((8 + -(-half // 8) * 8, width), F32),
        ],
        in_specs=[vmem] * 6 + [pl.BlockSpec(memory_space=pltpu.SMEM)] + [vmem] * 6 + [hbm] * 6,
        out_specs=[vmem] * 8 + [hbm] * 3 + [vmem] * 3,
        scratch_shapes=[
            mem((n, size, local), BF), mem((n, slots, 2 * local), BF),
            mem((n, local, width), BF), mem((n, width, local), BF), mem((n, local, width), BF),
            mem((half, width, hidden), BF), mem((half, hidden, width), BF), mem((half, 1, hidden), F32),
            mem((2, size, width), BF), mem((size, n * local), BF),
            mem((size, width), F32), mem((size, width), F32), mem((size, width), F32), mem((size, width), F32),
            mem((size, width), F32),
            mem((size, width), BF), mem((size, n * local), BF), mem((size, n * local), BF),
            mem((n * pairs, 1, 2 * size), F32), mem((size, n * local), BF),
            mem((2, size, width), BF), mem((half, 2, size, hidden), BF), mem((half, 2, size, hidden), BF),
            mem((size, width), BF), mem((size, width), BF), mem((size, width), BF), mem((size, width), BF),
            mem((size, width), BF), mem((size, n * local), BF), mem((size, width), BF),
            mem((n, size, local), BF), mem((n, slots, 2 * local), BF), mem((n, slots, 2 * local), BF),
            mem((slots, 2 * local), BF), recv_space(half, width, hidden, bits), recv_space(half, hidden, width, bits),
            dma((3, n - 1, hops)), dma((3, n - 1, hops)), dma((3,)),
            dma((2, few, hops)), dma((2, few, hops)), dma((2,)),
            dma((n,)), dma((n,)), dma(()),
            dma((n + 1,)), dma((n + 1,)), dma((half,)), dma((half,)), dma((2,)),
            dma((3,)), dma((3,)), dma((n,)), dma((n,)), dma((n,)), dma((n,)), dma((3,)), dma((2, 1 + 2 * bits)), dma((2, 1 + 2 * bits)),
        ],
        compiler_params=pltpu.CompilerParams(collective_id=1, has_side_effects=True, vmem_limit_bytes=VMEM_LIMIT),
        cost_estimate=pl.CostEstimate(flops=22 << 30, bytes_accessed=48 << 20, transcendentals=8 << 20),
    )(image, gain1, shift1, qkv, text, kv, length, gain2, shift2, gain3, shift3, in_bias, out_bias,
      so, cq, co, mi, mo, grad_out)


def back_kernel(
    sizes,
    gain1, qkv, kv, text, residual, projected, normed, mixed, totals, dmixed, dtext, early, mi_pieces, mo_pieces,
    image, so_grad, cq_grad, co_grad,
    image_grad, text_grad, early_out, late_out, mi_out, mo_out, so_out, cq_out, co_out, joint_out,
    image_rows, stacked, above, delta, dquery, dprojected,
    near_hold, near_send, near_recv, far_send, far_recv, dn1_own,
    mi_other, mi_final, mo_other, mo_final,
    so_ref, so_recv, so_pieces, so_other, so_final, cq_ref, cq_recv, cq_pieces, cq_other, cq_final,
    co_ref, co_recv, co_pieces, co_other, co_final, joint_ref, joint_recv, joint_pieces,
    early_dp, early_mp, early_own, late, late_dp, late_mp, late_own, text_send, text_recv,
    reduce_send, reduce_recv, spread_send, spread_recv, spread_keep, load_sem,
    near_ssem, near_rsem, far_ssem, far_rsem, text_ssem, text_rsem, vec_ssem, vec_rsem, vec_zsend, vec_zrecv,
):
    place = Place(sizes)
    n, dp = place.n, place.dp
    rows, width = normed.shape
    local = mixed.shape[1]
    size = rows // n
    half = n // 2
    pairs = local // PAIR
    offsets = list(range(1, n))
    everyone = [lax.rem(place.d + k, dp) for k in range(1, dp)]
    partners = [place.peer(k) for k in offsets] + [(device, place.m) for device in everyone]
    greet(partners)

    def remote(src, dst, send, recv, device):
        return pltpu.make_async_remote_copy(
            src_ref=src, dst_ref=dst, send_sem=send, recv_sem=recv, device_id=device, device_id_type=MESH
        )

    def block_of(index):
        return pl.ds(pl.multiple_of(index * size, size), size)

    loads = [
        pltpu.make_async_copy(src, dst, load_sem.at[t])
        for t, (src, dst) in enumerate((
            (so_grad, so_ref), (cq_grad, cq_ref), (co_grad, co_ref), (image.at[block_of(place.m), :], image_rows),
        ))
    ]
    for load in loads:
        load.start()

    def reduce(t, ref, recv, pieces):
        return Reduce(place, ref, recv, pieces, (reduce_send.at[t], reduce_recv.at[t])).phases()

    def spread(t, rows, pieces, other, final, whole, rule):
        sems = (spread_send.at[t], spread_recv.at[t], spread_keep.at[t])
        return Spread(place, rows, pieces, other, final, whole, rule, sems).phases()

    mi_steps = spread(0, width, mi_pieces, mi_other, mi_final, mi_out, "parity")
    mo_steps = spread(1, mo_out.shape[0], mo_pieces, mo_other, mo_final, mo_out, "parity")
    so_steps = reduce(0, so_ref, so_recv, so_pieces) + spread(2, local, so_pieces, so_other, so_final, so_out, "all")
    cq_steps = reduce(1, cq_ref, cq_recv, cq_pieces) + spread(3, width, cq_pieces, cq_other, cq_final, cq_out, "all")
    co_steps = reduce(2, co_ref, co_recv, co_pieces) + spread(4, local, co_pieces, co_other, co_final, co_out, "all")
    joint_steps = reduce(3, joint_ref, joint_recv, joint_pieces)
    joint_steps += spread(5, width, joint_pieces, None, joint_pieces, joint_out, "own")
    class Vectors:
        def __init__(self, value, over_dp, own, over_mp, base):
            self.value, self.over_dp, self.own, self.over_mp, self.base = value, over_dp, own, over_mp, base

        def first(self, k):
            return remote(self.value, self.over_dp.at[place.d], vec_ssem.at[self.base, k], vec_rsem.at[self.base, k],
                          (everyone[k - 1], place.m))

        def second(self, k):
            return remote(self.own, self.over_mp.at[place.m], vec_zsend.at[self.base, k], vec_zrecv.at[self.base, k],
                          place.peer(k))

        def begin(self):
            self.over_dp[place.d] = self.value[...]
            for k in range(1, dp):
                self.first(k).start()

        def turn(self):
            for k in range(1, dp):
                self.first(k).wait()
            total = self.over_dp[0]
            for j in range(1, dp):
                total += self.over_dp[j]
            self.own[...] = total
            self.over_mp[place.m] = total
            for k in offsets:
                self.second(k).start()

        def end(self):
            for k in offsets:
                self.second(k).wait()

        def total(self):
            value = self.over_mp[0]
            for j in range(1, n):
                value += self.over_mp[j]
            return value

    early_sum = Vectors(early, early_dp, early_own, early_mp, 0)
    late_sum = Vectors(late, late_dp, late_own, late_mp, 1)
    part = text_grad.shape[0]
    spread_text = nt(dtext[...], kv[...]).astype(BF)
    for g in range(n):
        text_send[g] = spread_text[g * part : (g + 1) * part, :]

    def text_copy(k):
        return remote(text_send.at[place.along(k)], text_recv.at[place.m], text_ssem.at[k], text_rsem.at[k], place.peer(k))

    for t in range(2):
        joint_ref[3 + t] = tn(text[...], dtext[:, t * local : (t + 1) * local]).astype(BF)

    def prepare(i, _):
        block = block_of(i)
        for hp in range(pairs):
            columns = slice(hp * PAIR, (hp + 1) * PAIR)
            stacked[hp, i] = stack_heads(projected[block, columns], SCALE)
            above[hp, i] = stack_heads(dmixed[block, columns])
            product = (dmixed[block, columns].astype(F32) * mixed[block, columns].astype(F32)).T
            delta[hp, i] = jnp.concatenate(
                [jnp.sum(product[:HEAD_DIM], axis=0, keepdims=True), jnp.sum(product[HEAD_DIM:], axis=0, keepdims=True)],
                axis=1,
            )
            dquery[hp, i] = jnp.zeros_like(dquery[hp, i])
        return 0

    lax.fori_loop(0, n, prepare, 0)
    meet(partners)
    mi_steps[0]()
    mo_steps[0]()
    for load, steps in zip(loads, (so_steps, cq_steps, co_steps)):
        load.wait()
        steps[0]()
    early_sum.begin()
    for k in offsets:
        text_copy(k).start()

    plan = [[so_steps[1]], [cq_steps[1]], [co_steps[1]]]
    each = -(-len(plan) // (n * pairs))
    parity = lax.rem(place.m, 2)
    mine = place.m // 2

    def near_copy(t):
        return remote(near_send.at[t], near_recv.at[t], near_ssem.at[t], near_rsem.at[t], (place.d, place.mate))

    def far_copy(t):
        gap = lax.rem(t - mine + half, half)
        return remote(far_send.at[t], far_recv.at[mine], far_ssem.at[gap], far_rsem.at[gap], (place.d, 2 * t + parity))

    def pass_on(t):
        near_copy(t).wait()
        total = near_hold[t] + near_recv[t].astype(F32)

        @pl.when(mine == t)
        def _():
            dn1_own[...] = total

        @pl.when(mine != t)
        def _():
            far_send[t] = total.astype(BF)
            far_copy(t).start()

    point = 0
    for j in range(n):
        keys = slice(j * size, (j + 1) * size)
        for hp in range(pairs):
            columns = slice(hp * PAIR, (hp + 1) * PAIR)
            key = projected[keys, local + hp * PAIR : local + (hp + 1) * PAIR]
            value = projected[keys, 2 * local + hp * PAIR : 2 * local + (hp + 1) * PAIR]

            def tile(i, carry, diagonal):
                dkey, dvalue = carry
                query, over = stacked[hp, i], above[hp, i]
                scores = nt(key, query)
                if diagonal:
                    scores = jnp.where(causal(size, size), scores, MASKED)
                weights = jnp.exp(scores - totals[hp, i])
                dscores = (weights * (nt(value, over) - delta[hp, i])).astype(BF)
                dvalue = dvalue + nn(weights.astype(BF), over)
                dkey = dkey + nn(dscores, query)
                turned = tn(key, dscores)
                dquery[hp, i] += jnp.concatenate([turned[:HEAD_DIM, :size], turned[HEAD_DIM:, size:]], axis=0)
                return dkey, dvalue

            carry = (jnp.zeros((size, PAIR), F32), jnp.zeros((size, PAIR), F32))
            carry = tile(j, carry, True)
            dkey, dvalue = lax.fori_loop(j + 1, n, lambda i, c: tile(i, c, False), carry)
            dprojected[keys, columns] = (dquery[hp, j].T * SCALE).astype(BF)
            dprojected[keys, local + hp * PAIR : local + (hp + 1) * PAIR] = dkey.astype(BF)
            dprojected[keys, 2 * local + hp * PAIR : 2 * local + (hp + 1) * PAIR] = dvalue.astype(BF)
            for phases in plan[point * each : (point + 1) * each]:
                for phase in phases:
                    phase()
            point += 1
        partial_sum = sum(nt(dprojected[keys, t * local : (t + 1) * local], qkv[t]) for t in range(3))

        @pl.when(parity == j % 2)
        def _():
            near_hold[j // 2] = partial_sum

        @pl.when(parity != j % 2)
        def _():
            near_send[j // 2] = partial_sum.astype(BF)
            near_copy(j // 2).start()

    tile_rows = min(256, width)

    def qkv_grad(t, _):
        at = pl.ds(pl.multiple_of(t * tile_rows, tile_rows), tile_rows)
        total = tn(normed[:, at], dprojected[...]).astype(BF)
        for t in range(3):
            joint_ref[t, at, :] = total[:, t * local : (t + 1) * local]
        return 0

    lax.fori_loop(0, width // tile_rows, qkv_grad, 0)
    bits = (dp // 2).bit_length() - 1
    small_steps = (so_steps, cq_steps, co_steps)
    for t in range(half - 1):
        pass_on(t)
    for steps in small_steps:
        steps[2]()
    joint_steps[0]()
    for k in range(1, bits):
        for steps in small_steps:
            steps[2 + k]()
    for steps in small_steps:
        steps[2 + bits]()
    joint_steps[1]()
    pass_on(half - 1)
    mi_steps[1]()
    mo_steps[1]()
    for k in range(bits):
        joint_steps[2 + k]()
    joint_steps[2 + bits]()
    joint_steps[3 + bits]()
    mi_steps[2]()
    mo_steps[2]()
    for steps in small_steps:
        steps[3 + bits]()
    for k in range(1, bits):
        mi_steps[2 + k]()
        mo_steps[2 + k]()
    joint_steps[4 + bits]()
    for k in range(bits - 1):
        for steps in small_steps:
            steps[4 + bits + k]()

    early_sum.turn()
    for k in range(1, half):
        far_copy(lax.rem(mine + k, half)).wait()
        dn1_own[...] += far_recv[lax.rem(mine + half - k, half)].astype(F32)
    loads[3].wait()
    late[...] = jnp.zeros_like(late)

    def last_back(chunk):
        grad = dn1_own[chunk, :]
        normal, inverse = norm_parts(image_rows[chunk, :].astype(F32))
        add_rows(late, 0, grad * normal)
        add_rows(late, 1, grad)
        image_grad[chunk, :] = residual[chunk, :] + norm_back(grad, normal, inverse, gain1[...])

    in_chunks(size, ROWS_AT_ONCE, last_back)
    late_sum.begin()
    for steps in small_steps:
        steps[3 + 2 * bits]()
    for k in offsets:
        text_copy(k).wait()
    total = text_send[place.m].astype(F32)
    for k in offsets:
        total += text_recv[place.along(k)].astype(F32)
    text_grad[...] = total
    late_sum.turn()
    early_sum.end()
    early_out[...] = early_sum.total()
    shared = early_out[pl.ds(8 + place.m // 2, 1), :] * 0.0
    for j in range(n):
        take = jnp.where(lax.rem(place.m + j, 2) == 0, 1.0, 0.0)
        shared += early_mp[j, pl.ds(8 + place.m // 2, 1), :] * take
    early_out[7:8, :] = shared
    for k in range(1, bits):
        joint_steps[4 + bits + k]()
    late_sum.end()
    late_out[...] = late_sum.total()
    for steps in (mi_steps, mo_steps, *small_steps, joint_steps):
        steps[-1]()


def back(sizes, gain1, qkv, kv, text, residual, projected, normed, mixed, totals, dmixed, dtext, early, mi_pieces, mo_pieces,
         image, so_grad, cq_grad, co_grad, hidden):
    n, dp = sizes["mp"], sizes["dp"]
    rows, width = normed.shape
    slots = text.shape[0]
    local = mixed.shape[1]
    size, pairs, half = rows // n, local // PAIR, n // 2
    bits = (dp // 2).bit_length() - 1
    vmem, hbm = pl.BlockSpec(memory_space=pltpu.VMEM), pl.BlockSpec(memory_space=pl.ANY)
    dma, mem = pltpu.SemaphoreType.DMA, pltpu.VMEM
    shape = jax.ShapeDtypeStruct

    def unit(count, height, columns, rule):
        pieces = piece_shape(count, height, columns, bits).shape
        scratch = []
        if rule != "parity":
            scratch += [mem((count, height, columns), BF), recv_space(count, height, columns, bits), mem(pieces, BF)]
        if rule != "own":
            scratch += [mem(pieces, BF), mem(pieces[1:], BF)]
        return scratch

    few = early.shape[0]
    whole = [(width, hidden), (hidden, width), (local, width), (width, local), (local, width), (5, width, local)]
    block = mem((half, size, width), BF)
    return pl.pallas_call(
        partial(back_kernel, sizes),
        out_shape=[
            shape((size, width), F32), shape((slots // n, width), F32), shape((few, width), F32), shape((2, width), F32),
        ] + [shape(extent, BF) for extent in whole],
        in_specs=[vmem] * 14 + [hbm] * 4,
        out_specs=[vmem] * 4 + [hbm] * 6,
        scratch_shapes=[
            mem((size, width), BF), mem((pairs, n, 2 * size, PAIR), BF), mem((pairs, n, 2 * size, PAIR), BF),
            mem((pairs, n, 1, 2 * size), F32), mem((pairs, n, PAIR, size), F32), mem((rows, 3 * local), BF),
            mem((half, size, width), F32), block, block, block, block, mem((size, width), F32),
            *unit(half, width, hidden, "parity"), *unit(half, hidden, width, "parity"),
            *unit(n, local, width, "all"), *unit(n, width, local, "all"), *unit(n, local, width, "all"),
            *unit(5, width, local, "own"),
            mem((dp, few, width), F32), mem((n, few, width), F32), mem((few, width), F32),
            mem((2, width), F32), mem((dp, 2, width), F32), mem((n, 2, width), F32), mem((2, width), F32),
            mem((n, slots // n, width), BF), mem((n, slots // n, width), BF),
            dma((4, 1 + 2 * bits)), dma((4, 1 + 2 * bits)), dma((6, 1 + 2 * bits + n)), dma((6, 1 + 2 * bits + n)), dma((6, 2)),
            dma((4,)), dma((half,)), dma((half,)), dma((half,)), dma((half,)), dma((n,)), dma((n,)),
            dma((2, dp)), dma((2, dp)), dma((2, n)), dma((2, n)),
        ],
        compiler_params=pltpu.CompilerParams(collective_id=2, has_side_effects=True, vmem_limit_bytes=VMEM_LIMIT),
        cost_estimate=pl.CostEstimate(flops=8 << 30, bytes_accessed=48 << 20, transcendentals=4 << 20),
    )(gain1, qkv, kv, text, residual, projected, normed, mixed, totals, dmixed, dtext, early, mi_pieces, mo_pieces,
      image, so_grad, cq_grad, co_grad)


def finish_kernel(slots, out, image_grad, text_grad, early, late, mi, mo, so, cq, co, joint,
                  to_out, to_image, to_text, to_mi, to_mo, to_so, to_cq, to_co, to_qkv, to_kv, to_bias, *to_vectors):
    to_out[...] = out[...]
    to_image[...] = image_grad[...]
    to_text[...] = text_grad[...]
    for source, target in ((mi, to_mi), (mo, to_mo), (so, to_so), (cq, to_cq), (co, to_co)):
        target[...] = source[...].astype(F32)
    for t in range(3):
        to_qkv[t] = joint[t].astype(F32)
    for t in range(2):
        to_kv[:, t, :] = joint[3 + t].astype(F32)
    for t in range(2):
        to_vectors[t][...] = late[t : t + 1, :]
    for t in range(2, 7):
        to_vectors[t][...] = early[t : t + 1, :]
    to_bias[...] = early[7:8, 0 : to_bias.shape[1]]


def finish(out, image_grad, text_grad, early, late, mi, mo, so, cq, co, joint):
    steps = 2
    width, hidden = mi.shape
    local = so.shape[0]

    def cut(value, axis=0):
        shape = list(value.shape)
        shape[axis] //= steps
        return pl.BlockSpec(tuple(shape), lambda i: tuple(i if t == axis else 0 for t in range(len(shape))))

    def whole(shape):
        return pl.BlockSpec(tuple(shape), lambda i: (0,) * len(shape))

    shape = jax.ShapeDtypeStruct
    sums = [shape(value.shape, F32) for value in (mi, mo, so, cq, co)]
    qkv, kv = shape((3, width, local), F32), shape((width, 2, local), F32)
    return pl.pallas_call(
        partial(finish_kernel, steps),
        grid=(steps,),
        out_shape=[shape(out.shape, BF), shape(image_grad.shape, F32), shape(text_grad.shape, F32), *sums, qkv, kv,
                   shape((1, hidden), F32)] + [shape((1, width), F32)] * 7,
        in_specs=[cut(out), cut(image_grad), whole(text_grad.shape), whole(early.shape), whole(late.shape)]
        + [cut(value) for value in (mi, mo, so, cq, co)] + [cut(joint, 1)],
        out_specs=[cut(out), cut(image_grad), whole(text_grad.shape)] + [cut(value) for value in sums]
        + [cut(qkv, 1), cut(kv), whole((1, hidden))] + [whole((1, width))] * 7,
        compiler_params=pltpu.CompilerParams(vmem_limit_bytes=VMEM_LIMIT),
        cost_estimate=pl.CostEstimate(flops=1 << 22, bytes_accessed=28 << 20, transcendentals=0),
    )(out, image_grad, text_grad, early, late, mi, mo, so, cq, co, joint)


def body(sizes, image, text, grad_out, lengths, gain1, shift1, qkv, so, gain2, shift2, cq, kv, co, gain3, shift3, mi,
         in_bias, mo, out_bias):
    n = sizes["mp"]
    image, text, grad_out = image[0], text[0], grad_out[0]
    rows, width = image.shape
    local = so.shape[0]
    sizes = dict(sizes, share=share_of(local, sizes["dp"]))
    qkv, kv = jnp.transpose(qkv, (1, 0, 2)), kv.reshape(width, 2 * local)
    row = lambda value: value[None]
    (projected, normed1, mixed, totals, out, residual, dmixed, dtext, so_grad, cq_grad, co_grad, mi_pieces, mo_pieces,
     early) = layer(
        sizes, image, row(gain1), row(shift1), qkv, text, kv, row(lengths), row(gain2), row(shift2), row(gain3),
        row(shift3), row(in_bias), row(out_bias), so, cq, co, mi, mo, grad_out)
    image_grad, text_grad, early, late, mi_sum, mo_sum, so_sum, cq_sum, co_sum, joint_sum = back(
        sizes, row(gain1), qkv, kv, text, residual, projected, normed1, mixed, totals, dmixed, dtext, early,
        mi_pieces, mo_pieces, image, so_grad, cq_grad, co_grad, mi.shape[1])
    (out, image_grad, text_grad, mi_sum, mo_sum, so_sum, cq_sum, co_sum, qkv_sum, kv_sum, bias_sum, *vectors) = finish(
        out, image_grad, text_grad, early, late, mi_sum, mo_sum, so_sum, cq_sum, co_sum, joint_sum)
    g1, s1, g2, s2, g3, s3, ob = (value[0] for value in vectors)
    return (
        out[None], image_grad[None], text_grad[None], g1, s1, jnp.transpose(qkv_sum, (1, 0, 2)), so_sum, g2, s2, cq_sum,
        kv_sum, co_sum, g3, s3, mi_sum, bias_sum[0], mo_sum, ob,
    )


def solution(mesh):
    rows3, rows2, rows1 = P(None, None, "mp"), P(None, "mp"), P("mp")
    item = P("dp", None, None)
    in_specs = (item, item, item, P("dp"), P(), P(), rows3, P("mp", None), P(), P(), rows2, rows3, P("mp", None), P(), P(),
                rows2, rows1, P("mp", None), P())
    split = P("dp", "mp", None)
    out_specs = (split, split, split, P(), P(), rows3, P("mp", None), P(), P(), rows2, rows3, P("mp", None), P(), P(),
                 rows2, rows1, P("mp", None), P())
    sizes = dict(mesh.shape)
    return jax.shard_map(partial(body, sizes), mesh=mesh, in_specs=in_specs, out_specs=out_specs, check_vma=False)
```

```python
from functools import partial

import jax
import jax.numpy as jnp
from jax import lax
from jax.experimental import pallas as pl
from jax.experimental.pallas import tpu as pltpu
from jax.sharding import PartitionSpec as P

HEAD_DIM = 64
PAIR = 2 * HEAD_DIM
EPSILON = 1e-05
SCALE = HEAD_DIM ** (-0.5)
MASKED = -1e30
BF = jnp.bfloat16
F32 = jnp.float32
MESH = pl.DeviceIdType.MESH
VMEM_LIMIT = 60 << 20


def nn(a, b):
    return lax.dot_general(a, b, (((1,), (0,)), ((), ())), preferred_element_type=F32)


def nt(a, b):
    return lax.dot_general(a, b, (((1,), (1,)), ((), ())), preferred_element_type=F32)


def tn(a, b):
    return lax.dot_general(a, b, (((0,), (0,)), ((), ())), preferred_element_type=F32)


def norm_parts(value):
    center = value - jnp.mean(value, axis=-1, keepdims=True)
    inverse = lax.rsqrt(jnp.mean(center * center, axis=-1, keepdims=True) + EPSILON)
    return center * inverse, inverse


def half_masks():
    lane = lax.broadcasted_iota(jnp.int32, (1, PAIR), 1)
    first = jnp.where(lane < HEAD_DIM, 1.0, 0.0)
    return first, 1.0 - first


def stack_heads(pair, scale=None):
    first, second = half_masks()
    if scale is not None:
        first, second = first * scale, second * scale
    wide = pair.astype(F32)
    return jnp.concatenate([wide * first, wide * second], axis=0).astype(BF)


def fold_heads(stacked):
    rows = stacked.shape[1] // 2
    both = jnp.concatenate([stacked[:HEAD_DIM, :rows], stacked[HEAD_DIM:, rows:]], axis=0)
    return both.T


def causal(tile_keys, tile_rows):
    key = lax.broadcasted_iota(jnp.int32, (tile_keys, tile_rows), 0)
    row = lax.broadcasted_iota(jnp.int32, (tile_keys, tile_rows), 1)
    both = key <= row
    return jnp.concatenate([both, both], axis=1)


class Place:
    def __init__(self, sizes):
        self.n = sizes["mp"]
        self.dp = sizes["dp"]
        self.share = sizes["share"]
        self.d = lax.axis_index("dp")
        self.m = lax.axis_index("mp")
        self.core = lax.rem(self.d, 2)
        self.mate = self.m + 1 - 2 * lax.rem(self.m, 2)
        self.partner = (self.d + 1 - 2 * self.core, self.m)
        self.member = lax.rem(self.d, self.share)
        self.chip = self.member // 2
        self.base = self.d - self.member
        self.piece = self.core * (self.share // 2) + self.chip

    def along(self, offset):
        return lax.rem(self.m + offset, self.n)

    def mate_along(self, offset):
        return lax.rem(self.mate + offset, self.n)

    def peer(self, offset):
        return (self.d, self.along(offset))

    def chip_peer(self, offset):
        chip = lax.rem(self.chip + offset, self.share // 2)
        return (self.base + 2 * chip + self.core, self.m), self.core * (self.share // 2) + chip


def greet(devices):
    for device in devices:
        pl.semaphore_signal(pltpu.get_barrier_semaphore(), inc=1, device_id=device, device_id_type=MESH)


def meet(devices):
    pl.semaphore_wait(pltpu.get_barrier_semaphore(), len(devices))


class Gather:
    def __init__(self, place, own, full, everyone, slot_of, sems):
        self.place, self.own, self.full, self.slot_of = place, own, full, slot_of
        self.count = own.shape[0] // place.share
        self.sems = sems
        self.even = list(range(2, place.n, 2))
        self.sources = [place.along(place.n - k) for k in self.even]
        if everyone:
            self.sources.append(place.mate)
            self.sources += [place.mate_along(place.n - k) for k in self.even]
        self.everyone = everyone

    def rows_of(self, slot, piece, pieces=1):
        start = pl.multiple_of(piece * self.count, self.count)
        return self.full.at[slot, pl.ds(start, pieces * self.count), :]

    def copy(self, src, dst, index, hop, device):
        return pltpu.make_async_remote_copy(
            src_ref=src, dst_ref=dst, send_sem=self.sems[0].at[index, hop], recv_sem=self.sems[1].at[index, hop],
            device_id=device, device_id_type=MESH,
        )

    def first(self, index):
        place, parity = self.place, len(self.even)
        mine = self.own.at[pl.ds(pl.multiple_of(place.piece * self.count, self.count), self.count), :]
        slot = self.slot_of(place.m)
        if index < parity:
            device = place.peer(self.even[index])
        else:
            device = (place.d, place.mate)
        if index > parity:
            slot = self.slot_of(self.sources[index - parity - 1])
            mine = self.rows_of(slot, place.piece)
        return self.copy(mine, self.rows_of(slot, place.piece), index, 0, device)

    def second(self, index, hop):
        block = self.rows_of(self.slot_of(self.sources[index]), self.place.piece)
        return self.copy(block, block, index, hop, self.place.chip_peer(hop)[0])

    def third(self, index):
        half = self.place.share // 2
        block = self.rows_of(self.slot_of(self.sources[index]), self.place.core * half, half)
        return self.copy(block, block, index, half, self.place.partner)

    def local(self):
        return pltpu.make_async_copy(self.own, self.full.at[self.slot_of(self.place.m)], self.sems[2])

    def step(self, number):
        hops = range(1, self.place.share // 2)
        parity = len(self.even)
        everything = range(len(self.sources))
        if number == 0:
            for index in everything:
                if index <= parity:
                    self.first(index).start()
        elif number == 1:
            for index in range(parity):
                self.first(index).wait_recv()
                if self.everyone:
                    self.first(parity + 1 + index).start()
                for hop in hops:
                    self.second(index, hop).start()
        elif number == 2:
            for index in everything[parity:]:
                self.first(index).wait_recv()
                for hop in hops:
                    self.second(index, hop).start()
        elif number == 3:
            for index in everything:
                for hop in hops:
                    self.second(index, hop).wait_recv()
                self.third(index).start()
        else:
            for index in everything:
                self.third(index).wait()
                self.first(index).wait_send()
                for hop in hops:
                    self.second(index, hop).wait_send()

    def finish(self):
        self.step(4)
        self.local().wait()


def attend_block(projected, mixed, totals, i, hp, size, local):
    rows = pl.ds(pl.multiple_of(i * size, size), size)
    column = pl.multiple_of(hp * PAIR, PAIR)
    query = stack_heads(projected[rows, pl.ds(column, PAIR)], SCALE)

    def tile(j, carry, diagonal):
        largest, total, acc = carry
        keys = pl.ds(pl.multiple_of(j * size, size), size)
        key = projected[keys, pl.ds(column + local, PAIR)]
        value = projected[keys, pl.ds(column + 2 * local, PAIR)]
        scores = nt(key, query)
        if diagonal:
            scores = jnp.where(causal(size, size), scores, MASKED)
        top = jnp.maximum(largest, jnp.max(scores, axis=0, keepdims=True))
        powers = jnp.exp(scores - top)
        shrink = jnp.exp(largest - top)
        total = total * shrink + jnp.sum(powers, axis=0, keepdims=True)
        acc = acc * shrink + tn(value, powers.astype(BF))
        return top, total, acc

    carry = (
        jnp.full((1, 2 * size), MASKED, F32),
        jnp.zeros((1, 2 * size), F32),
        jnp.zeros((PAIR, 2 * size), F32),
    )
    carry = tile(i, carry, True)
    largest, total, acc = lax.fori_loop(0, i, lambda j, c: tile(j, c, False), carry)
    mixed[rows, pl.ds(column, PAIR)] = fold_heads(acc / total).astype(BF)
    totals[hp, i] = largest + jnp.log(total)


def share_of(local, dp):
    share = dp
    while (local // share) % 16:
        share //= 2
    return share


def halvings(rows, bits):
    left = [rows // 4]
    for _ in range(bits):
        left.append(left[-1] // 2 if left[-1] % 32 == 0 else left[-1])
    return left


def arrivals(rows, bits):
    left = halvings(rows, bits)
    return left[1:]


class Rows:
    def __init__(self, place, rows):
        self.place = place
        self.half = rows // 2
        self.bits = (place.dp // 2).bit_length() - 1
        self.left = halvings(rows, self.bits)
        self.count = self.left[-1]
        self.chip = place.d // 2

    def bit(self, p, k):
        b = k if p == 0 else self.bits - 1 - k
        value = lax.rem(self.chip // (1 << b), 2)
        chip = self.chip + (1 - 2 * value) * (1 << b)
        return value, (2 * chip + self.place.core, self.place.m)

    def cut(self, k):
        return self.left[k + 1] < self.left[k]

    def region(self, p, k):
        start = self.place.core * self.half + p * self.left[0]
        for t in range(k):
            if self.cut(t):
                start = start + self.bit(p, t)[0] * self.left[t + 1]
        return start

    def span(self, start, count):
        return pl.ds(pl.multiple_of(start, 16), count)


class Reduce:
    def __init__(self, place, ref, recv, pieces, sems):
        self.place, self.ref, self.recv, self.pieces = place, ref, recv, pieces
        self.rows = Rows(place, ref.shape[1])
        self.send, self.recv_sem = sems

    def copy(self, src, dst, index, device):
        return pltpu.make_async_remote_copy(
            src_ref=src, dst_ref=dst, send_sem=self.send.at[index], recv_sem=self.recv_sem.at[index],
            device_id=device, device_id_type=MESH,
        )

    def core_copy(self):
        half = self.rows.half
        away = self.rows.span((1 - self.place.core) * half, half)
        return self.copy(self.ref.at[:, away, :], self.recv.at[:, pl.ds(0, half), :], 0, self.place.partner)

    def offset(self, p, k):
        into = self.rows.left[1:]
        return self.rows.half + p * sum(into) + sum(into[:k])

    def chip_copy(self, p, k):
        rows = self.rows
        value, device = rows.bit(p, k)
        count = rows.left[k + 1]
        start = rows.region(p, k)
        if rows.cut(k):
            start = start + (1 - value) * count
        return self.copy(
            self.ref.at[:, rows.span(start, count), :], self.recv.at[:, pl.ds(self.offset(p, k), count), :],
            1 + p * rows.bits + k, device)

    def add(self, start, offset, count, target, target_start):
        chunk = min(32, count)
        span = self.rows.span

        def run(t, _):
            at = t * chunk
            for s in range(self.ref.shape[0]):
                mine = self.ref[s, span(start + at, chunk), :].astype(F32)
                theirs = self.recv[s, span(offset + at, chunk), :].astype(F32)
                target[s, span(target_start + at, chunk), :] = (mine + theirs).astype(BF)
            return 0

        lax.fori_loop(0, count // chunk, run, 0)

    def phases(self):
        rows = self.rows

        def begin():
            self.core_copy().start()

        def core_sum():
            self.core_copy().wait()
            self.add(self.place.core * rows.half, 0, rows.half, self.ref, self.place.core * rows.half)
            for p in range(2):
                self.chip_copy(p, 0).start()

        def chip_sum(k):
            last = k == rows.bits - 1
            for p in range(2):
                self.chip_copy(p, k).wait()
                start = rows.region(p, k + 1)
                self.add(start, self.offset(p, k), rows.left[k + 1], self.pieces if last else self.ref,
                         p * rows.count if last else start)
                if not last:
                    self.chip_copy(p, k + 1).start()

        return [begin, core_sum] + [partial(chip_sum, k) for k in range(rows.bits)]


class Spread:
    def __init__(self, place, rows, pieces, other, final, whole, rule, sems):
        self.place, self.pieces, self.other, self.final, self.whole = place, pieces, other, final, whole
        self.rows = Rows(place, rows)
        self.rule, (self.send, self.recv_sem, self.keep) = rule, sems
        if rule == "all":
            self.hops = [(k, place.along(k)) for k in range(1, place.n)]
            self.slot = place.m
        elif rule == "parity":
            half = place.n // 2
            self.hops = [(2 * k, lax.rem(place.m // 2 + k, half)) for k in range(1, half)]
            self.slot = place.m // 2
        else:
            self.hops, self.slot = [], 0

    def copy(self, src, dst, index, device):
        return pltpu.make_async_remote_copy(
            src_ref=src, dst_ref=dst, send_sem=self.send.at[index], recv_sem=self.recv_sem.at[index],
            device_id=device, device_id_type=MESH,
        )

    def far_copy(self, index):
        hop, slot = self.hops[index]
        return self.copy(self.pieces.at[slot], self.other.at[self.slot], 1 + 2 * self.rows.bits + index, self.place.peer(hop))

    def view(self, ref, start, count):
        span = self.rows.span(start, count)
        return ref.at[:, span, :] if self.rule == "own" else ref.at[span, :]

    def spread_copy(self, p, k):
        rows = self.rows
        count = rows.left[k + 1]
        block = self.view(self.whole, rows.region(p, k + 1), count)
        first = not any(rows.cut(t) for t in range(k + 1, rows.bits))
        src = self.view(self.final, p * rows.count, rows.count) if first else block
        return self.copy(src, block, 1 + p * rows.bits + k, rows.bit(p, k)[1])

    def keep_copy(self, p):
        rows = self.rows
        block = self.view(self.whole, rows.region(p, rows.bits), rows.count)
        return pltpu.make_async_copy(self.view(self.final, p * rows.count, rows.count), block, self.keep.at[p])

    def core_spread(self):
        half = self.rows.half
        block = self.view(self.whole, self.place.core * half, half)
        return self.copy(block, block, 0, self.place.partner)

    def phases(self):
        rows = self.rows
        cuts = [k for k in reversed(range(rows.bits)) if rows.cut(k)]

        def far():
            for index in range(len(self.hops)):
                self.far_copy(index).start()

        def far_sum():
            if self.hops:
                total = self.pieces[self.slot].astype(F32)
                for index, (hop, _) in enumerate(self.hops):
                    self.far_copy(index).wait()
                    source = self.place.along(self.place.n - hop)
                    total += self.other[source if self.rule == "all" else source // 2].astype(F32)
                self.final[...] = total.astype(BF)
            for p in range(2):
                self.keep_copy(p).start()
                self.spread_copy(p, cuts[0]).start()
            for p in range(2):
                self.keep_copy(p).wait()

        def spread(t):
            for p in range(2):
                self.spread_copy(p, cuts[t]).wait()
                if t + 1 < len(cuts):
                    self.spread_copy(p, cuts[t + 1]).start()
            if t + 1 == len(cuts):
                self.core_spread().start()

        def end():
            self.core_spread().wait()

        nothing = [lambda: None] * (rows.bits - len(cuts))
        return [far, far_sum] + [partial(spread, t) for t in range(len(cuts))] + nothing + [end]


def recv_space(count, rows, columns, bits):
    return pltpu.VMEM((count, rows // 2 + 2 * sum(arrivals(rows, bits)), columns), BF)


def piece_shape(count, rows, columns, bits):
    return jax.ShapeDtypeStruct((count, 2 * halvings(rows, bits)[-1], columns), BF)


def norm_back(grad, normal, inverse, gain):
    scaled = grad * gain
    return inverse * (
        scaled
        - jnp.mean(scaled, axis=-1, keepdims=True)
        - normal * jnp.mean(scaled * normal, axis=-1, keepdims=True)
    )


def add_rows(ref, index, value):
    ref[pl.ds(index, 1), :] += jnp.sum(value, axis=0, keepdims=True)


def in_chunks(total, chunk, step):
    def run(i, _):
        step(pl.ds(pl.multiple_of(i * chunk, chunk), chunk))
        return 0

    lax.fori_loop(0, total // chunk, run, 0)


def cross_pair(query, text_proj, length, idx, local):
    per = local // PAIR
    g, hp = idx // per, lax.rem(idx, per)
    near = pl.multiple_of(hp * PAIR, PAIR)
    column = pl.multiple_of(idx * PAIR, PAIR)
    stacked = stack_heads(query[:, pl.ds(column, PAIR)], SCALE)
    key = text_proj[g, :, pl.ds(near, PAIR)]
    value = text_proj[g, :, pl.ds(near + local, PAIR)]
    scores = nt(key, stacked)
    slot = lax.broadcasted_iota(jnp.int32, scores.shape, 0)
    return g, near, column, stacked, key, value, jnp.where(slot < length, scores, MASKED)


ROWS_AT_ONCE = 32


def layer_kernel(
    sizes,
    image, gain1, shift1, qkv, text, kv, length, gain2, shift2, gain3, shift3, in_bias, out_bias,
    so, cq, co, mi, mo, grad_out,
    projected, normed, mixed, totals, out, residual, dmixed, dtext, so_grad, cq_grad, co_grad, mi_pieces, mo_pieces,
    vectors,
    mixed_rows, text_proj, so_full, cq_full, co_full, mi_full, mo_full, bias_full,
    grad_pair, mixed_all, first, second, work, grad2, out_part,
    n2, query, cross, cross_totals, dquery, n3_pair, active, dhidden,
    dn3_send, dn3_recv, out_send, out_recv, r2, dcross, r1, dmixed_send, dtext_send, dtext_recv,
    text_own, mi_recv, mo_recv, small_send, small_recv, small_own, wide_send, wide_recv, wide_own,
    mix_send, mix_recv, mix_own, text_send, text_recv, bias_send, bias_recv, load_sem,
    pair_send, pair_recv, dmix_send, dmix_recv, dtext_ssem, dtext_rsem, store_sem, reduce_send, reduce_recv,
):
    place = Place(sizes)
    n, share = place.n, place.share
    rows, width = image.shape
    size = rows // n
    local, hidden = so.shape[0], mi.shape[1]
    half = n // 2
    offsets = list(range(1, n))
    mate = (place.d, place.mate)
    mine = place.m // 2
    chips = place.dp // 2
    partners = [place.peer(k) for k in offsets] + [place.partner]
    partners += [(2 * lax.rem(place.d // 2 + k, chips) + place.core, place.m) for k in range(1, chips)]
    greet(partners)
    meet(partners)

    def remote(src, dst, send, recv, device):
        return pltpu.make_async_remote_copy(
            src_ref=src, dst_ref=dst, send_sem=send, recv_sem=recv, device_id=device, device_id_type=MESH
        )

    small = [
        Gather(place, own, full, True, lambda s: s, (small_send.at[t], small_recv.at[t], small_own.at[t]))
        for t, (own, full) in enumerate(((so, so_full), (cq, cq_full), (co, co_full)))
    ]
    wide = [
        Gather(place, own, full, False, lambda s: s // 2, (wide_send.at[t], wide_recv.at[t], wide_own.at[t]))
        for t, (own, full) in enumerate(((mi, mi_full), (mo, mo_full)))
    ]
    for item in small:
        item.step(0)
    for item in small + wide:
        item.local().start()
    wide[0].step(0)

    def block_of(index):
        return pl.ds(pl.multiple_of(index * size, size), size)

    own_rows = block_of(place.m)
    loads = [
        pltpu.make_async_copy(grad_out.at[own_rows, :], grad_pair.at[0], load_sem.at[0]),
        pltpu.make_async_copy(grad_out.at[block_of(mate[1]), :], grad_pair.at[1], load_sem.at[1]),
    ]
    for load in loads:
        load.start()
    bias_full[mine] = in_bias[...]

    def bias_copy(k):
        return remote(in_bias, bias_full.at[mine], bias_send.at[k], bias_recv.at[k], place.peer(2 * k))

    for k in range(1, half):
        bias_copy(k).start()

    def project(i, _):
        block = block_of(i)

        def norm(chunk):
            at = pl.ds(pl.multiple_of(i * size + chunk.start, ROWS_AT_ONCE), ROWS_AT_ONCE)
            normal, _ = norm_parts(image[at, :].astype(F32))
            normed[at, :] = (normal * gain1[...] + shift1[...]).astype(BF)

        in_chunks(size, ROWS_AT_ONCE, norm)
        for t in range(3):
            projected[block, t * local : (t + 1) * local] = nn(normed[block, :], qkv[t]).astype(BF)
        return 0

    lax.fori_loop(0, n, project, 0)
    text_own[...] = nn(text[...], kv[...]).astype(BF)
    text_proj[place.m] = text_own[...]

    even = list(range(2, n, 2))

    def text_copy(k):
        return remote(text_own, text_proj.at[place.m], text_send.at[k], text_recv.at[k], place.peer(k) if k else mate)

    def text_pass(k):
        block = text_proj.at[place.along(n - k)]
        return remote(block, block, text_send.at[k + 1], text_recv.at[k + 1], mate)

    for k in [0] + even:
        text_copy(k).start()

    def mix_copy(i):
        gap = lax.rem(i - place.m + n, n)
        return remote(mixed.at[block_of(i), :], mixed_rows.at[place.m], mix_send.at[gap], mix_recv.at[gap], (place.d, i))

    mix_keep = pltpu.make_async_copy(mixed.at[own_rows, :], mixed_rows.at[place.m], mix_own)
    for item in small:
        item.step(1)
    plan = [[] for _ in range(n)]
    plan[1] = [small[0]]
    plan[2] = [small[1]]
    plan[n - 1] += [small[2]]
    for i in range(n):
        lax.fori_loop(0, local // PAIR, lambda hp, _: (attend_block(projected, mixed, totals, i, hp, size, local), 0)[1], 0)

        @pl.when(place.m != i)
        def _():
            mix_copy(i).start()

        @pl.when(place.m == i)
        def _():
            mix_keep.start()

        for item in plan[i]:
            item.step(2)

    wide[1].step(0)
    for k in even:
        text_copy(k).wait_recv()
        text_pass(k).start()
    small[0].step(3)

    for k in offsets:
        mix_copy(place.along(k)).wait()
    mix_keep.wait()
    small[0].finish()
    small[1].step(3)
    for g in range(n):
        mixed_all[:, g * local : (g + 1) * local] = mixed_rows[g]
    first[...] = nn(mixed_all[...], so_full[...].reshape(n * local, width))

    def first_norm(chunk):
        at = pl.ds(pl.multiple_of(place.m * size + chunk.start, ROWS_AT_ONCE), ROWS_AT_ONCE)
        value = image[at, :].astype(F32) + first[chunk, :]
        first[chunk, :] = value
        n2[chunk, :] = (norm_parts(value)[0] * gain2[...] + shift2[...]).astype(BF)

    in_chunks(size, ROWS_AT_ONCE, first_norm)
    small[1].finish()
    small[2].step(3)
    for g in range(n):
        query[:, g * local : (g + 1) * local] = nn(n2[...], cq_full[g]).astype(BF)
    text_copy(0).wait()
    for k in even:
        text_copy(k).wait_send()
        text_pass(k).wait()
    for item in wide:
        item.step(1)
    limit = length[0, 0]
    all_pairs = n * local // PAIR

    def cross_forward(idx, _):
        g, near, column, stacked, key, value, scores = cross_pair(query, text_proj, limit, idx, local)
        largest = jnp.max(scores, axis=0, keepdims=True)
        powers = jnp.exp(scores - largest)
        total = jnp.sum(powers, axis=0, keepdims=True)
        cross_totals[idx] = largest + jnp.log(total)
        cross[:, pl.ds(column, PAIR)] = fold_heads(tn(value, (powers / total).astype(BF))).astype(BF)
        return 0

    lax.fori_loop(0, all_pairs, cross_forward, 0)
    small[2].finish()
    second[...] = nn(cross[...], co_full[...].reshape(n * local, width))

    def second_norm(chunk):
        value = first[chunk, :] + second[chunk, :]
        second[chunk, :] = value
        n3_pair[0, chunk, :] = (norm_parts(value)[0] * gain3[...] + shift3[...]).astype(BF)

    in_chunks(size, ROWS_AT_ONCE, second_norm)

    n3_copy = remote(n3_pair.at[0], n3_pair.at[1], pair_send.at[0], pair_recv.at[0], mate)
    n3_copy.start()
    for load in loads:
        load.wait()
    for k in range(1, half):
        bias_copy(k).wait()
    for item in wide:
        item.local().wait()
    step = min(256, hidden)

    def feed(p, slot):
        grads = grad_pair[p]

        def chunk(c, _):
            columns = pl.ds(pl.multiple_of(c * step, step), step)
            value = nn(n3_pair[p], mi_full[slot, :, columns]) + bias_full[slot, :, columns]
            inner = 0.5 * (1.0 + lax.erf(value * (0.5**0.5)))
            slope = inner + value * jnp.exp(-0.5 * value * value) * ((2.0 * jnp.pi) ** -0.5)
            active[slot, p, :, columns] = (value * inner).astype(BF)
            dhidden[slot, p, :, columns] = (nt(grads, mo_full[slot, columns, :]) * slope).astype(BF)
            return 0

        lax.fori_loop(0, hidden // step, chunk, 0)

    def sum_slots(term):
        total = term(0)
        for slot in range(1, half):
            total += term(slot)
        return total

    feed(0, mine)
    for item in wide:
        item.step(3)
    n3_copy.wait()
    feed(1, mine)
    for item in wide:
        item.step(4)
    others = [lax.rem(mine + k, half) for k in range(1, half)]
    for slot in others:
        feed(1, slot)
    dn3_send[...] = sum_slots(lambda slot: nt(dhidden[slot, 1], mi_full[slot])).astype(BF)
    dn3_copy = remote(dn3_send, dn3_recv, pair_send.at[1], pair_recv.at[1], mate)
    dn3_copy.start()
    for slot in others:
        feed(0, slot)
    work[...] = sum_slots(lambda slot: nt(dhidden[slot, 0], mi_full[slot]))
    tile = min(256, width)

    def wide_grads(slot, first):
        inner = n3_pair.shape[0] * size
        hidden_grad = dhidden[slot].reshape(inner, hidden)
        grads = grad_pair[...].reshape(inner, width)
        if first:
            vectors[8 + slot : 9 + slot, 0:hidden] = jnp.sum(hidden_grad.astype(F32), axis=0, keepdims=True)

        def into(t, _):
            at = pl.ds(pl.multiple_of(t * tile, tile), tile)
            mi_full[slot, at, :] = tn(n3_pair[:, :, at].reshape(inner, tile), hidden_grad).astype(BF)
            return 0

        if first:
            lax.fori_loop(0, width // tile, into, 0)
            return

        def back(t, _):
            at = pl.ds(pl.multiple_of(t * step, step), step)
            mo_full[slot, at, :] = tn(active[slot, :, :, at].reshape(inner, step), grads).astype(BF)
            return 0

        lax.fori_loop(0, hidden // step, back, 0)

    mi_steps = Reduce(place, mi_full, mi_recv, mi_pieces, (reduce_send.at[0], reduce_recv.at[0])).phases()
    mo_steps = Reduce(place, mo_full, mo_recv, mo_pieces, (reduce_send.at[1], reduce_recv.at[1])).phases()
    wide_steps = [step for pair in zip(mi_steps, mo_steps) for step in pair]
    vectors[...] = jnp.zeros_like(vectors)
    for slot in range(half):
        wide_grads(slot, True)
    wide_steps[0]()
    out_send[...] = sum_slots(lambda slot: nn(active[slot, 1], mo_full[slot])).astype(BF)
    out_copy = remote(out_send, out_recv, pair_send.at[2], pair_recv.at[2], mate)
    out_copy.start()
    out_part[...] = sum_slots(lambda slot: nn(active[slot, 0], mo_full[slot]))
    for slot in range(half):
        wide_grads(slot, False)
    wide_steps[1]()
    wide_steps[2]()
    dn3_copy.wait()


    def third_back(chunk):
        grad = work[chunk, :] + dn3_recv[chunk, :].astype(F32)
        normal, inverse = norm_parts(second[chunk, :])
        above = grad_pair[0, chunk, :].astype(F32)
        add_rows(vectors, 4, grad * normal)
        add_rows(vectors, 5, grad)
        add_rows(vectors, 6, above)
        value = above + norm_back(grad, normal, inverse, gain3[...])
        work[chunk, :] = value
        r2[chunk, :] = value.astype(BF)

    in_chunks(size, ROWS_AT_ONCE, third_back)
    wide_steps[3]()
    dcross[...] = nt(r2[...], co_full[...].reshape(n * local, width)).astype(BF)

    def cross_back(idx, _):
        g, near, column, stacked, key, value, scores = cross_pair(query, text_proj, limit, idx, local)
        weights = jnp.exp(scores - cross_totals[idx])
        above = stack_heads(dcross[:, pl.ds(column, PAIR)])
        dweights = nt(value, above)
        dscores = (weights * (dweights - jnp.sum(weights * dweights, axis=0, keepdims=True))).astype(BF)
        dquery[:, pl.ds(column, PAIR)] = (fold_heads(tn(key, dscores)) * SCALE).astype(BF)
        dtext_send[g, :, pl.ds(near, PAIR)] = nn(dscores, stacked).astype(BF)
        dtext_send[g, :, pl.ds(near + local, PAIR)] = nn(weights.astype(BF), above).astype(BF)
        return 0

    lax.fori_loop(0, all_pairs, cross_back, 0)
    wide_steps[4]()

    def dtext_copy(k):
        return remote(dtext_send.at[place.along(k)], dtext_recv.at[place.m], dtext_ssem.at[k], dtext_rsem.at[k], place.peer(k))

    for k in offsets:
        dtext_copy(k).start()
    def both(term):
        total = term(0)
        for g in range(1, n):
            total += term(g)
        return total

    grad2[...] = both(lambda g: nt(dquery[:, g * local : (g + 1) * local], cq_full[g]))

    def second_back(chunk):
        grad = grad2[chunk, :]
        normal, inverse = norm_parts(first[chunk, :])
        add_rows(vectors, 2, grad * normal)
        add_rows(vectors, 3, grad)
        value = work[chunk, :] + norm_back(grad, normal, inverse, gain2[...])
        residual[chunk, :] = value
        r1[chunk, :] = value.astype(BF)

    in_chunks(size, ROWS_AT_ONCE, second_back)

    def dmix_copy(k):
        return remote(dmixed_send.at[k], dmixed.at[own_rows, :], dmix_send.at[k], dmix_recv.at[k], place.peer(k))

    for k in offsets:
        dmixed_send[k] = nt(r1[...], so_full[place.along(k)]).astype(BF)
        dmix_copy(k).start()
    dmixed[own_rows, :] = nt(r1[...], so_full[place.m]).astype(BF)
    wide_steps[5]()

    stores = []

    def small_grad(left, right, keep, target, index):
        for g in range(n):
            heads = slice(g * local, (g + 1) * local)
            if keep.shape[1] == local:
                keep[g] = tn(left[:, heads], right[...]).astype(BF)
            else:
                keep[g] = tn(left[...], right[:, heads]).astype(BF)
        copy = pltpu.make_async_copy(keep, target, store_sem.at[index])
        copy.start()
        stores.append(copy)

    small_grad(n2, dquery, cq_full, cq_grad, 0)
    small_grad(mixed_all, r1, so_full, so_grad, 1)
    small_grad(cross, r2, co_full, co_grad, 2)

    out_copy.wait()

    def finish_out(chunk):
        value = second[chunk, :] + out_part[chunk, :] + out_recv[chunk, :].astype(F32) + out_bias[...]
        out[chunk, :] = value.astype(BF)

    in_chunks(size, ROWS_AT_ONCE, finish_out)
    for run in wide_steps[6:]:
        run()
    for k in offsets:
        dtext_copy(k).wait()
    total = dtext_send[place.m].astype(F32)
    for k in offsets:
        total += dtext_recv[place.along(k)].astype(F32)
    dtext[...] = total.astype(BF)
    for k in offsets:
        dmix_copy(k).wait()
    for store in stores:
        store.wait()


def layer(sizes, image, gain1, shift1, qkv, text, kv, length, gain2, shift2, gain3, shift3, in_bias, out_bias,
          so, cq, co, mi, mo, grad_out):
    n, share = sizes["mp"], sizes["share"]
    rows, width = image.shape
    slots = text.shape[0]
    local, hidden = so.shape[0], mi.shape[1]
    size = rows // n
    pairs = local // PAIR
    hops = share // 2 + 1
    half = n // 2
    vmem, hbm = pl.BlockSpec(memory_space=pltpu.VMEM), pl.BlockSpec(memory_space=pl.ANY)
    dma, mem = pltpu.SemaphoreType.DMA, pltpu.VMEM
    shape = jax.ShapeDtypeStruct
    few = max(half - 1, 1)
    bits = (sizes["dp"] // 2).bit_length() - 1
    return pl.pallas_call(
        partial(layer_kernel, sizes),
        out_shape=[
            shape((rows, 3 * local), BF), shape((rows, width), BF), shape((rows, local), BF),
            shape((pairs, n, 1, 2 * size), F32), shape((size, width), BF), shape((size, width), F32),
            shape((rows, local), BF), shape((slots, 2 * local), BF),
            shape((n, local, width), BF), shape((n, width, local), BF), shape((n, local, width), BF),
            piece_shape(half, width, hidden, bits), piece_shape(half, hidden, width, bits),
            shape((8 + -(-half // 8) * 8, width), F32),
        ],
        in_specs=[vmem] * 6 + [pl.BlockSpec(memory_space=pltpu.SMEM)] + [vmem] * 6 + [hbm] * 6,
        out_specs=[vmem] * 8 + [hbm] * 3 + [vmem] * 3,
        scratch_shapes=[
            mem((n, size, local), BF), mem((n, slots, 2 * local), BF),
            mem((n, local, width), BF), mem((n, width, local), BF), mem((n, local, width), BF),
            mem((half, width, hidden), BF), mem((half, hidden, width), BF), mem((half, 1, hidden), F32),
            mem((2, size, width), BF), mem((size, n * local), BF),
            mem((size, width), F32), mem((size, width), F32), mem((size, width), F32), mem((size, width), F32),
            mem((size, width), F32),
            mem((size, width), BF), mem((size, n * local), BF), mem((size, n * local), BF),
            mem((n * pairs, 1, 2 * size), F32), mem((size, n * local), BF),
            mem((2, size, width), BF), mem((half, 2, size, hidden), BF), mem((half, 2, size, hidden), BF),
            mem((size, width), BF), mem((size, width), BF), mem((size, width), BF), mem((size, width), BF),
            mem((size, width), BF), mem((size, n * local), BF), mem((size, width), BF),
            mem((n, size, local), BF), mem((n, slots, 2 * local), BF), mem((n, slots, 2 * local), BF),
            mem((slots, 2 * local), BF), recv_space(half, width, hidden, bits), recv_space(half, hidden, width, bits),
            dma((3, n - 1, hops)), dma((3, n - 1, hops)), dma((3,)),
            dma((2, few, hops)), dma((2, few, hops)), dma((2,)),
            dma((n,)), dma((n,)), dma(()),
            dma((n + 1,)), dma((n + 1,)), dma((half,)), dma((half,)), dma((2,)),
            dma((3,)), dma((3,)), dma((n,)), dma((n,)), dma((n,)), dma((n,)), dma((3,)), dma((2, 1 + 2 * bits)), dma((2, 1 + 2 * bits)),
        ],
        compiler_params=pltpu.CompilerParams(collective_id=1, has_side_effects=True, vmem_limit_bytes=VMEM_LIMIT),
        cost_estimate=pl.CostEstimate(flops=22 << 30, bytes_accessed=48 << 20, transcendentals=8 << 20),
    )(image, gain1, shift1, qkv, text, kv, length, gain2, shift2, gain3, shift3, in_bias, out_bias,
      so, cq, co, mi, mo, grad_out)


def back_kernel(
    sizes,
    gain1, qkv, kv, text, residual, projected, normed, mixed, totals, dmixed, dtext, early, mi_pieces, mo_pieces,
    image, so_grad, cq_grad, co_grad,
    image_grad, text_grad, early_out, late_out, mi_out, mo_out, so_out, cq_out, co_out, joint_out,
    image_rows, stacked, above, delta, dquery, dprojected,
    near_hold, near_send, near_recv, far_send, far_recv, dn1_own,
    mi_other, mi_final, mo_other, mo_final,
    so_ref, so_recv, so_pieces, so_other, so_final, cq_ref, cq_recv, cq_pieces, cq_other, cq_final,
    co_ref, co_recv, co_pieces, co_other, co_final, joint_ref, joint_recv, joint_pieces,
    early_dp, early_mp, early_own, late, late_dp, late_mp, late_own, text_send, text_recv,
    reduce_send, reduce_recv, spread_send, spread_recv, spread_keep, load_sem,
    near_ssem, near_rsem, far_ssem, far_rsem, text_ssem, text_rsem, vec_ssem, vec_rsem, vec_zsend, vec_zrecv,
):
    place = Place(sizes)
    n, dp = place.n, place.dp
    rows, width = normed.shape
    local = mixed.shape[1]
    size = rows // n
    half = n // 2
    pairs = local // PAIR
    offsets = list(range(1, n))
    everyone = [lax.rem(place.d + k, dp) for k in range(1, dp)]
    partners = [place.peer(k) for k in offsets] + [(device, place.m) for device in everyone]
    greet(partners)

    def remote(src, dst, send, recv, device):
        return pltpu.make_async_remote_copy(
            src_ref=src, dst_ref=dst, send_sem=send, recv_sem=recv, device_id=device, device_id_type=MESH
        )

    def block_of(index):
        return pl.ds(pl.multiple_of(index * size, size), size)

    loads = [
        pltpu.make_async_copy(src, dst, load_sem.at[t])
        for t, (src, dst) in enumerate((
            (so_grad, so_ref), (cq_grad, cq_ref), (co_grad, co_ref), (image.at[block_of(place.m), :], image_rows),
        ))
    ]
    for load in loads:
        load.start()

    def reduce(t, ref, recv, pieces):
        return Reduce(place, ref, recv, pieces, (reduce_send.at[t], reduce_recv.at[t])).phases()

    def spread(t, rows, pieces, other, final, whole, rule):
        sems = (spread_send.at[t], spread_recv.at[t], spread_keep.at[t])
        return Spread(place, rows, pieces, other, final, whole, rule, sems).phases()

    mi_steps = spread(0, width, mi_pieces, mi_other, mi_final, mi_out, "parity")
    mo_steps = spread(1, mo_out.shape[0], mo_pieces, mo_other, mo_final, mo_out, "parity")
    so_steps = reduce(0, so_ref, so_recv, so_pieces) + spread(2, local, so_pieces, so_other, so_final, so_out, "all")
    cq_steps = reduce(1, cq_ref, cq_recv, cq_pieces) + spread(3, width, cq_pieces, cq_other, cq_final, cq_out, "all")
    co_steps = reduce(2, co_ref, co_recv, co_pieces) + spread(4, local, co_pieces, co_other, co_final, co_out, "all")
    joint_steps = reduce(3, joint_ref, joint_recv, joint_pieces)
    joint_steps += spread(5, width, joint_pieces, None, joint_pieces, joint_out, "own")
    class Vectors:
        def __init__(self, value, over_dp, own, over_mp, base):
            self.value, self.over_dp, self.own, self.over_mp, self.base = value, over_dp, own, over_mp, base

        def first(self, k):
            return remote(self.value, self.over_dp.at[place.d], vec_ssem.at[self.base, k], vec_rsem.at[self.base, k],
                          (everyone[k - 1], place.m))

        def second(self, k):
            return remote(self.own, self.over_mp.at[place.m], vec_zsend.at[self.base, k], vec_zrecv.at[self.base, k],
                          place.peer(k))

        def begin(self):
            self.over_dp[place.d] = self.value[...]
            for k in range(1, dp):
                self.first(k).start()

        def turn(self):
            for k in range(1, dp):
                self.first(k).wait()
            total = self.over_dp[0]
            for j in range(1, dp):
                total += self.over_dp[j]
            self.own[...] = total
            self.over_mp[place.m] = total
            for k in offsets:
                self.second(k).start()

        def end(self):
            for k in offsets:
                self.second(k).wait()

        def total(self):
            value = self.over_mp[0]
            for j in range(1, n):
                value += self.over_mp[j]
            return value

    early_sum = Vectors(early, early_dp, early_own, early_mp, 0)
    late_sum = Vectors(late, late_dp, late_own, late_mp, 1)
    part = text_grad.shape[0]
    spread_text = nt(dtext[...], kv[...]).astype(BF)
    for g in range(n):
        text_send[g] = spread_text[g * part : (g + 1) * part, :]

    def text_copy(k):
        return remote(text_send.at[place.along(k)], text_recv.at[place.m], text_ssem.at[k], text_rsem.at[k], place.peer(k))

    for t in range(2):
        joint_ref[3 + t] = tn(text[...], dtext[:, t * local : (t + 1) * local]).astype(BF)

    def prepare(i, _):
        block = block_of(i)
        for hp in range(pairs):
            columns = slice(hp * PAIR, (hp + 1) * PAIR)
            stacked[hp, i] = stack_heads(projected[block, columns], SCALE)
            above[hp, i] = stack_heads(dmixed[block, columns])
            product = (dmixed[block, columns].astype(F32) * mixed[block, columns].astype(F32)).T
            delta[hp, i] = jnp.concatenate(
                [jnp.sum(product[:HEAD_DIM], axis=0, keepdims=True), jnp.sum(product[HEAD_DIM:], axis=0, keepdims=True)],
                axis=1,
            )
            dquery[hp, i] = jnp.zeros_like(dquery[hp, i])
        return 0

    lax.fori_loop(0, n, prepare, 0)
    meet(partners)
    mi_steps[0]()
    mo_steps[0]()
    for load, steps in zip(loads, (so_steps, cq_steps, co_steps)):
        load.wait()
        steps[0]()
    early_sum.begin()
    for k in offsets:
        text_copy(k).start()

    plan = [[so_steps[1]], [cq_steps[1]], [co_steps[1]]]
    each = -(-len(plan) // (n * pairs))
    parity = lax.rem(place.m, 2)
    mine = place.m // 2

    def near_copy(t):
        return remote(near_send.at[t], near_recv.at[t], near_ssem.at[t], near_rsem.at[t], (place.d, place.mate))

    def far_copy(t):
        gap = lax.rem(t - mine + half, half)
        return remote(far_send.at[t], far_recv.at[mine], far_ssem.at[gap], far_rsem.at[gap], (place.d, 2 * t + parity))

    def pass_on(t):
        near_copy(t).wait()
        total = near_hold[t] + near_recv[t].astype(F32)

        @pl.when(mine == t)
        def _():
            dn1_own[...] = total

        @pl.when(mine != t)
        def _():
            far_send[t] = total.astype(BF)
            far_copy(t).start()

    point = 0
    for j in range(n):
        keys = slice(j * size, (j + 1) * size)
        for hp in range(pairs):
            columns = slice(hp * PAIR, (hp + 1) * PAIR)
            key = projected[keys, local + hp * PAIR : local + (hp + 1) * PAIR]
            value = projected[keys, 2 * local + hp * PAIR : 2 * local + (hp + 1) * PAIR]

            def tile(i, carry, diagonal):
                dkey, dvalue = carry
                query, over = stacked[hp, i], above[hp, i]
                scores = nt(key, query)
                if diagonal:
                    scores = jnp.where(causal(size, size), scores, MASKED)
                weights = jnp.exp(scores - totals[hp, i])
                dscores = (weights * (nt(value, over) - delta[hp, i])).astype(BF)
                dvalue = dvalue + nn(weights.astype(BF), over)
                dkey = dkey + nn(dscores, query)
                turned = tn(key, dscores)
                dquery[hp, i] += jnp.concatenate([turned[:HEAD_DIM, :size], turned[HEAD_DIM:, size:]], axis=0)
                return dkey, dvalue

            carry = (jnp.zeros((size, PAIR), F32), jnp.zeros((size, PAIR), F32))
            carry = tile(j, carry, True)
            dkey, dvalue = lax.fori_loop(j + 1, n, lambda i, c: tile(i, c, False), carry)
            dprojected[keys, columns] = (dquery[hp, j].T * SCALE).astype(BF)
            dprojected[keys, local + hp * PAIR : local + (hp + 1) * PAIR] = dkey.astype(BF)
            dprojected[keys, 2 * local + hp * PAIR : 2 * local + (hp + 1) * PAIR] = dvalue.astype(BF)
            for phases in plan[point * each : (point + 1) * each]:
                for phase in phases:
                    phase()
            point += 1
        partial_sum = sum(nt(dprojected[keys, t * local : (t + 1) * local], qkv[t]) for t in range(3))

        @pl.when(parity == j % 2)
        def _():
            near_hold[j // 2] = partial_sum

        @pl.when(parity != j % 2)
        def _():
            near_send[j // 2] = partial_sum.astype(BF)
            near_copy(j // 2).start()

    tile_rows = min(256, width)

    def qkv_grad(t, _):
        at = pl.ds(pl.multiple_of(t * tile_rows, tile_rows), tile_rows)
        total = tn(normed[:, at], dprojected[...]).astype(BF)
        for t in range(3):
            joint_ref[t, at, :] = total[:, t * local : (t + 1) * local]
        return 0

    lax.fori_loop(0, width // tile_rows, qkv_grad, 0)
    bits = (dp // 2).bit_length() - 1
    small_steps = (so_steps, cq_steps, co_steps)
    for t in range(half - 1):
        pass_on(t)
    for steps in small_steps:
        steps[2]()
    joint_steps[0]()
    for k in range(1, bits):
        for steps in small_steps:
            steps[2 + k]()
    for steps in small_steps:
        steps[2 + bits]()
    joint_steps[1]()
    pass_on(half - 1)
    mi_steps[1]()
    mo_steps[1]()
    for k in range(bits):
        joint_steps[2 + k]()
    joint_steps[2 + bits]()
    joint_steps[3 + bits]()
    mi_steps[2]()
    mo_steps[2]()
    for steps in small_steps:
        steps[3 + bits]()
    for k in range(1, bits):
        mi_steps[2 + k]()
        mo_steps[2 + k]()
    joint_steps[4 + bits]()
    for k in range(bits - 1):
        for steps in small_steps:
            steps[4 + bits + k]()

    early_sum.turn()
    for k in range(1, half):
        far_copy(lax.rem(mine + k, half)).wait()
        dn1_own[...] += far_recv[lax.rem(mine + half - k, half)].astype(F32)
    loads[3].wait()
    late[...] = jnp.zeros_like(late)

    def last_back(chunk):
        grad = dn1_own[chunk, :]
        normal, inverse = norm_parts(image_rows[chunk, :].astype(F32))
        add_rows(late, 0, grad * normal)
        add_rows(late, 1, grad)
        image_grad[chunk, :] = residual[chunk, :] + norm_back(grad, normal, inverse, gain1[...])

    in_chunks(size, ROWS_AT_ONCE, last_back)
    late_sum.begin()
    for steps in small_steps:
        steps[3 + 2 * bits]()
    for k in offsets:
        text_copy(k).wait()
    total = text_send[place.m].astype(F32)
    for k in offsets:
        total += text_recv[place.along(k)].astype(F32)
    text_grad[...] = total
    late_sum.turn()
    early_sum.end()
    early_out[...] = early_sum.total()
    shared = early_out[pl.ds(8 + place.m // 2, 1), :] * 0.0
    for j in range(n):
        take = jnp.where(lax.rem(place.m + j, 2) == 0, 1.0, 0.0)
        shared += early_mp[j, pl.ds(8 + place.m // 2, 1), :] * take
    early_out[7:8, :] = shared
    for k in range(1, bits):
        joint_steps[4 + bits + k]()
    late_sum.end()
    late_out[...] = late_sum.total()
    for steps in (mi_steps, mo_steps, *small_steps, joint_steps):
        steps[-1]()


def back(sizes, gain1, qkv, kv, text, residual, projected, normed, mixed, totals, dmixed, dtext, early, mi_pieces, mo_pieces,
         image, so_grad, cq_grad, co_grad, hidden):
    n, dp = sizes["mp"], sizes["dp"]
    rows, width = normed.shape
    slots = text.shape[0]
    local = mixed.shape[1]
    size, pairs, half = rows // n, local // PAIR, n // 2
    bits = (dp // 2).bit_length() - 1
    vmem, hbm = pl.BlockSpec(memory_space=pltpu.VMEM), pl.BlockSpec(memory_space=pl.ANY)
    dma, mem = pltpu.SemaphoreType.DMA, pltpu.VMEM
    shape = jax.ShapeDtypeStruct

    def unit(count, height, columns, rule):
        pieces = piece_shape(count, height, columns, bits).shape
        scratch = []
        if rule != "parity":
            scratch += [mem((count, height, columns), BF), recv_space(count, height, columns, bits), mem(pieces, BF)]
        if rule != "own":
            scratch += [mem(pieces, BF), mem(pieces[1:], BF)]
        return scratch

    few = early.shape[0]
    whole = [(width, hidden), (hidden, width), (local, width), (width, local), (local, width), (5, width, local)]
    block = mem((half, size, width), BF)
    return pl.pallas_call(
        partial(back_kernel, sizes),
        out_shape=[
            shape((size, width), F32), shape((slots // n, width), F32), shape((few, width), F32), shape((2, width), F32),
        ] + [shape(extent, BF) for extent in whole],
        in_specs=[vmem] * 14 + [hbm] * 4,
        out_specs=[vmem] * 4 + [hbm] * 6,
        scratch_shapes=[
            mem((size, width), BF), mem((pairs, n, 2 * size, PAIR), BF), mem((pairs, n, 2 * size, PAIR), BF),
            mem((pairs, n, 1, 2 * size), F32), mem((pairs, n, PAIR, size), F32), mem((rows, 3 * local), BF),
            mem((half, size, width), F32), block, block, block, block, mem((size, width), F32),
            *unit(half, width, hidden, "parity"), *unit(half, hidden, width, "parity"),
            *unit(n, local, width, "all"), *unit(n, width, local, "all"), *unit(n, local, width, "all"),
            *unit(5, width, local, "own"),
            mem((dp, few, width), F32), mem((n, few, width), F32), mem((few, width), F32),
            mem((2, width), F32), mem((dp, 2, width), F32), mem((n, 2, width), F32), mem((2, width), F32),
            mem((n, slots // n, width), BF), mem((n, slots // n, width), BF),
            dma((4, 1 + 2 * bits)), dma((4, 1 + 2 * bits)), dma((6, 1 + 2 * bits + n)), dma((6, 1 + 2 * bits + n)), dma((6, 2)),
            dma((4,)), dma((half,)), dma((half,)), dma((half,)), dma((half,)), dma((n,)), dma((n,)),
            dma((2, dp)), dma((2, dp)), dma((2, n)), dma((2, n)),
        ],
        compiler_params=pltpu.CompilerParams(collective_id=2, has_side_effects=True, vmem_limit_bytes=VMEM_LIMIT),
        cost_estimate=pl.CostEstimate(flops=8 << 30, bytes_accessed=48 << 20, transcendentals=4 << 20),
    )(gain1, qkv, kv, text, residual, projected, normed, mixed, totals, dmixed, dtext, early, mi_pieces, mo_pieces,
      image, so_grad, cq_grad, co_grad)


def finish_kernel(slots, out, image_grad, text_grad, early, late, mi, mo, so, cq, co, joint,
                  to_out, to_image, to_text, to_mi, to_mo, to_so, to_cq, to_co, to_qkv, to_kv, to_bias, *to_vectors):
    to_out[...] = out[...]
    to_image[...] = image_grad[...]
    to_text[...] = text_grad[...]
    for source, target in ((mi, to_mi), (mo, to_mo), (so, to_so), (cq, to_cq), (co, to_co)):
        target[...] = source[...].astype(F32)
    for t in range(3):
        to_qkv[t] = joint[t].astype(F32)
    for t in range(2):
        to_kv[:, t, :] = joint[3 + t].astype(F32)
    for t in range(2):
        to_vectors[t][...] = late[t : t + 1, :]
    for t in range(2, 7):
        to_vectors[t][...] = early[t : t + 1, :]
    to_bias[...] = early[7:8, 0 : to_bias.shape[1]]


def finish(out, image_grad, text_grad, early, late, mi, mo, so, cq, co, joint):
    steps = 2
    width, hidden = mi.shape
    local = so.shape[0]

    def cut(value, axis=0):
        shape = list(value.shape)
        shape[axis] //= steps
        return pl.BlockSpec(tuple(shape), lambda i: tuple(i if t == axis else 0 for t in range(len(shape))))

    def whole(shape):
        return pl.BlockSpec(tuple(shape), lambda i: (0,) * len(shape))

    shape = jax.ShapeDtypeStruct
    sums = [shape(value.shape, F32) for value in (mi, mo, so, cq, co)]
    qkv, kv = shape((3, width, local), F32), shape((width, 2, local), F32)
    return pl.pallas_call(
        partial(finish_kernel, steps),
        grid=(steps,),
        out_shape=[shape(out.shape, BF), shape(image_grad.shape, F32), shape(text_grad.shape, F32), *sums, qkv, kv,
                   shape((1, hidden), F32)] + [shape((1, width), F32)] * 7,
        in_specs=[cut(out), cut(image_grad), whole(text_grad.shape), whole(early.shape), whole(late.shape)]
        + [cut(value) for value in (mi, mo, so, cq, co)] + [cut(joint, 1)],
        out_specs=[cut(out), cut(image_grad), whole(text_grad.shape)] + [cut(value) for value in sums]
        + [cut(qkv, 1), cut(kv), whole((1, hidden))] + [whole((1, width))] * 7,
        compiler_params=pltpu.CompilerParams(vmem_limit_bytes=VMEM_LIMIT),
        cost_estimate=pl.CostEstimate(flops=1 << 22, bytes_accessed=28 << 20, transcendentals=0),
    )(out, image_grad, text_grad, early, late, mi, mo, so, cq, co, joint)


def body(sizes, image, text, grad_out, lengths, gain1, shift1, qkv, so, gain2, shift2, cq, kv, co, gain3, shift3, mi,
         in_bias, mo, out_bias):
    n = sizes["mp"]
    image, text, grad_out = image[0], text[0], grad_out[0]
    rows, width = image.shape
    local = so.shape[0]
    sizes = dict(sizes, share=share_of(local, sizes["dp"]))
    qkv, kv = jnp.transpose(qkv, (1, 0, 2)), kv.reshape(width, 2 * local)
    row = lambda value: value[None]
    (projected, normed1, mixed, totals, out, residual, dmixed, dtext, so_grad, cq_grad, co_grad, mi_pieces, mo_pieces,
     early) = layer(
        sizes, image, row(gain1), row(shift1), qkv, text, kv, row(lengths), row(gain2), row(shift2), row(gain3),
        row(shift3), row(in_bias), row(out_bias), so, cq, co, mi, mo, grad_out)
    image_grad, text_grad, early, late, mi_sum, mo_sum, so_sum, cq_sum, co_sum, joint_sum = back(
        sizes, row(gain1), qkv, kv, text, residual, projected, normed1, mixed, totals, dmixed, dtext, early,
        mi_pieces, mo_pieces, image, so_grad, cq_grad, co_grad, mi.shape[1])
    (out, image_grad, text_grad, mi_sum, mo_sum, so_sum, cq_sum, co_sum, qkv_sum, kv_sum, bias_sum, *vectors) = finish(
        out, image_grad, text_grad, early, late, mi_sum, mo_sum, so_sum, cq_sum, co_sum, joint_sum)
    g1, s1, g2, s2, g3, s3, ob = (value[0] for value in vectors)
    return (
        out[None], image_grad[None], text_grad[None], g1, s1, jnp.transpose(qkv_sum, (1, 0, 2)), so_sum, g2, s2, cq_sum,
        kv_sum, co_sum, g3, s3, mi_sum, bias_sum[0], mo_sum, ob,
    )


def solution(mesh):
    rows3, rows2, rows1 = P(None, None, "mp"), P(None, "mp"), P("mp")
    item = P("dp", None, None)
    in_specs = (item, item, item, P("dp"), P(), P(), rows3, P("mp", None), P(), P(), rows2, rows3, P("mp", None), P(), P(),
                rows2, rows1, P("mp", None), P())
    split = P("dp", "mp", None)
    out_specs = (split, split, split, P(), P(), rows3, P("mp", None), P(), P(), rows2, rows3, P("mp", None), P(), P(),
                 rows2, rows1, P("mp", None), P())
    sizes = dict(mesh.shape)
    return jax.shard_map(partial(body, sizes), mesh=mesh, in_specs=in_specs, out_specs=out_specs, check_vma=False)
```

```python
from functools import partial

import jax
import jax.numpy as jnp
from jax import lax
from jax.experimental import pallas as pl
from jax.experimental.pallas import tpu as pltpu
from jax.sharding import PartitionSpec as P

HEAD_DIM = 64
PAIR = 2 * HEAD_DIM
EPSILON = 1e-05
SCALE = HEAD_DIM ** (-0.5)
MASKED = -1e30
BF = jnp.bfloat16
F32 = jnp.float32
MESH = pl.DeviceIdType.MESH
VMEM_LIMIT = 60 << 20


def nn(a, b):
    return lax.dot_general(a, b, (((1,), (0,)), ((), ())), preferred_element_type=F32)


def nt(a, b):
    return lax.dot_general(a, b, (((1,), (1,)), ((), ())), preferred_element_type=F32)


def tn(a, b):
    return lax.dot_general(a, b, (((0,), (0,)), ((), ())), preferred_element_type=F32)


def norm_parts(value):
    center = value - jnp.mean(value, axis=-1, keepdims=True)
    inverse = lax.rsqrt(jnp.mean(center * center, axis=-1, keepdims=True) + EPSILON)
    return center * inverse, inverse


def half_masks():
    lane = lax.broadcasted_iota(jnp.int32, (1, PAIR), 1)
    first = jnp.where(lane < HEAD_DIM, 1.0, 0.0)
    return first, 1.0 - first


def stack_heads(pair, scale=None):
    first, second = half_masks()
    if scale is not None:
        first, second = first * scale, second * scale
    wide = pair.astype(F32)
    return jnp.concatenate([wide * first, wide * second], axis=0).astype(BF)


def fold_heads(stacked):
    rows = stacked.shape[1] // 2
    both = jnp.concatenate([stacked[:HEAD_DIM, :rows], stacked[HEAD_DIM:, rows:]], axis=0)
    return both.T


def causal(tile_keys, tile_rows):
    key = lax.broadcasted_iota(jnp.int32, (tile_keys, tile_rows), 0)
    row = lax.broadcasted_iota(jnp.int32, (tile_keys, tile_rows), 1)
    both = key <= row
    return jnp.concatenate([both, both], axis=1)


class Place:
    def __init__(self, sizes):
        self.n = sizes["mp"]
        self.dp = sizes["dp"]
        self.share = sizes["share"]
        self.d = lax.axis_index("dp")
        self.m = lax.axis_index("mp")
        self.core = lax.rem(self.d, 2)
        self.mate = self.m + 1 - 2 * lax.rem(self.m, 2)
        self.partner = (self.d + 1 - 2 * self.core, self.m)
        self.member = lax.rem(self.d, self.share)
        self.chip = self.member // 2
        self.base = self.d - self.member
        self.piece = self.core * (self.share // 2) + self.chip

    def along(self, offset):
        return lax.rem(self.m + offset, self.n)

    def mate_along(self, offset):
        return lax.rem(self.mate + offset, self.n)

    def peer(self, offset):
        return (self.d, self.along(offset))

    def chip_peer(self, offset):
        chip = lax.rem(self.chip + offset, self.share // 2)
        return (self.base + 2 * chip + self.core, self.m), self.core * (self.share // 2) + chip


def greet(devices):
    for device in devices:
        pl.semaphore_signal(pltpu.get_barrier_semaphore(), inc=1, device_id=device, device_id_type=MESH)


def meet(devices):
    pl.semaphore_wait(pltpu.get_barrier_semaphore(), len(devices))


class Gather:
    def __init__(self, place, own, full, everyone, slot_of, sems):
        self.place, self.own, self.full, self.slot_of = place, own, full, slot_of
        self.count = own.shape[0] // place.share
        self.sems = sems
        self.even = list(range(2, place.n, 2))
        self.sources = [place.along(place.n - k) for k in self.even]
        if everyone:
            self.sources.append(place.mate)
            self.sources += [place.mate_along(place.n - k) for k in self.even]
        self.everyone = everyone

    def rows_of(self, slot, piece, pieces=1):
        start = pl.multiple_of(piece * self.count, self.count)
        return self.full.at[slot, pl.ds(start, pieces * self.count), :]

    def copy(self, src, dst, index, hop, device):
        return pltpu.make_async_remote_copy(
            src_ref=src, dst_ref=dst, send_sem=self.sems[0].at[index, hop], recv_sem=self.sems[1].at[index, hop],
            device_id=device, device_id_type=MESH,
        )

    def first(self, index):
        place, parity = self.place, len(self.even)
        mine = self.own.at[pl.ds(pl.multiple_of(place.piece * self.count, self.count), self.count), :]
        slot = self.slot_of(place.m)
        if index < parity:
            device = place.peer(self.even[index])
        else:
            device = (place.d, place.mate)
        if index > parity:
            slot = self.slot_of(self.sources[index - parity - 1])
            mine = self.rows_of(slot, place.piece)
        return self.copy(mine, self.rows_of(slot, place.piece), index, 0, device)

    def second(self, index, hop):
        block = self.rows_of(self.slot_of(self.sources[index]), self.place.piece)
        return self.copy(block, block, index, hop, self.place.chip_peer(hop)[0])

    def third(self, index):
        half = self.place.share // 2
        block = self.rows_of(self.slot_of(self.sources[index]), self.place.core * half, half)
        return self.copy(block, block, index, half, self.place.partner)

    def local(self):
        return pltpu.make_async_copy(self.own, self.full.at[self.slot_of(self.place.m)], self.sems[2])

    def step(self, number):
        hops = range(1, self.place.share // 2)
        parity = len(self.even)
        everything = range(len(self.sources))
        if number == 0:
            for index in everything:
                if index <= parity:
                    self.first(index).start()
        elif number == 1:
            for index in range(parity):
                self.first(index).wait_recv()
                if self.everyone:
                    self.first(parity + 1 + index).start()
                for hop in hops:
                    self.second(index, hop).start()
        elif number == 2:
            for index in everything[parity:]:
                self.first(index).wait_recv()
                for hop in hops:
                    self.second(index, hop).start()
        elif number == 3:
            for index in everything:
                for hop in hops:
                    self.second(index, hop).wait_recv()
                self.third(index).start()
        else:
            for index in everything:
                self.third(index).wait()
                self.first(index).wait_send()
                for hop in hops:
                    self.second(index, hop).wait_send()

    def finish(self):
        self.step(4)
        self.local().wait()


def attend_block(projected, mixed, totals, i, hp, size, local):
    rows = pl.ds(pl.multiple_of(i * size, size), size)
    column = pl.multiple_of(hp * PAIR, PAIR)
    query = stack_heads(projected[rows, pl.ds(column, PAIR)], SCALE)

    def tile(j, carry, diagonal):
        largest, total, acc = carry
        keys = pl.ds(pl.multiple_of(j * size, size), size)
        key = projected[keys, pl.ds(column + local, PAIR)]
        value = projected[keys, pl.ds(column + 2 * local, PAIR)]
        scores = nt(key, query)
        if diagonal:
            scores = jnp.where(causal(size, size), scores, MASKED)
        top = jnp.maximum(largest, jnp.max(scores, axis=0, keepdims=True))
        powers = jnp.exp(scores - top)
        shrink = jnp.exp(largest - top)
        total = total * shrink + jnp.sum(powers, axis=0, keepdims=True)
        acc = acc * shrink + tn(value, powers.astype(BF))
        return top, total, acc

    carry = (
        jnp.full((1, 2 * size), MASKED, F32),
        jnp.zeros((1, 2 * size), F32),
        jnp.zeros((PAIR, 2 * size), F32),
    )
    carry = tile(i, carry, True)
    largest, total, acc = lax.fori_loop(0, i, lambda j, c: tile(j, c, False), carry)
    mixed[rows, pl.ds(column, PAIR)] = fold_heads(acc / total).astype(BF)
    totals[hp, i] = largest + jnp.log(total)


def share_of(local, dp):
    share = dp
    while (local // share) % 16:
        share //= 2
    return share


def halvings(rows, bits):
    left = [rows // 4]
    for _ in range(bits):
        left.append(left[-1] // 2 if left[-1] % 32 == 0 else left[-1])
    return left


def arrivals(rows, bits):
    left = halvings(rows, bits)
    return left[1:]


class Rows:
    def __init__(self, place, rows):
        self.place = place
        self.half = rows // 2
        self.bits = (place.dp // 2).bit_length() - 1
        self.left = halvings(rows, self.bits)
        self.count = self.left[-1]
        self.chip = place.d // 2

    def bit(self, p, k):
        b = k if p == 0 else self.bits - 1 - k
        value = lax.rem(self.chip // (1 << b), 2)
        chip = self.chip + (1 - 2 * value) * (1 << b)
        return value, (2 * chip + self.place.core, self.place.m)

    def cut(self, k):
        return self.left[k + 1] < self.left[k]

    def region(self, p, k):
        start = self.place.core * self.half + p * self.left[0]
        for t in range(k):
            if self.cut(t):
                start = start + self.bit(p, t)[0] * self.left[t + 1]
        return start

    def span(self, start, count):
        return pl.ds(pl.multiple_of(start, 16), count)


class Reduce:
    def __init__(self, place, ref, recv, pieces, sems):
        self.place, self.ref, self.recv, self.pieces = place, ref, recv, pieces
        self.rows = Rows(place, ref.shape[1])
        self.send, self.recv_sem = sems

    def copy(self, src, dst, index, device):
        return pltpu.make_async_remote_copy(
            src_ref=src, dst_ref=dst, send_sem=self.send.at[index], recv_sem=self.recv_sem.at[index],
            device_id=device, device_id_type=MESH,
        )

    def core_copy(self):
        half = self.rows.half
        away = self.rows.span((1 - self.place.core) * half, half)
        return self.copy(self.ref.at[:, away, :], self.recv.at[:, pl.ds(0, half), :], 0, self.place.partner)

    def offset(self, p, k):
        into = self.rows.left[1:]
        return self.rows.half + p * sum(into) + sum(into[:k])

    def chip_copy(self, p, k):
        rows = self.rows
        value, device = rows.bit(p, k)
        count = rows.left[k + 1]
        start = rows.region(p, k)
        if rows.cut(k):
            start = start + (1 - value) * count
        return self.copy(
            self.ref.at[:, rows.span(start, count), :], self.recv.at[:, pl.ds(self.offset(p, k), count), :],
            1 + p * rows.bits + k, device)

    def add(self, start, offset, count, target, target_start):
        chunk = min(32, count)
        span = self.rows.span

        def run(t, _):
            at = t * chunk
            for s in range(self.ref.shape[0]):
                mine = self.ref[s, span(start + at, chunk), :].astype(F32)
                theirs = self.recv[s, span(offset + at, chunk), :].astype(F32)
                target[s, span(target_start + at, chunk), :] = (mine + theirs).astype(BF)
            return 0

        lax.fori_loop(0, count // chunk, run, 0)

    def phases(self):
        rows = self.rows

        def begin():
            self.core_copy().start()

        def core_sum():
            self.core_copy().wait()
            self.add(self.place.core * rows.half, 0, rows.half, self.ref, self.place.core * rows.half)
            for p in range(2):
                self.chip_copy(p, 0).start()

        def chip_sum(k):
            last = k == rows.bits - 1
            for p in range(2):
                self.chip_copy(p, k).wait()
                start = rows.region(p, k + 1)
                self.add(start, self.offset(p, k), rows.left[k + 1], self.pieces if last else self.ref,
                         p * rows.count if last else start)
                if not last:
                    self.chip_copy(p, k + 1).start()

        return [begin, core_sum] + [partial(chip_sum, k) for k in range(rows.bits)]


class Spread:
    def __init__(self, place, rows, pieces, other, final, whole, rule, sems):
        self.place, self.pieces, self.other, self.final, self.whole = place, pieces, other, final, whole
        self.rows = Rows(place, rows)
        self.rule, (self.send, self.recv_sem, self.keep) = rule, sems
        if rule == "all":
            self.hops = [(k, place.along(k)) for k in range(1, place.n)]
            self.slot = place.m
        elif rule == "parity":
            half = place.n // 2
            self.hops = [(2 * k, lax.rem(place.m // 2 + k, half)) for k in range(1, half)]
            self.slot = place.m // 2
        else:
            self.hops, self.slot = [], 0

    def copy(self, src, dst, index, device):
        return pltpu.make_async_remote_copy(
            src_ref=src, dst_ref=dst, send_sem=self.send.at[index], recv_sem=self.recv_sem.at[index],
            device_id=device, device_id_type=MESH,
        )

    def far_copy(self, index):
        hop, slot = self.hops[index]
        return self.copy(self.pieces.at[slot], self.other.at[self.slot], 1 + 2 * self.rows.bits + index, self.place.peer(hop))

    def view(self, ref, start, count):
        span = self.rows.span(start, count)
        return ref.at[:, span, :] if self.rule == "own" else ref.at[span, :]

    def spread_copy(self, p, k):
        rows = self.rows
        count = rows.left[k + 1]
        block = self.view(self.whole, rows.region(p, k + 1), count)
        first = not any(rows.cut(t) for t in range(k + 1, rows.bits))
        src = self.view(self.final, p * rows.count, rows.count) if first else block
        return self.copy(src, block, 1 + p * rows.bits + k, rows.bit(p, k)[1])

    def keep_copy(self, p):
        rows = self.rows
        block = self.view(self.whole, rows.region(p, rows.bits), rows.count)
        return pltpu.make_async_copy(self.view(self.final, p * rows.count, rows.count), block, self.keep.at[p])

    def core_spread(self):
        half = self.rows.half
        block = self.view(self.whole, self.place.core * half, half)
        return self.copy(block, block, 0, self.place.partner)

    def phases(self):
        rows = self.rows
        cuts = [k for k in reversed(range(rows.bits)) if rows.cut(k)]

        def far():
            for index in range(len(self.hops)):
                self.far_copy(index).start()

        def far_sum():
            if self.hops:
                total = self.pieces[self.slot].astype(F32)
                for index, (hop, _) in enumerate(self.hops):
                    self.far_copy(index).wait()
                    source = self.place.along(self.place.n - hop)
                    total += self.other[source if self.rule == "all" else source // 2].astype(F32)
                self.final[...] = total.astype(BF)
            for p in range(2):
                self.keep_copy(p).start()
                self.spread_copy(p, cuts[0]).start()
            for p in range(2):
                self.keep_copy(p).wait()

        def spread(t):
            for p in range(2):
                self.spread_copy(p, cuts[t]).wait()
                if t + 1 < len(cuts):
                    self.spread_copy(p, cuts[t + 1]).start()
            if t + 1 == len(cuts):
                self.core_spread().start()

        def end():
            self.core_spread().wait()

        nothing = [lambda: None] * (rows.bits - len(cuts))
        return [far, far_sum] + [partial(spread, t) for t in range(len(cuts))] + nothing + [end]


def recv_space(count, rows, columns, bits):
    return pltpu.VMEM((count, rows // 2 + 2 * sum(arrivals(rows, bits)), columns), BF)


def piece_shape(count, rows, columns, bits):
    return jax.ShapeDtypeStruct((count, 2 * halvings(rows, bits)[-1], columns), BF)


def norm_back(grad, normal, inverse, gain):
    scaled = grad * gain
    return inverse * (
        scaled
        - jnp.mean(scaled, axis=-1, keepdims=True)
        - normal * jnp.mean(scaled * normal, axis=-1, keepdims=True)
    )


def add_rows(ref, index, value):
    ref[pl.ds(index, 1), :] += jnp.sum(value, axis=0, keepdims=True)


def in_chunks(total, chunk, step):
    def run(i, _):
        step(pl.ds(pl.multiple_of(i * chunk, chunk), chunk))
        return 0

    lax.fori_loop(0, total // chunk, run, 0)


def cross_pair(query, text_proj, length, idx, local):
    per = local // PAIR
    g, hp = idx // per, lax.rem(idx, per)
    near = pl.multiple_of(hp * PAIR, PAIR)
    column = pl.multiple_of(idx * PAIR, PAIR)
    stacked = stack_heads(query[:, pl.ds(column, PAIR)], SCALE)
    key = text_proj[g, :, pl.ds(near, PAIR)]
    value = text_proj[g, :, pl.ds(near + local, PAIR)]
    scores = nt(key, stacked)
    slot = lax.broadcasted_iota(jnp.int32, scores.shape, 0)
    return g, near, column, stacked, key, value, jnp.where(slot < length, scores, MASKED)


ROWS_AT_ONCE = 32


def layer_kernel(
    sizes,
    image, gain1, shift1, qkv, text, kv, length, gain2, shift2, gain3, shift3, in_bias, out_bias,
    so, cq, co, mi, mo, grad_out,
    projected, normed, mixed, totals, out, residual, dmixed, dtext, so_grad, cq_grad, co_grad, mi_pieces, mo_pieces,
    vectors,
    mixed_rows, text_proj, so_full, cq_full, co_full, mi_full, mo_full, bias_full,
    grad_pair, mixed_all, first, second, work, grad2, out_part,
    n2, query, cross, cross_totals, dquery, n3_pair, active, dhidden,
    dn3_send, dn3_recv, out_send, out_recv, r2, dcross, r1, dmixed_send, dtext_send, dtext_recv,
    text_own, mi_recv, mo_recv, small_send, small_recv, small_own, wide_send, wide_recv, wide_own,
    mix_send, mix_recv, mix_own, text_send, text_recv, bias_send, bias_recv, load_sem,
    pair_send, pair_recv, dmix_send, dmix_recv, dtext_ssem, dtext_rsem, store_sem, reduce_send, reduce_recv,
):
    place = Place(sizes)
    n, share = place.n, place.share
    rows, width = image.shape
    size = rows // n
    local, hidden = so.shape[0], mi.shape[1]
    half = n // 2
    offsets = list(range(1, n))
    mate = (place.d, place.mate)
    mine = place.m // 2
    chips = place.dp // 2
    partners = [place.peer(k) for k in offsets] + [place.partner]
    partners += [(2 * lax.rem(place.d // 2 + k, chips) + place.core, place.m) for k in range(1, chips)]
    greet(partners)
    meet(partners)

    def remote(src, dst, send, recv, device):
        return pltpu.make_async_remote_copy(
            src_ref=src, dst_ref=dst, send_sem=send, recv_sem=recv, device_id=device, device_id_type=MESH
        )

    small = [
        Gather(place, own, full, True, lambda s: s, (small_send.at[t], small_recv.at[t], small_own.at[t]))
        for t, (own, full) in enumerate(((so, so_full), (cq, cq_full), (co, co_full)))
    ]
    wide = [
        Gather(place, own, full, False, lambda s: s // 2, (wide_send.at[t], wide_recv.at[t], wide_own.at[t]))
        for t, (own, full) in enumerate(((mi, mi_full), (mo, mo_full)))
    ]
    for item in small:
        item.step(0)
    for item in small + wide:
        item.local().start()
    wide[0].step(0)

    def block_of(index):
        return pl.ds(pl.multiple_of(index * size, size), size)

    own_rows = block_of(place.m)
    loads = [
        pltpu.make_async_copy(grad_out.at[own_rows, :], grad_pair.at[0], load_sem.at[0]),
        pltpu.make_async_copy(grad_out.at[block_of(mate[1]), :], grad_pair.at[1], load_sem.at[1]),
    ]
    for load in loads:
        load.start()
    bias_full[mine] = in_bias[...]

    def bias_copy(k):
        return remote(in_bias, bias_full.at[mine], bias_send.at[k], bias_recv.at[k], place.peer(2 * k))

    for k in range(1, half):
        bias_copy(k).start()

    def project(i, _):
        block = block_of(i)

        def norm(chunk):
            at = pl.ds(pl.multiple_of(i * size + chunk.start, ROWS_AT_ONCE), ROWS_AT_ONCE)
            normal, _ = norm_parts(image[at, :].astype(F32))
            normed[at, :] = (normal * gain1[...] + shift1[...]).astype(BF)

        in_chunks(size, ROWS_AT_ONCE, norm)
        for t in range(3):
            projected[block, t * local : (t + 1) * local] = nn(normed[block, :], qkv[t]).astype(BF)
        return 0

    lax.fori_loop(0, n, project, 0)
    text_own[...] = nn(text[...], kv[...]).astype(BF)
    text_proj[place.m] = text_own[...]

    even = list(range(2, n, 2))

    def text_copy(k):
        return remote(text_own, text_proj.at[place.m], text_send.at[k], text_recv.at[k], place.peer(k) if k else mate)

    def text_pass(k):
        block = text_proj.at[place.along(n - k)]
        return remote(block, block, text_send.at[k + 1], text_recv.at[k + 1], mate)

    for k in [0] + even:
        text_copy(k).start()

    def mix_copy(i):
        gap = lax.rem(i - place.m + n, n)
        return remote(mixed.at[block_of(i), :], mixed_rows.at[place.m], mix_send.at[gap], mix_recv.at[gap], (place.d, i))

    mix_keep = pltpu.make_async_copy(mixed.at[own_rows, :], mixed_rows.at[place.m], mix_own)
    for item in small:
        item.step(1)
    plan = [[] for _ in range(n)]
    plan[1] = [small[0]]
    plan[2] = [small[1]]
    plan[n - 1] += [small[2]]
    for i in range(n):
        lax.fori_loop(0, local // PAIR, lambda hp, _: (attend_block(projected, mixed, totals, i, hp, size, local), 0)[1], 0)

        @pl.when(place.m != i)
        def _():
            mix_copy(i).start()

        @pl.when(place.m == i)
        def _():
            mix_keep.start()

        for item in plan[i]:
            item.step(2)

    wide[1].step(0)
    for k in even:
        text_copy(k).wait_recv()
        text_pass(k).start()
    small[0].step(3)

    for k in offsets:
        mix_copy(place.along(k)).wait()
    mix_keep.wait()
    small[0].finish()
    small[1].step(3)
    for g in range(n):
        mixed_all[:, g * local : (g + 1) * local] = mixed_rows[g]
    first[...] = nn(mixed_all[...], so_full[...].reshape(n * local, width))

    def first_norm(chunk):
        at = pl.ds(pl.multiple_of(place.m * size + chunk.start, ROWS_AT_ONCE), ROWS_AT_ONCE)
        value = image[at, :].astype(F32) + first[chunk, :]
        first[chunk, :] = value
        n2[chunk, :] = (norm_parts(value)[0] * gain2[...] + shift2[...]).astype(BF)

    in_chunks(size, ROWS_AT_ONCE, first_norm)
    small[1].finish()
    small[2].step(3)
    for g in range(n):
        query[:, g * local : (g + 1) * local] = nn(n2[...], cq_full[g]).astype(BF)
    text_copy(0).wait()
    for k in even:
        text_copy(k).wait_send()
        text_pass(k).wait()
    for item in wide:
        item.step(1)
    limit = length[0, 0]
    all_pairs = n * local // PAIR

    def cross_forward(idx, _):
        g, near, column, stacked, key, value, scores = cross_pair(query, text_proj, limit, idx, local)
        largest = jnp.max(scores, axis=0, keepdims=True)
        powers = jnp.exp(scores - largest)
        total = jnp.sum(powers, axis=0, keepdims=True)
        cross_totals[idx] = largest + jnp.log(total)
        cross[:, pl.ds(column, PAIR)] = fold_heads(tn(value, (powers / total).astype(BF))).astype(BF)
        return 0

    lax.fori_loop(0, all_pairs, cross_forward, 0)
    small[2].finish()
    second[...] = nn(cross[...], co_full[...].reshape(n * local, width))

    def second_norm(chunk):
        value = first[chunk, :] + second[chunk, :]
        second[chunk, :] = value
        n3_pair[0, chunk, :] = (norm_parts(value)[0] * gain3[...] + shift3[...]).astype(BF)

    in_chunks(size, ROWS_AT_ONCE, second_norm)

    n3_copy = remote(n3_pair.at[0], n3_pair.at[1], pair_send.at[0], pair_recv.at[0], mate)
    n3_copy.start()
    for load in loads:
        load.wait()
    for k in range(1, half):
        bias_copy(k).wait()
    for item in wide:
        item.local().wait()
    step = min(256, hidden)

    def feed(p, slot):
        grads = grad_pair[p]

        def chunk(c, _):
            columns = pl.ds(pl.multiple_of(c * step, step), step)
            value = nn(n3_pair[p], mi_full[slot, :, columns]) + bias_full[slot, :, columns]
            inner = 0.5 * (1.0 + lax.erf(value * (0.5**0.5)))
            slope = inner + value * jnp.exp(-0.5 * value * value) * ((2.0 * jnp.pi) ** -0.5)
            active[slot, p, :, columns] = (value * inner).astype(BF)
            dhidden[slot, p, :, columns] = (nt(grads, mo_full[slot, columns, :]) * slope).astype(BF)
            return 0

        lax.fori_loop(0, hidden // step, chunk, 0)

    def sum_slots(term):
        total = term(0)
        for slot in range(1, half):
            total += term(slot)
        return total

    feed(0, mine)
    for item in wide:
        item.step(3)
    n3_copy.wait()
    feed(1, mine)
    for item in wide:
        item.step(4)
    others = [lax.rem(mine + k, half) for k in range(1, half)]
    for slot in others:
        feed(1, slot)
    dn3_send[...] = sum_slots(lambda slot: nt(dhidden[slot, 1], mi_full[slot])).astype(BF)
    dn3_copy = remote(dn3_send, dn3_recv, pair_send.at[1], pair_recv.at[1], mate)
    dn3_copy.start()
    for slot in others:
        feed(0, slot)
    work[...] = sum_slots(lambda slot: nt(dhidden[slot, 0], mi_full[slot]))
    tile = min(256, width)

    def wide_grads(slot, first):
        inner = n3_pair.shape[0] * size
        hidden_grad = dhidden[slot].reshape(inner, hidden)
        grads = grad_pair[...].reshape(inner, width)
        if first:
            vectors[8 + slot : 9 + slot, 0:hidden] = jnp.sum(hidden_grad.astype(F32), axis=0, keepdims=True)

        def into(t, _):
            at = pl.ds(pl.multiple_of(t * tile, tile), tile)
            mi_full[slot, at, :] = tn(n3_pair[:, :, at].reshape(inner, tile), hidden_grad).astype(BF)
            return 0

        if first:
            lax.fori_loop(0, width // tile, into, 0)
            return

        def back(t, _):
            at = pl.ds(pl.multiple_of(t * step, step), step)
            mo_full[slot, at, :] = tn(active[slot, :, :, at].reshape(inner, step), grads).astype(BF)
            return 0

        lax.fori_loop(0, hidden // step, back, 0)

    mi_steps = Reduce(place, mi_full, mi_recv, mi_pieces, (reduce_send.at[0], reduce_recv.at[0])).phases()
    mo_steps = Reduce(place, mo_full, mo_recv, mo_pieces, (reduce_send.at[1], reduce_recv.at[1])).phases()
    wide_steps = [step for pair in zip(mi_steps, mo_steps) for step in pair]
    vectors[...] = jnp.zeros_like(vectors)
    for slot in range(half):
        wide_grads(slot, True)
    wide_steps[0]()
    out_send[...] = sum_slots(lambda slot: nn(active[slot, 1], mo_full[slot])).astype(BF)
    out_copy = remote(out_send, out_recv, pair_send.at[2], pair_recv.at[2], mate)
    out_copy.start()
    out_part[...] = sum_slots(lambda slot: nn(active[slot, 0], mo_full[slot]))
    for slot in range(half):
        wide_grads(slot, False)
    wide_steps[1]()
    wide_steps[2]()
    dn3_copy.wait()


    def third_back(chunk):
        grad = work[chunk, :] + dn3_recv[chunk, :].astype(F32)
        normal, inverse = norm_parts(second[chunk, :])
        above = grad_pair[0, chunk, :].astype(F32)
        add_rows(vectors, 4, grad * normal)
        add_rows(vectors, 5, grad)
        add_rows(vectors, 6, above)
        value = above + norm_back(grad, normal, inverse, gain3[...])
        work[chunk, :] = value
        r2[chunk, :] = value.astype(BF)

    in_chunks(size, ROWS_AT_ONCE, third_back)
    wide_steps[3]()
    dcross[...] = nt(r2[...], co_full[...].reshape(n * local, width)).astype(BF)

    def cross_back(idx, _):
        g, near, column, stacked, key, value, scores = cross_pair(query, text_proj, limit, idx, local)
        weights = jnp.exp(scores - cross_totals[idx])
        above = stack_heads(dcross[:, pl.ds(column, PAIR)])
        dweights = nt(value, above)
        dscores = (weights * (dweights - jnp.sum(weights * dweights, axis=0, keepdims=True))).astype(BF)
        dquery[:, pl.ds(column, PAIR)] = (fold_heads(tn(key, dscores)) * SCALE).astype(BF)
        dtext_send[g, :, pl.ds(near, PAIR)] = nn(dscores, stacked).astype(BF)
        dtext_send[g, :, pl.ds(near + local, PAIR)] = nn(weights.astype(BF), above).astype(BF)
        return 0

    lax.fori_loop(0, all_pairs, cross_back, 0)
    wide_steps[4]()

    def dtext_copy(k):
        return remote(dtext_send.at[place.along(k)], dtext_recv.at[place.m], dtext_ssem.at[k], dtext_rsem.at[k], place.peer(k))

    for k in offsets:
        dtext_copy(k).start()
    def both(term):
        total = term(0)
        for g in range(1, n):
            total += term(g)
        return total

    grad2[...] = both(lambda g: nt(dquery[:, g * local : (g + 1) * local], cq_full[g]))

    def second_back(chunk):
        grad = grad2[chunk, :]
        normal, inverse = norm_parts(first[chunk, :])
        add_rows(vectors, 2, grad * normal)
        add_rows(vectors, 3, grad)
        value = work[chunk, :] + norm_back(grad, normal, inverse, gain2[...])
        residual[chunk, :] = value
        r1[chunk, :] = value.astype(BF)

    in_chunks(size, ROWS_AT_ONCE, second_back)

    def dmix_copy(k):
        return remote(dmixed_send.at[k], dmixed.at[own_rows, :], dmix_send.at[k], dmix_recv.at[k], place.peer(k))

    for k in offsets:
        dmixed_send[k] = nt(r1[...], so_full[place.along(k)]).astype(BF)
        dmix_copy(k).start()
    dmixed[own_rows, :] = nt(r1[...], so_full[place.m]).astype(BF)
    wide_steps[5]()

    stores = []

    def small_grad(left, right, keep, target, index):
        for g in range(n):
            heads = slice(g * local, (g + 1) * local)
            if keep.shape[1] == local:
                keep[g] = tn(left[:, heads], right[...]).astype(BF)
            else:
                keep[g] = tn(left[...], right[:, heads]).astype(BF)
        copy = pltpu.make_async_copy(keep, target, store_sem.at[index])
        copy.start()
        stores.append(copy)

    small_grad(n2, dquery, cq_full, cq_grad, 0)
    small_grad(mixed_all, r1, so_full, so_grad, 1)
    small_grad(cross, r2, co_full, co_grad, 2)

    out_copy.wait()

    def finish_out(chunk):
        value = second[chunk, :] + out_part[chunk, :] + out_recv[chunk, :].astype(F32) + out_bias[...]
        out[chunk, :] = value.astype(BF)

    in_chunks(size, ROWS_AT_ONCE, finish_out)
    for run in wide_steps[6:]:
        run()
    for k in offsets:
        dtext_copy(k).wait()
    total = dtext_send[place.m].astype(F32)
    for k in offsets:
        total += dtext_recv[place.along(k)].astype(F32)
    dtext[...] = total.astype(BF)
    for k in offsets:
        dmix_copy(k).wait()
    for store in stores:
        store.wait()


def layer(sizes, image, gain1, shift1, qkv, text, kv, length, gain2, shift2, gain3, shift3, in_bias, out_bias,
          so, cq, co, mi, mo, grad_out):
    n, share = sizes["mp"], sizes["share"]
    rows, width = image.shape
    slots = text.shape[0]
    local, hidden = so.shape[0], mi.shape[1]
    size = rows // n
    pairs = local // PAIR
    hops = share // 2 + 1
    half = n // 2
    vmem, hbm = pl.BlockSpec(memory_space=pltpu.VMEM), pl.BlockSpec(memory_space=pl.ANY)
    dma, mem = pltpu.SemaphoreType.DMA, pltpu.VMEM
    shape = jax.ShapeDtypeStruct
    few = max(half - 1, 1)
    bits = (sizes["dp"] // 2).bit_length() - 1
    return pl.pallas_call(
        partial(layer_kernel, sizes),
        out_shape=[
            shape((rows, 3 * local), BF), shape((rows, width), BF), shape((rows, local), BF),
            shape((pairs, n, 1, 2 * size), F32), shape((size, width), BF), shape((size, width), F32),
            shape((rows, local), BF), shape((slots, 2 * local), BF),
            shape((n, local, width), BF), shape((n, width, local), BF), shape((n, local, width), BF),
            piece_shape(half, width, hidden, bits), piece_shape(half, hidden, width, bits),
            shape((8 + -(-half // 8) * 8, width), F32),
        ],
        in_specs=[vmem] * 6 + [pl.BlockSpec(memory_space=pltpu.SMEM)] + [vmem] * 6 + [hbm] * 6,
        out_specs=[vmem] * 8 + [hbm] * 3 + [vmem] * 3,
        scratch_shapes=[
            mem((n, size, local), BF), mem((n, slots, 2 * local), BF),
            mem((n, local, width), BF), mem((n, width, local), BF), mem((n, local, width), BF),
            mem((half, width, hidden), BF), mem((half, hidden, width), BF), mem((half, 1, hidden), F32),
            mem((2, size, width), BF), mem((size, n * local), BF),
            mem((size, width), F32), mem((size, width), F32), mem((size, width), F32), mem((size, width), F32),
            mem((size, width), F32),
            mem((size, width), BF), mem((size, n * local), BF), mem((size, n * local), BF),
            mem((n * pairs, 1, 2 * size), F32), mem((size, n * local), BF),
            mem((2, size, width), BF), mem((half, 2, size, hidden), BF), mem((half, 2, size, hidden), BF),
            mem((size, width), BF), mem((size, width), BF), mem((size, width), BF), mem((size, width), BF),
            mem((size, width), BF), mem((size, n * local), BF), mem((size, width), BF),
            mem((n, size, local), BF), mem((n, slots, 2 * local), BF), mem((n, slots, 2 * local), BF),
            mem((slots, 2 * local), BF), recv_space(half, width, hidden, bits), recv_space(half, hidden, width, bits),
            dma((3, n - 1, hops)), dma((3, n - 1, hops)), dma((3,)),
            dma((2, few, hops)), dma((2, few, hops)), dma((2,)),
            dma((n,)), dma((n,)), dma(()),
            dma((n + 1,)), dma((n + 1,)), dma((half,)), dma((half,)), dma((2,)),
            dma((3,)), dma((3,)), dma((n,)), dma((n,)), dma((n,)), dma((n,)), dma((3,)), dma((2, 1 + 2 * bits)), dma((2, 1 + 2 * bits)),
        ],
        compiler_params=pltpu.CompilerParams(collective_id=1, has_side_effects=True, vmem_limit_bytes=VMEM_LIMIT),
        cost_estimate=pl.CostEstimate(flops=22 << 30, bytes_accessed=48 << 20, transcendentals=8 << 20),
    )(image, gain1, shift1, qkv, text, kv, length, gain2, shift2, gain3, shift3, in_bias, out_bias,
      so, cq, co, mi, mo, grad_out)


def back_kernel(
    sizes,
    gain1, qkv, kv, text, residual, projected, normed, mixed, totals, dmixed, dtext, early, mi_pieces, mo_pieces,
    image, so_grad, cq_grad, co_grad,
    image_grad, text_grad, early_out, late_out, mi_out, mo_out, so_out, cq_out, co_out, joint_out,
    image_rows, stacked, above, delta, dquery, dprojected,
    near_hold, near_send, near_recv, far_send, far_recv, dn1_own,
    mi_other, mi_final, mo_other, mo_final,
    so_ref, so_recv, so_pieces, so_other, so_final, cq_ref, cq_recv, cq_pieces, cq_other, cq_final,
    co_ref, co_recv, co_pieces, co_other, co_final, joint_ref, joint_recv, joint_pieces,
    early_dp, early_mp, early_own, late, late_dp, late_mp, late_own, text_send, text_recv,
    reduce_send, reduce_recv, spread_send, spread_recv, spread_keep, load_sem,
    near_ssem, near_rsem, far_ssem, far_rsem, text_ssem, text_rsem, vec_ssem, vec_rsem, vec_zsend, vec_zrecv,
):
    place = Place(sizes)
    n, dp = place.n, place.dp
    rows, width = normed.shape
    local = mixed.shape[1]
    size = rows // n
    half = n // 2
    pairs = local // PAIR
    offsets = list(range(1, n))
    everyone = [lax.rem(place.d + k, dp) for k in range(1, dp)]
    partners = [place.peer(k) for k in offsets] + [(device, place.m) for device in everyone]
    greet(partners)

    def remote(src, dst, send, recv, device):
        return pltpu.make_async_remote_copy(
            src_ref=src, dst_ref=dst, send_sem=send, recv_sem=recv, device_id=device, device_id_type=MESH
        )

    def block_of(index):
        return pl.ds(pl.multiple_of(index * size, size), size)

    loads = [
        pltpu.make_async_copy(src, dst, load_sem.at[t])
        for t, (src, dst) in enumerate((
            (so_grad, so_ref), (cq_grad, cq_ref), (co_grad, co_ref), (image.at[block_of(place.m), :], image_rows),
        ))
    ]
    for load in loads:
        load.start()

    def reduce(t, ref, recv, pieces):
        return Reduce(place, ref, recv, pieces, (reduce_send.at[t], reduce_recv.at[t])).phases()

    def spread(t, rows, pieces, other, final, whole, rule):
        sems = (spread_send.at[t], spread_recv.at[t], spread_keep.at[t])
        return Spread(place, rows, pieces, other, final, whole, rule, sems).phases()

    mi_steps = spread(0, width, mi_pieces, mi_other, mi_final, mi_out, "parity")
    mo_steps = spread(1, mo_out.shape[0], mo_pieces, mo_other, mo_final, mo_out, "parity")
    so_steps = reduce(0, so_ref, so_recv, so_pieces) + spread(2, local, so_pieces, so_other, so_final, so_out, "all")
    cq_steps = reduce(1, cq_ref, cq_recv, cq_pieces) + spread(3, width, cq_pieces, cq_other, cq_final, cq_out, "all")
    co_steps = reduce(2, co_ref, co_recv, co_pieces) + spread(4, local, co_pieces, co_other, co_final, co_out, "all")
    joint_steps = reduce(3, joint_ref, joint_recv, joint_pieces)
    joint_steps += spread(5, width, joint_pieces, None, joint_pieces, joint_out, "own")
    class Vectors:
        def __init__(self, value, over_dp, own, over_mp, base):
            self.value, self.over_dp, self.own, self.over_mp, self.base = value, over_dp, own, over_mp, base

        def first(self, k):
            return remote(self.value, self.over_dp.at[place.d], vec_ssem.at[self.base, k], vec_rsem.at[self.base, k],
                          (everyone[k - 1], place.m))

        def second(self, k):
            return remote(self.own, self.over_mp.at[place.m], vec_zsend.at[self.base, k], vec_zrecv.at[self.base, k],
                          place.peer(k))

        def begin(self):
            self.over_dp[place.d] = self.value[...]
            for k in range(1, dp):
                self.first(k).start()

        def turn(self):
            for k in range(1, dp):
                self.first(k).wait()
            total = self.over_dp[0]
            for j in range(1, dp):
                total += self.over_dp[j]
            self.own[...] = total
            self.over_mp[place.m] = total
            for k in offsets:
                self.second(k).start()

        def end(self):
            for k in offsets:
                self.second(k).wait()

        def total(self):
            value = self.over_mp[0]
            for j in range(1, n):
                value += self.over_mp[j]
            return value

    early_sum = Vectors(early, early_dp, early_own, early_mp, 0)
    late_sum = Vectors(late, late_dp, late_own, late_mp, 1)
    part = text_grad.shape[0]
    spread_text = nt(dtext[...], kv[...]).astype(BF)
    for g in range(n):
        text_send[g] = spread_text[g * part : (g + 1) * part, :]

    def text_copy(k):
        return remote(text_send.at[place.along(k)], text_recv.at[place.m], text_ssem.at[k], text_rsem.at[k], place.peer(k))

    for t in range(2):
        joint_ref[3 + t] = tn(text[...], dtext[:, t * local : (t + 1) * local]).astype(BF)

    def prepare(i, _):
        block = block_of(i)
        for hp in range(pairs):
            columns = slice(hp * PAIR, (hp + 1) * PAIR)
            stacked[hp, i] = stack_heads(projected[block, columns], SCALE)
            above[hp, i] = stack_heads(dmixed[block, columns])
            product = (dmixed[block, columns].astype(F32) * mixed[block, columns].astype(F32)).T
            delta[hp, i] = jnp.concatenate(
                [jnp.sum(product[:HEAD_DIM], axis=0, keepdims=True), jnp.sum(product[HEAD_DIM:], axis=0, keepdims=True)],
                axis=1,
            )
            dquery[hp, i] = jnp.zeros_like(dquery[hp, i])
        return 0

    meet(partners)
    mi_steps[0]()
    mo_steps[0]()
    for load, steps in zip(loads, (so_steps, cq_steps, co_steps)):
        load.wait()
        steps[0]()
    early_sum.begin()
    for k in offsets:
        text_copy(k).start()
    lax.fori_loop(0, n, prepare, 0)

    plan = [[so_steps[1]], [cq_steps[1]], [co_steps[1]]]
    each = -(-len(plan) // (n * pairs))
    parity = lax.rem(place.m, 2)
    mine = place.m // 2

    def near_copy(t):
        return remote(near_send.at[t], near_recv.at[t], near_ssem.at[t], near_rsem.at[t], (place.d, place.mate))

    def far_copy(t):
        gap = lax.rem(t - mine + half, half)
        return remote(far_send.at[t], far_recv.at[mine], far_ssem.at[gap], far_rsem.at[gap], (place.d, 2 * t + parity))

    def pass_on(t):
        near_copy(t).wait()
        total = near_hold[t] + near_recv[t].astype(F32)

        @pl.when(mine == t)
        def _():
            dn1_own[...] = total

        @pl.when(mine != t)
        def _():
            far_send[t] = total.astype(BF)
            far_copy(t).start()

    point = 0
    for j in range(n):
        keys = slice(j * size, (j + 1) * size)
        for hp in range(pairs):
            columns = slice(hp * PAIR, (hp + 1) * PAIR)
            key = projected[keys, local + hp * PAIR : local + (hp + 1) * PAIR]
            value = projected[keys, 2 * local + hp * PAIR : 2 * local + (hp + 1) * PAIR]

            def tile(i, carry, diagonal):
                dkey, dvalue = carry
                query, over = stacked[hp, i], above[hp, i]
                scores = nt(key, query)
                if diagonal:
                    scores = jnp.where(causal(size, size), scores, MASKED)
                weights = jnp.exp(scores - totals[hp, i])
                dscores = (weights * (nt(value, over) - delta[hp, i])).astype(BF)
                dvalue = dvalue + nn(weights.astype(BF), over)
                dkey = dkey + nn(dscores, query)
                turned = tn(key, dscores)
                dquery[hp, i] += jnp.concatenate([turned[:HEAD_DIM, :size], turned[HEAD_DIM:, size:]], axis=0)
                return dkey, dvalue

            carry = (jnp.zeros((size, PAIR), F32), jnp.zeros((size, PAIR), F32))
            carry = tile(j, carry, True)
            dkey, dvalue = lax.fori_loop(j + 1, n, lambda i, c: tile(i, c, False), carry)
            dprojected[keys, columns] = (dquery[hp, j].T * SCALE).astype(BF)
            dprojected[keys, local + hp * PAIR : local + (hp + 1) * PAIR] = dkey.astype(BF)
            dprojected[keys, 2 * local + hp * PAIR : 2 * local + (hp + 1) * PAIR] = dvalue.astype(BF)
            for phases in plan[point * each : (point + 1) * each]:
                for phase in phases:
                    phase()
            point += 1
        partial_sum = sum(nt(dprojected[keys, t * local : (t + 1) * local], qkv[t]) for t in range(3))

        @pl.when(parity == j % 2)
        def _():
            near_hold[j // 2] = partial_sum

        @pl.when(parity != j % 2)
        def _():
            near_send[j // 2] = partial_sum.astype(BF)
            near_copy(j // 2).start()

    tile_rows = min(256, width)

    def qkv_grad(t, _):
        at = pl.ds(pl.multiple_of(t * tile_rows, tile_rows), tile_rows)
        total = tn(normed[:, at], dprojected[...]).astype(BF)
        for t in range(3):
            joint_ref[t, at, :] = total[:, t * local : (t + 1) * local]
        return 0

    lax.fori_loop(0, width // tile_rows, qkv_grad, 0)
    bits = (dp // 2).bit_length() - 1
    small_steps = (so_steps, cq_steps, co_steps)
    for t in range(half - 1):
        pass_on(t)
    for steps in small_steps:
        steps[2]()
    joint_steps[0]()
    for k in range(1, bits):
        for steps in small_steps:
            steps[2 + k]()
    for steps in small_steps:
        steps[2 + bits]()
    joint_steps[1]()
    pass_on(half - 1)
    mi_steps[1]()
    mo_steps[1]()
    for k in range(bits):
        joint_steps[2 + k]()
    joint_steps[2 + bits]()
    joint_steps[3 + bits]()
    mi_steps[2]()
    mo_steps[2]()
    for steps in small_steps:
        steps[3 + bits]()
    for k in range(1, bits):
        mi_steps[2 + k]()
        mo_steps[2 + k]()
    joint_steps[4 + bits]()
    for k in range(bits - 1):
        for steps in small_steps:
            steps[4 + bits + k]()

    early_sum.turn()
    for k in range(1, half):
        far_copy(lax.rem(mine + k, half)).wait()
        dn1_own[...] += far_recv[lax.rem(mine + half - k, half)].astype(F32)
    loads[3].wait()
    late[...] = jnp.zeros_like(late)

    def last_back(chunk):
        grad = dn1_own[chunk, :]
        normal, inverse = norm_parts(image_rows[chunk, :].astype(F32))
        add_rows(late, 0, grad * normal)
        add_rows(late, 1, grad)
        image_grad[chunk, :] = residual[chunk, :] + norm_back(grad, normal, inverse, gain1[...])

    in_chunks(size, ROWS_AT_ONCE, last_back)
    late_sum.begin()
    for steps in small_steps:
        steps[3 + 2 * bits]()
    for k in offsets:
        text_copy(k).wait()
    total = text_send[place.m].astype(F32)
    for k in offsets:
        total += text_recv[place.along(k)].astype(F32)
    text_grad[...] = total
    late_sum.turn()
    early_sum.end()
    early_out[...] = early_sum.total()
    shared = early_out[pl.ds(8 + place.m // 2, 1), :] * 0.0
    for j in range(n):
        take = jnp.where(lax.rem(place.m + j, 2) == 0, 1.0, 0.0)
        shared += early_mp[j, pl.ds(8 + place.m // 2, 1), :] * take
    early_out[7:8, :] = shared
    for k in range(1, bits):
        joint_steps[4 + bits + k]()
    late_sum.end()
    late_out[...] = late_sum.total()
    for steps in (mi_steps, mo_steps, *small_steps, joint_steps):
        steps[-1]()


def back(sizes, gain1, qkv, kv, text, residual, projected, normed, mixed, totals, dmixed, dtext, early, mi_pieces, mo_pieces,
         image, so_grad, cq_grad, co_grad, hidden):
    n, dp = sizes["mp"], sizes["dp"]
    rows, width = normed.shape
    slots = text.shape[0]
    local = mixed.shape[1]
    size, pairs, half = rows // n, local // PAIR, n // 2
    bits = (dp // 2).bit_length() - 1
    vmem, hbm = pl.BlockSpec(memory_space=pltpu.VMEM), pl.BlockSpec(memory_space=pl.ANY)
    dma, mem = pltpu.SemaphoreType.DMA, pltpu.VMEM
    shape = jax.ShapeDtypeStruct

    def unit(count, height, columns, rule):
        pieces = piece_shape(count, height, columns, bits).shape
        scratch = []
        if rule != "parity":
            scratch += [mem((count, height, columns), BF), recv_space(count, height, columns, bits), mem(pieces, BF)]
        if rule != "own":
            scratch += [mem(pieces, BF), mem(pieces[1:], BF)]
        return scratch

    few = early.shape[0]
    whole = [(width, hidden), (hidden, width), (local, width), (width, local), (local, width), (5, width, local)]
    block = mem((half, size, width), BF)
    return pl.pallas_call(
        partial(back_kernel, sizes),
        out_shape=[
            shape((size, width), F32), shape((slots // n, width), F32), shape((few, width), F32), shape((2, width), F32),
        ] + [shape(extent, BF) for extent in whole],
        in_specs=[vmem] * 14 + [hbm] * 4,
        out_specs=[vmem] * 4 + [hbm] * 6,
        scratch_shapes=[
            mem((size, width), BF), mem((pairs, n, 2 * size, PAIR), BF), mem((pairs, n, 2 * size, PAIR), BF),
            mem((pairs, n, 1, 2 * size), F32), mem((pairs, n, PAIR, size), F32), mem((rows, 3 * local), BF),
            mem((half, size, width), F32), block, block, block, block, mem((size, width), F32),
            *unit(half, width, hidden, "parity"), *unit(half, hidden, width, "parity"),
            *unit(n, local, width, "all"), *unit(n, width, local, "all"), *unit(n, local, width, "all"),
            *unit(5, width, local, "own"),
            mem((dp, few, width), F32), mem((n, few, width), F32), mem((few, width), F32),
            mem((2, width), F32), mem((dp, 2, width), F32), mem((n, 2, width), F32), mem((2, width), F32),
            mem((n, slots // n, width), BF), mem((n, slots // n, width), BF),
            dma((4, 1 + 2 * bits)), dma((4, 1 + 2 * bits)), dma((6, 1 + 2 * bits + n)), dma((6, 1 + 2 * bits + n)), dma((6, 2)),
            dma((4,)), dma((half,)), dma((half,)), dma((half,)), dma((half,)), dma((n,)), dma((n,)),
            dma((2, dp)), dma((2, dp)), dma((2, n)), dma((2, n)),
        ],
        compiler_params=pltpu.CompilerParams(collective_id=2, has_side_effects=True, vmem_limit_bytes=VMEM_LIMIT),
        cost_estimate=pl.CostEstimate(flops=8 << 30, bytes_accessed=48 << 20, transcendentals=4 << 20),
    )(gain1, qkv, kv, text, residual, projected, normed, mixed, totals, dmixed, dtext, early, mi_pieces, mo_pieces,
      image, so_grad, cq_grad, co_grad)


def finish_kernel(slots, out, image_grad, text_grad, early, late, mi, mo, so, cq, co, joint,
                  to_out, to_image, to_text, to_mi, to_mo, to_so, to_cq, to_co, to_qkv, to_kv, to_bias, *to_vectors):
    to_out[...] = out[...]
    to_image[...] = image_grad[...]
    to_text[...] = text_grad[...]
    for source, target in ((mi, to_mi), (mo, to_mo), (so, to_so), (cq, to_cq), (co, to_co)):
        target[...] = source[...].astype(F32)
    for t in range(3):
        to_qkv[t] = joint[t].astype(F32)
    for t in range(2):
        to_kv[:, t, :] = joint[3 + t].astype(F32)
    for t in range(2):
        to_vectors[t][...] = late[t : t + 1, :]
    for t in range(2, 7):
        to_vectors[t][...] = early[t : t + 1, :]
    to_bias[...] = early[7:8, 0 : to_bias.shape[1]]


def finish(out, image_grad, text_grad, early, late, mi, mo, so, cq, co, joint):
    steps = 2
    width, hidden = mi.shape
    local = so.shape[0]

    def cut(value, axis=0):
        shape = list(value.shape)
        shape[axis] //= steps
        return pl.BlockSpec(tuple(shape), lambda i: tuple(i if t == axis else 0 for t in range(len(shape))))

    def whole(shape):
        return pl.BlockSpec(tuple(shape), lambda i: (0,) * len(shape))

    shape = jax.ShapeDtypeStruct
    sums = [shape(value.shape, F32) for value in (mi, mo, so, cq, co)]
    qkv, kv = shape((3, width, local), F32), shape((width, 2, local), F32)
    return pl.pallas_call(
        partial(finish_kernel, steps),
        grid=(steps,),
        out_shape=[shape(out.shape, BF), shape(image_grad.shape, F32), shape(text_grad.shape, F32), *sums, qkv, kv,
                   shape((1, hidden), F32)] + [shape((1, width), F32)] * 7,
        in_specs=[cut(out), cut(image_grad), whole(text_grad.shape), whole(early.shape), whole(late.shape)]
        + [cut(value) for value in (mi, mo, so, cq, co)] + [cut(joint, 1)],
        out_specs=[cut(out), cut(image_grad), whole(text_grad.shape)] + [cut(value) for value in sums]
        + [cut(qkv, 1), cut(kv), whole((1, hidden))] + [whole((1, width))] * 7,
        compiler_params=pltpu.CompilerParams(vmem_limit_bytes=VMEM_LIMIT),
        cost_estimate=pl.CostEstimate(flops=1 << 22, bytes_accessed=28 << 20, transcendentals=0),
    )(out, image_grad, text_grad, early, late, mi, mo, so, cq, co, joint)


def body(sizes, image, text, grad_out, lengths, gain1, shift1, qkv, so, gain2, shift2, cq, kv, co, gain3, shift3, mi,
         in_bias, mo, out_bias):
    n = sizes["mp"]
    image, text, grad_out = image[0], text[0], grad_out[0]
    rows, width = image.shape
    local = so.shape[0]
    sizes = dict(sizes, share=share_of(local, sizes["dp"]))
    qkv, kv = jnp.transpose(qkv, (1, 0, 2)), kv.reshape(width, 2 * local)
    row = lambda value: value[None]
    (projected, normed1, mixed, totals, out, residual, dmixed, dtext, so_grad, cq_grad, co_grad, mi_pieces, mo_pieces,
     early) = layer(
        sizes, image, row(gain1), row(shift1), qkv, text, kv, row(lengths), row(gain2), row(shift2), row(gain3),
        row(shift3), row(in_bias), row(out_bias), so, cq, co, mi, mo, grad_out)
    image_grad, text_grad, early, late, mi_sum, mo_sum, so_sum, cq_sum, co_sum, joint_sum = back(
        sizes, row(gain1), qkv, kv, text, residual, projected, normed1, mixed, totals, dmixed, dtext, early,
        mi_pieces, mo_pieces, image, so_grad, cq_grad, co_grad, mi.shape[1])
    (out, image_grad, text_grad, mi_sum, mo_sum, so_sum, cq_sum, co_sum, qkv_sum, kv_sum, bias_sum, *vectors) = finish(
        out, image_grad, text_grad, early, late, mi_sum, mo_sum, so_sum, cq_sum, co_sum, joint_sum)
    g1, s1, g2, s2, g3, s3, ob = (value[0] for value in vectors)
    return (
        out[None], image_grad[None], text_grad[None], g1, s1, jnp.transpose(qkv_sum, (1, 0, 2)), so_sum, g2, s2, cq_sum,
        kv_sum, co_sum, g3, s3, mi_sum, bias_sum[0], mo_sum, ob,
    )


def solution(mesh):
    rows3, rows2, rows1 = P(None, None, "mp"), P(None, "mp"), P("mp")
    item = P("dp", None, None)
    in_specs = (item, item, item, P("dp"), P(), P(), rows3, P("mp", None), P(), P(), rows2, rows3, P("mp", None), P(), P(),
                rows2, rows1, P("mp", None), P())
    split = P("dp", "mp", None)
    out_specs = (split, split, split, P(), P(), rows3, P("mp", None), P(), P(), rows2, rows3, P("mp", None), P(), P(),
                 rows2, rows1, P("mp", None), P())
    sizes = dict(mesh.shape)
    return jax.shard_map(partial(body, sizes), mesh=mesh, in_specs=in_specs, out_specs=out_specs, check_vma=False)
```
